32 devices in a mesh: groups: 2 (over x), tensor: 4 (over y, core), dp: 4 (over z).
Axes of the slice: x: 2, y: 2, z: 4, core: 2. Of those that a mesh axis runs over, the one named last changes fastest.
Arguments:
- first_out: bfloat16 [4096, 1024], P(('groups', 'tensor', 'dp')), parts along dimension 0, may hold values from -6 to 6
- second_out: bfloat16 [4096, 1024], P(('groups', 'tensor', 'dp')), parts along dimension 0, may hold values from -6 to 6
- grad_first: bfloat16 [4096, 1024], P(('groups', 'tensor', 'dp')), parts along dimension 0, may hold values from -6 to 6
- grad_second: bfloat16 [4096, 1024], P(('groups', 'tensor', 'dp')), parts along dimension 0, may hold values from -6 to 6
- w_up: bfloat16 [1024, 8192], P('dp', 'tensor'), may hold values from -0.1875 to 0.1875
- w_down: bfloat16 [8192, 1024], P('tensor', 'dp'), may hold values from -0.0625 to 0.0625
- norm_gain: float32 [1024], replicated, may hold values from 0.25 to 1.75
- norm_bias: float32 [1024], replicated, may hold values from -3 to 3
Outputs:
- second_in: bfloat16 [4096, 1024], P(('groups', 'tensor', 'dp')), parts along dimension 0
- grad_first_in: float32 [4096, 1024], P(('groups', 'tensor', 'dp')), parts along dimension 0
- grad_up: float32 [2048, 8192], P(('groups', 'dp'), 'tensor'), parts along dimension 0
- grad_down: float32 [16384, 1024], P(('groups', 'tensor'), 'dp'), parts along dimension 0
- grad_norm: float32 [4, 1024], P('groups'), parts along dimension 0
The draws below stay inside these ranges and needn't reach their ends.
There are 2 independent parts, one for each index of `groups`. The reference program is written for one: setup_inputs(seed, part) draws one part's arguments, and reference() takes and returns one part's arrays. A program takes and returns all parts, laid end to end along the dimension named above; an argument that names none is the same for every part. Nothing has to cross between parts.
All inputs are finite; a program needn't handle non-finite values.
Results may differ from the reference program's by a relative error of at most 0.017.
Values may be sent and summed in bfloat16 or wider, within the bound.
No kernel may reach another device: no remote copies, remote signals or barrier semaphores. Data moves between devices by JAX's collectives and lax.ppermute only.
A program may use at most 64 MiB of HBM per device.

```python
import jax
import jax.numpy as jnp
from jax import lax

D = 1024
FF = 8192
TOKENS = 2048
N_TENSOR = 4


def block_scale(key, dims, split, least, top_value):
    level, own = 1.0, jax.random.fold_in(key, 6)
    for dim, shards_of in split:
        heights = jnp.exp(jax.random.uniform(jax.random.fold_in(own, dim), (shards_of,), jnp.float32, least / len(split), top_value / len(split)))
        level = level * jnp.repeat(heights, dims[dim] // shards_of).reshape([-1 if axis == dim else 1 for axis in range(len(dims))])
    return level


def noise(rng, extent, width, limit, shards=(), kind=jnp.bfloat16):
    loudness = block_scale(rng, extent, shards, -0.22, 0.18) if shards else 1.0
    result = jax.random.normal(rng, extent, jnp.float32) * width * loudness
    return jnp.minimum(jnp.maximum(result, -limit), limit).astype(kind)


def setup_inputs(seed: int = 0, part: int = 0) -> dict:
    splits = jax.random.split(jax.random.key(seed), 9)
    part_splits = jax.random.split(jax.random.fold_in(splits[8], part), 9)
    first_out = noise(part_splits[0], (TOKENS, D), 1.0, 6.0, ((0, 16),))
    second_out = noise(part_splits[1], (TOKENS, D), 1.0, 6.0, ((0, 16),))
    grad_first = noise(part_splits[2], (TOKENS, D), 1.0, 6.0, ((0, 16),))
    grad_second = noise(part_splits[3], (TOKENS, D), 1.0, 6.0, ((0, 16),))
    w_up = noise(splits[4], (D, FF), D ** -0.5, 0.1875, ((0, 4), (1, 4)))
    w_down = noise(splits[5], (FF, D), FF ** -0.5, 0.0625, ((0, 4), (1, 4)))
    norm_gain = jnp.clip(1.0 + 0.15 * jax.random.normal(splits[6], (D,), jnp.float32), 0.25, 1.75)
    norm_bias = noise(splits[7], (D,), 0.5, 3.0, (), jnp.float32)
    return dict(first_out=first_out, second_out=second_out, grad_first=grad_first, grad_second=grad_second, w_up=w_up, w_down=w_down, norm_gain=norm_gain, norm_bias=norm_bias)


epsilon = 1e-06

def normalize(row_data, norm_gain, norm_bias):
    values = row_data.astype(jnp.float32)
    row_mean = lax.optimization_barrier(jnp.mean(values, axis=-1, keepdims=True))
    centred = values - row_mean
    inv_std = lax.rsqrt(lax.optimization_barrier(jnp.mean(centred * centred, axis=-1, keepdims=True)) + epsilon)
    standard = centred * inv_std
    normed = (standard * norm_gain.astype(jnp.float32) + norm_bias.astype(jnp.float32)).astype(jnp.bfloat16)
    return (standard, inv_std, normed)

def round_half(values):
    return lax.optimization_barrier(values.astype(jnp.bfloat16)).astype(jnp.float32)

def reference(first_out, second_out, grad_first, grad_second, w_up, w_down, norm_gain, norm_bias):
    standard, inv_std, normed = normalize(first_out, norm_gain, norm_bias)
    block_width = FF // N_TENSOR
    up_blocks = jnp.transpose(w_up.reshape(D, N_TENSOR, block_width), (1, 0, 2))
    down_blocks = w_down.reshape(N_TENSOR, block_width, D)

    def step_block(totals, blocks):
        branch, grad_normed = totals
        up_block, down_block = blocks
        preact = jnp.dot(normed, up_block, preferred_element_type=jnp.float32)
        hidden = jax.nn.gelu(preact).astype(jnp.bfloat16)
        branch = branch + round_half(jnp.dot(hidden, down_block, preferred_element_type=jnp.float32))
        grad_hidden = lax.dot_general(grad_second, down_block, (((1,), (1,)), ((), ())), preferred_element_type=jnp.float32)
        grad_pre = jax.vjp(jax.nn.gelu, preact)[1](grad_hidden)[0].astype(jnp.bfloat16)
        grad_down = lax.dot_general(hidden, grad_second, (((0,), (0,)), ((), ())), preferred_element_type=jnp.float32)
        grad_up = lax.dot_general(normed, grad_pre, (((0,), (0,)), ((), ())), preferred_element_type=jnp.float32)
        grad_normed = grad_normed + round_half(lax.dot_general(grad_pre, up_block, (((1,), (1,)), ((), ())), preferred_element_type=jnp.float32))
        return ((branch, grad_normed), (grad_up, grad_down))
    empty_rows = jnp.zeros((TOKENS, D), jnp.float32)
    (branch, grad_normed), (up_grads, down_grads) = lax.scan(step_block, (empty_rows, empty_rows), (up_blocks, down_blocks))
    grad_scale = TOKENS ** (-0.5)
    second_in = (second_out.astype(jnp.float32) - branch).astype(jnp.bfloat16)
    grad_std = grad_normed * norm_gain.astype(jnp.float32)
    grad_rows = inv_std * (grad_std - lax.optimization_barrier(jnp.mean(grad_std, axis=-1, keepdims=True)) - standard * lax.optimization_barrier(jnp.mean(grad_std * standard, axis=-1, keepdims=True)))
    grad_first_in = grad_first.astype(jnp.float32) + grad_rows
    grad_norm = jnp.stack([lax.optimization_barrier(jnp.sum(grad_normed * standard, axis=0)), lax.optimization_barrier(jnp.sum(grad_normed, axis=0))]) * grad_scale
    grad_up = jnp.transpose(up_grads, (1, 0, 2)).reshape(D, FF) * grad_scale
    grad_down = down_grads.reshape(FF, D) * grad_scale
    return (second_in, grad_first_in, grad_up, grad_down, grad_norm)
```

```python
import jax
import jax.numpy as jnp
from jax import lax
from jax.sharding import PartitionSpec as P

epsilon = 1e-06


def normalize(row_data, norm_gain, norm_bias):
    values = row_data.astype(jnp.float32)
    row_mean = jnp.mean(values, axis=-1, keepdims=True)
    centred = values - row_mean
    inv_std = lax.rsqrt(jnp.mean(centred * centred, axis=-1, keepdims=True) + epsilon)
    standard = centred * inv_std
    normed = (standard * norm_gain + norm_bias).astype(jnp.bfloat16)
    return (standard, inv_std, normed)


def contract_tokens(left_rows, right_rows):
    return lax.dot_general(
        left_rows, right_rows, (((0,), (0,)), ((), ())), preferred_element_type=jnp.float32
    )


def contract_last(left_rows, right_rows):
    return lax.dot_general(
        left_rows, right_rows, (((1,), (1,)), ((), ())), preferred_element_type=jnp.float32
    )


def finish_rows(branch, grad_normed, second_out, grad_first, standard, inv_std, norm_gain):
    second_in = (second_out.astype(jnp.float32) - branch).astype(jnp.bfloat16)
    grad_std = grad_normed * norm_gain
    grad_rows = inv_std * (
        grad_std
        - jnp.mean(grad_std, axis=-1, keepdims=True)
        - standard * jnp.mean(grad_std * standard, axis=-1, keepdims=True)
    )
    grad_first_in = grad_first.astype(jnp.float32) + grad_rows
    local_stats = jnp.stack([jnp.sum(grad_normed * standard, axis=0), jnp.sum(grad_normed, axis=0)])
    return second_in, grad_first_in, local_stats


def gather_weights_body(
    first_out, second_out, grad_first, grad_second, w_up, w_down, norm_gain, norm_bias
):
    own_rows = first_out.shape[0]
    up_full = lax.all_gather(w_up, "dp", axis=0, tiled=True)
    down_full = lax.all_gather(w_down, "dp", axis=1, tiled=True)
    first_all = lax.all_gather(first_out, "tensor", axis=0, tiled=True)
    grad_all = lax.all_gather(grad_second, "tensor", axis=0, tiled=True)
    standard_all, inv_std_all, normed = normalize(first_all, norm_gain, norm_bias)
    offset = lax.axis_index("tensor") * own_rows
    standard = lax.dynamic_slice_in_dim(standard_all, offset, own_rows, 0)
    inv_std = lax.dynamic_slice_in_dim(inv_std_all, offset, own_rows, 0)
    preact = jnp.dot(normed, up_full, preferred_element_type=jnp.float32)
    hidden = jax.nn.gelu(preact).astype(jnp.bfloat16)
    branch = lax.psum_scatter(
        jnp.dot(hidden, down_full, preferred_element_type=jnp.float32).astype(jnp.bfloat16),
        "tensor",
        scatter_dimension=0,
        tiled=True,
    ).astype(jnp.float32)
    tokens = own_rows * lax.axis_size("tensor") * lax.axis_size("dp")
    grad_scale = tokens ** (-0.5)
    grad_down_part = contract_tokens(hidden, grad_all)
    grad_down = (
        lax.psum_scatter(
            grad_down_part.astype(jnp.bfloat16), "dp", scatter_dimension=1, tiled=True
        ).astype(jnp.float32)
        * grad_scale
    )
    grad_hidden = contract_last(grad_all, down_full)
    grad_pre = jax.vjp(jax.nn.gelu, preact)[1](grad_hidden)[0].astype(jnp.bfloat16)
    grad_up_part = contract_tokens(normed, grad_pre)
    grad_up = (
        lax.psum_scatter(
            grad_up_part.astype(jnp.bfloat16), "dp", scatter_dimension=0, tiled=True
        ).astype(jnp.float32)
        * grad_scale
    )
    grad_normed = lax.psum_scatter(
        contract_last(grad_pre, up_full).astype(jnp.bfloat16),
        "tensor",
        scatter_dimension=0,
        tiled=True,
    ).astype(jnp.float32)
    second_in, grad_first_in, local_stats = finish_rows(
        branch, grad_normed, second_out, grad_first, standard, inv_std, norm_gain
    )
    grad_norm = lax.psum(local_stats, ("tensor", "dp")) * grad_scale
    return (second_in, grad_first_in, grad_up, grad_down, grad_norm)


def swap(values, axis, mask):
    return lax.ppermute(values, axis, [(i, i ^ mask) for i in range(lax.axis_size(axis))])


def bits_of(size):
    return [1 << b for b in reversed(range(size.bit_length() - 1))]


def gather_tokens_body(
    first_out, second_out, grad_first, grad_second, w_up, w_down, norm_gain, norm_bias
):
    n_dp, n_tensor = lax.axis_size("dp"), lax.axis_size("tensor")
    own_rows, depth = first_out.shape[0], w_up.shape[0]
    units = w_up.shape[1] // n_dp
    place = lax.axis_index("dp")
    standard, inv_std, normed = normalize(first_out, norm_gain, norm_bias)

    up = jnp.zeros((depth * n_dp, units), w_up.dtype)
    down = jnp.zeros((units, depth * n_dp), w_down.dtype)
    for k in range(n_dp):
        other = place ^ k
        block = lax.dynamic_slice_in_dim(w_up, other * units, units, 1)
        block = swap(block, "dp", k) if k else block
        up = lax.dynamic_update_slice_in_dim(up, block, other * depth, 0)
    for k in range(n_dp):
        other = place ^ k
        block = lax.dynamic_slice_in_dim(w_down, other * units, units, 0)
        block = swap(block, "dp", k) if k else block
        down = lax.dynamic_update_slice_in_dim(down, block, other * depth, 1)

    chunks = {0: jnp.stack([normed, grad_second])}
    for bit in bits_of(n_dp):
        chunks.update({k | bit: swap(chunk, "dp", bit) for k, chunk in chunks.items()})

    sums = {}
    up_total = down_total = 0.0
    for k in sorted(chunks):
        chunk = chunks[k]
        for bit in bits_of(n_tensor):
            chunk = jnp.concatenate([chunk, swap(chunk, "tensor", bit)], axis=1)
        rows, grads = chunk[0], chunk[1]
        preact = jnp.dot(rows, up, preferred_element_type=jnp.float32)
        hidden = jax.nn.gelu(preact).astype(jnp.bfloat16)
        grad_hidden = contract_last(grads, down)
        grad_pre = jax.vjp(jax.nn.gelu, preact)[1](grad_hidden)[0].astype(jnp.bfloat16)
        part = jnp.stack(
            [
                jnp.dot(hidden, down, preferred_element_type=jnp.float32).astype(jnp.bfloat16),
                contract_last(grad_pre, up).astype(jnp.bfloat16),
            ]
        )
        up_total = up_total + contract_tokens(rows, grad_pre)
        down_total = down_total + contract_tokens(hidden, grads)
        for bit in reversed(bits_of(n_tensor)):
            half = part.shape[1] // 2
            part = part[:, :half] + swap(part[:, half:], "tensor", bit)
        sums[k] = part
    for bit in reversed(bits_of(n_dp)):
        for k in [k for k in sums if k & bit]:
            got = swap(sums.pop(k), "dp", bit).astype(jnp.float32)
            total = sums[k ^ bit].astype(jnp.float32) + got
            sums[k ^ bit] = total if k == bit and bit == bits_of(n_dp)[0] else total.astype(jnp.bfloat16)
    branch, grad_normed = sums[0][0], sums[0][1]
    second_in, grad_first_in, stats = finish_rows(
        branch, grad_normed, second_out, grad_first, standard, inv_std, norm_gain
    )

    grad_scale = (own_rows * n_tensor * n_dp) ** (-0.5)
    up_total, down_total = up_total.astype(jnp.bfloat16), down_total.astype(jnp.bfloat16)
    grad_up = jnp.zeros(w_up.shape, jnp.float32)
    grad_down = jnp.zeros(w_down.shape, jnp.float32)
    for k in range(n_dp):
        other = place ^ k
        block = lax.dynamic_slice_in_dim(up_total, other * depth, depth, 0)
        block = swap(block, "dp", k) if k else block
        block = block.astype(jnp.float32) * grad_scale
        grad_up = lax.dynamic_update_slice_in_dim(grad_up, block, other * units, 1)
    for k in range(n_dp):
        other = place ^ k
        block = lax.dynamic_slice_in_dim(down_total, other * depth, depth, 1)
        block = swap(block, "dp", k) if k else block
        block = block.astype(jnp.float32) * grad_scale
        grad_down = lax.dynamic_update_slice_in_dim(grad_down, block, other * units, 0)

    for axis in ("dp", "tensor"):
        for bit in bits_of(lax.axis_size(axis)):
            stats = stats + swap(stats, axis, bit)
    return (second_in, grad_first_in, grad_up, grad_down, stats * grad_scale)


def body(first_out, second_out, grad_first, grad_second, w_up, *rest):
    n_dp, n_tensor = lax.axis_size("dp"), lax.axis_size("tensor")
    powers = all(size & (size - 1) == 0 for size in (n_dp, n_tensor))
    few_tokens = first_out.shape[0] * n_tensor < w_up.shape[1]
    fits = w_up.shape[1] % n_dp == 0
    pick = gather_tokens_body if powers and few_tokens and fits else gather_weights_body
    return pick(first_out, second_out, grad_first, grad_second, w_up, *rest)


def solution(mesh):
    in_specs = (
        P(("groups", "tensor", "dp"), None),
        P(("groups", "tensor", "dp"), None),
        P(("groups", "tensor", "dp"), None),
        P(("groups", "tensor", "dp"), None),
        P("dp", "tensor"),
        P("tensor", "dp"),
        P(),
        P(),
    )
    out_specs = (
        P(("groups", "tensor", "dp"), None),
        P(("groups", "tensor", "dp"), None),
        P(("groups", "dp"), "tensor"),
        P(("groups", "tensor"), "dp"),
        P("groups", None),
    )
    return jax.shard_map(body, mesh=mesh, in_specs=in_specs, out_specs=out_specs, check_vma=False)
```

```python
import jax
import jax.numpy as jnp
from jax import lax
from jax.experimental import pallas as pl
from jax.experimental.pallas import tpu as pltpu
from jax.sharding import PartitionSpec as P

epsilon = 1e-06


def normalize(row_data, norm_gain, norm_bias):
    values = row_data.astype(jnp.float32)
    row_mean = jnp.mean(values, axis=-1, keepdims=True)
    centred = values - row_mean
    inv_std = lax.rsqrt(jnp.mean(centred * centred, axis=-1, keepdims=True) + epsilon)
    standard = centred * inv_std
    normed = (standard * norm_gain + norm_bias).astype(jnp.bfloat16)
    return (standard, inv_std, normed)


def contract_tokens(left_rows, right_rows):
    return lax.dot_general(
        left_rows, right_rows, (((0,), (0,)), ((), ())), preferred_element_type=jnp.float32
    )


def contract_last(left_rows, right_rows):
    return lax.dot_general(
        left_rows, right_rows, (((1,), (1,)), ((), ())), preferred_element_type=jnp.float32
    )


def finish_rows(branch, grad_normed, second_out, grad_first, standard, inv_std, norm_gain):
    second_in = (second_out.astype(jnp.float32) - branch).astype(jnp.bfloat16)
    grad_std = grad_normed * norm_gain
    grad_rows = inv_std * (
        grad_std
        - jnp.mean(grad_std, axis=-1, keepdims=True)
        - standard * jnp.mean(grad_std * standard, axis=-1, keepdims=True)
    )
    grad_first_in = grad_first.astype(jnp.float32) + grad_rows
    local_stats = jnp.stack([jnp.sum(grad_normed * standard, axis=0), jnp.sum(grad_normed, axis=0)])
    return second_in, grad_first_in, local_stats


def gather_weights_body(
    first_out, second_out, grad_first, grad_second, w_up, w_down, norm_gain, norm_bias
):
    own_rows = first_out.shape[0]
    up_full = lax.all_gather(w_up, "dp", axis=0, tiled=True)
    down_full = lax.all_gather(w_down, "dp", axis=1, tiled=True)
    first_all = lax.all_gather(first_out, "tensor", axis=0, tiled=True)
    grad_all = lax.all_gather(grad_second, "tensor", axis=0, tiled=True)
    standard_all, inv_std_all, normed = normalize(first_all, norm_gain, norm_bias)
    offset = lax.axis_index("tensor") * own_rows
    standard = lax.dynamic_slice_in_dim(standard_all, offset, own_rows, 0)
    inv_std = lax.dynamic_slice_in_dim(inv_std_all, offset, own_rows, 0)
    preact = jnp.dot(normed, up_full, preferred_element_type=jnp.float32)
    hidden = jax.nn.gelu(preact).astype(jnp.bfloat16)
    branch = lax.psum_scatter(
        jnp.dot(hidden, down_full, preferred_element_type=jnp.float32).astype(jnp.bfloat16),
        "tensor",
        scatter_dimension=0,
        tiled=True,
    ).astype(jnp.float32)
    tokens = own_rows * lax.axis_size("tensor") * lax.axis_size("dp")
    grad_scale = tokens ** (-0.5)
    grad_down_part = contract_tokens(hidden, grad_all)
    grad_down = (
        lax.psum_scatter(
            grad_down_part.astype(jnp.bfloat16), "dp", scatter_dimension=1, tiled=True
        ).astype(jnp.float32)
        * grad_scale
    )
    grad_hidden = contract_last(grad_all, down_full)
    grad_pre = jax.vjp(jax.nn.gelu, preact)[1](grad_hidden)[0].astype(jnp.bfloat16)
    grad_up_part = contract_tokens(normed, grad_pre)
    grad_up = (
        lax.psum_scatter(
            grad_up_part.astype(jnp.bfloat16), "dp", scatter_dimension=0, tiled=True
        ).astype(jnp.float32)
        * grad_scale
    )
    grad_normed = lax.psum_scatter(
        contract_last(grad_pre, up_full).astype(jnp.bfloat16),
        "tensor",
        scatter_dimension=0,
        tiled=True,
    ).astype(jnp.float32)
    second_in, grad_first_in, local_stats = finish_rows(
        branch, grad_normed, second_out, grad_first, standard, inv_std, norm_gain
    )
    grad_norm = lax.psum(local_stats, ("tensor", "dp")) * grad_scale
    return (second_in, grad_first_in, grad_up, grad_down, grad_norm)


def swap(values, axis, mask):
    return lax.ppermute(values, axis, [(i, i ^ mask) for i in range(lax.axis_size(axis))])


def bits_of(size):
    return [1 << b for b in reversed(range(size.bit_length() - 1))]


def pack_weights(w_up, w_down, mates):
    n_dp = lax.axis_size("dp")
    depth, units = w_up.shape[0], w_up.shape[1] // n_dp
    up_rows, down_rows, strips = depth // mates, units // mates, units // depth
    strip_rows = down_rows // strips

    def kernel(up_ref, down_ref, *rest):
        sends, sem = rest[:-1], rest[-1]
        place, mate = lax.axis_index("dp"), lax.rem(lax.axis_index("groups"), mates)
        copies = []

        def copy(src, dst):
            one = pltpu.make_async_copy(src, dst, sem.at[len(copies)])
            one.start()
            copies.append(one)

        for k in range(1, n_dp):
            first = pl.multiple_of((place ^ k) * units, units)
            send = sends[k - 1]
            copy(
                up_ref.at[pl.ds(pl.multiple_of(mate * up_rows, up_rows), up_rows), pl.ds(first, units)],
                send.at[pl.ds(0, up_rows), :],
            )
            for c in range(strips):
                row = pl.multiple_of(first + mate * down_rows + c * strip_rows, strip_rows)
                copy(
                    down_ref.at[pl.ds(row, strip_rows), :],
                    send.at[pl.ds(up_rows, strip_rows), pl.ds(c * depth, depth)],
                )
        for one in copies:
            one.wait()

    return pl.pallas_call(
        kernel,
        out_shape=[jax.ShapeDtypeStruct((2 * up_rows, units), w_up.dtype)] * (n_dp - 1),
        in_specs=[pl.BlockSpec(memory_space=pl.ANY)] * 2,
        out_specs=[pl.BlockSpec(memory_space=pl.ANY)] * (n_dp - 1),
        scratch_shapes=[pltpu.SemaphoreType.DMA(((n_dp - 1) * (1 + strips),))],
        name="pack_weights",
    )(w_up, w_down)


def unpack_weights(w_up, w_down, got, mates):
    n_dp = lax.axis_size("dp")
    depth, units = w_up.shape[0], w_up.shape[1] // n_dp
    up_rows, down_rows, strips = depth // mates, units // mates, units // depth
    strip_rows = down_rows // strips

    def kernel(up_ref, down_ref, *rest):
        pieces, (up_out, down_out, sem) = rest[:-3], rest[-3:]
        place, mate = lax.axis_index("dp"), lax.rem(lax.axis_index("groups"), mates)
        copies = []

        def copy(src, dst):
            one = pltpu.make_async_copy(src, dst, sem.at[len(copies)])
            one.start()
            copies.append(one)

        copy(
            up_ref.at[:, pl.ds(pl.multiple_of(place * units, units), units)],
            up_out.at[pl.ds(pl.multiple_of(place * depth, depth), depth), :],
        )
        copy(
            down_ref.at[pl.ds(pl.multiple_of(place * units, units), units), :],
            down_out.at[:, pl.ds(pl.multiple_of(place * depth, depth), depth)],
        )
        for k in range(1, n_dp):
            first = pl.multiple_of((place ^ k) * depth, depth)
            for j in range(mates):
                piece = pieces[j * (n_dp - 1) + k - 1]
                part = mate ^ j
                row = pl.multiple_of(first + part * up_rows, up_rows)
                copy(piece.at[pl.ds(0, up_rows), :], up_out.at[pl.ds(row, up_rows), :])
                for c in range(strips):
                    row = pl.multiple_of(part * down_rows + c * strip_rows, strip_rows)
                    copy(
                        piece.at[pl.ds(up_rows, strip_rows), pl.ds(c * depth, depth)],
                        down_out.at[pl.ds(row, strip_rows), pl.ds(first, depth)],
                    )
        for one in copies:
            one.wait()

    return pl.pallas_call(
        kernel,
        out_shape=[
            jax.ShapeDtypeStruct((depth * n_dp, units), w_up.dtype),
            jax.ShapeDtypeStruct((units, depth * n_dp), w_down.dtype),
        ],
        in_specs=[pl.BlockSpec(memory_space=pl.ANY)] * (2 + mates * (n_dp - 1)),
        out_specs=[pl.BlockSpec(memory_space=pl.ANY)] * 2,
        scratch_shapes=[pltpu.SemaphoreType.DMA((2 + mates * (n_dp - 1) * (1 + strips),))],
        name="unpack_weights",
    )(w_up, w_down, *[piece for pieces in got for piece in pieces])


def weight_grads(place, chunks, hiddens, grad_pres, n_dp):
    n_chunks, (_, rows, width), units = len(chunks), chunks[0].shape, hiddens[0].shape[1]
    depth = width // n_dp
    strips = units // depth

    def kernel(place_ref, *refs):
        toks, hids, pres = refs[:n_chunks], refs[n_chunks : 2 * n_chunks], refs[2 * n_chunks : -1]
        out = refs[-1]
        up = down = None
        for tok, hid, pre in zip(toks, hids, pres, strict=True):
            one = contract_tokens(tok[0], pre[...])
            two = contract_tokens(hid[...], tok[1])
            up, down = (one, two) if up is None else (up + one, down + two)
        out[0, :depth, :] = up.astype(out.dtype)
        for c in range(strips):
            out[0, depth:, c * depth : (c + 1) * depth] = down[c * depth : (c + 1) * depth].astype(out.dtype)

    return pl.pallas_call(
        kernel,
        out_shape=jax.ShapeDtypeStruct((n_dp, 2 * depth, units), jnp.bfloat16),
        grid_spec=pltpu.PrefetchScalarGridSpec(
            num_scalar_prefetch=1,
            grid=(n_dp,),
            in_specs=[pl.BlockSpec((2, rows, depth), lambda k, p: (0, 0, p[0] ^ k))] * n_chunks
            + [pl.BlockSpec((rows, units), lambda k, p: (0, 0))] * (2 * n_chunks),
            out_specs=pl.BlockSpec((1, 2 * depth, units), lambda k, p: (k, 0, 0)),
        ),
        compiler_params=pltpu.CompilerParams(vmem_limit_bytes=40 * 1024 * 1024),
        cost_estimate=pl.CostEstimate(
            flops=4 * n_chunks * rows * width * units,
            bytes_accessed=4 * n_chunks * rows * (width + units) + 4 * width * units,
            transcendentals=0,
        ),
        name="weight_grads",
    )(place.reshape(1), *chunks, *hiddens, *grad_pres)


def gather_tokens_body(
    first_out, second_out, grad_first, grad_second, w_up, w_down, norm_gain, norm_bias
):
    n_dp, n_tensor, n_groups = (lax.axis_size(axis) for axis in ("dp", "tensor", "groups"))
    own_rows, depth = first_out.shape[0], w_up.shape[0]
    units = w_up.shape[1] // n_dp
    mates = 2 if n_groups % 2 == 0 else 1
    place = lax.axis_index("dp")
    standard, inv_std, normed = normalize(first_out, norm_gain, norm_bias)

    chunks = {0: jnp.stack([normed, grad_second])}
    for bit in bits_of(n_dp):
        chunks.update({k | bit: swap(chunk, "dp", bit) for k, chunk in chunks.items()})

    sends = pack_weights(w_up, w_down, mates)
    got = [[swap(sends[k - 1], "dp", k) for k in range(1, n_dp)]]
    if mates == 2:
        got.append([swap(piece, "groups", 1) for piece in got[0]])
    up, down = unpack_weights(w_up, w_down, got, mates)

    sums, hiddens, grad_pres = {}, {}, {}
    for k in sorted(chunks):
        chunk = chunks[k]
        for bit in bits_of(n_tensor):
            chunk = jnp.concatenate([chunk, swap(chunk, "tensor", bit)], axis=1)
        chunks[k] = chunk
    for k in sorted(chunks, key=lambda k: (k & 1 == 0, -k)):
        rows, grads = chunks[k][0], chunks[k][1]
        preact = jnp.dot(rows, up, preferred_element_type=jnp.float32)
        hiddens[k] = jax.nn.gelu(preact).astype(jnp.bfloat16)
        grad_hidden = contract_last(grads, down)
        grad_pres[k] = jax.vjp(jax.nn.gelu, preact)[1](grad_hidden)[0].astype(jnp.bfloat16)
        part = jnp.stack(
            [
                jnp.dot(hiddens[k], down, preferred_element_type=jnp.float32).astype(jnp.bfloat16),
                contract_last(grad_pres[k], up).astype(jnp.bfloat16),
            ]
        )
        for bit in reversed(bits_of(n_tensor)):
            half = part.shape[1] // 2
            part = part[:, :half] + swap(part[:, half:], "tensor", bit)
        sums[k] = part
    order = sorted(chunks)
    blocks = weight_grads(
        place, [chunks[k] for k in order], [hiddens[k] for k in order], [grad_pres[k] for k in order], n_dp
    )
    for bit in reversed(bits_of(n_dp)):
        for k in [k for k in sums if k & bit]:
            got = swap(sums.pop(k), "dp", bit).astype(jnp.float32)
            total = sums[k ^ bit].astype(jnp.float32) + got
            sums[k ^ bit] = total if k == bit and bit == bits_of(n_dp)[0] else total.astype(jnp.bfloat16)
    branch, grad_normed = sums[0][0], sums[0][1]
    second_in, grad_first_in, stats = finish_rows(
        branch, grad_normed, second_out, grad_first, standard, inv_std, norm_gain
    )

    grad_scale = (own_rows * n_tensor * n_dp) ** (-0.5)
    grad_up = jnp.zeros(w_up.shape, jnp.float32)
    grad_down = jnp.zeros(w_down.shape, jnp.float32)
    for k in range(n_dp):
        other = place ^ k
        block = swap(blocks[k], "dp", k) if k else blocks[k]
        block = block.astype(jnp.float32) * grad_scale
        grad_up = lax.dynamic_update_slice_in_dim(grad_up, block[:depth], other * units, 1)
        strips = [block[depth:, c * depth : (c + 1) * depth] for c in range(units // depth)]
        grad_down = lax.dynamic_update_slice_in_dim(
            grad_down, jnp.concatenate(strips, axis=0), other * units, 0
        )

    for axis in ("dp", "tensor"):
        for bit in bits_of(lax.axis_size(axis)):
            stats = stats + swap(stats, axis, bit)
    return (second_in, grad_first_in, grad_up, grad_down, stats * grad_scale)


def body(first_out, second_out, grad_first, grad_second, w_up, *rest):
    n_dp, n_tensor = lax.axis_size("dp"), lax.axis_size("tensor")
    powers = all(size & (size - 1) == 0 for size in (n_dp, n_tensor))
    few_tokens = first_out.shape[0] * n_tensor < w_up.shape[1]
    units, depth = w_up.shape[1] // n_dp, w_up.shape[0]
    fits = w_up.shape[1] % n_dp == 0 and units % depth == 0 and depth % 128 == 0
    pick = gather_tokens_body if powers and few_tokens and fits else gather_weights_body
    return pick(first_out, second_out, grad_first, grad_second, w_up, *rest)


def solution(mesh):
    in_specs = (
        P(("groups", "tensor", "dp"), None),
        P(("groups", "tensor", "dp"), None),
        P(("groups", "tensor", "dp"), None),
        P(("groups", "tensor", "dp"), None),
        P("dp", "tensor"),
        P("tensor", "dp"),
        P(),
        P(),
    )
    out_specs = (
        P(("groups", "tensor", "dp"), None),
        P(("groups", "tensor", "dp"), None),
        P(("groups", "dp"), "tensor"),
        P(("groups", "tensor"), "dp"),
        P("groups", None),
    )
    return jax.shard_map(body, mesh=mesh, in_specs=in_specs, out_specs=out_specs, check_vma=False)
```

```python
import math

import jax
import jax.numpy as jnp
from jax import lax
from jax.experimental import pallas as pl
from jax.experimental.pallas import tpu as pltpu
from jax.sharding import PartitionSpec as P

epsilon = 1e-06


def normalize(row_data, norm_gain, norm_bias):
    values = row_data.astype(jnp.float32)
    row_mean = jnp.mean(values, axis=-1, keepdims=True)
    centred = values - row_mean
    inv_std = lax.rsqrt(jnp.mean(centred * centred, axis=-1, keepdims=True) + epsilon)
    standard = centred * inv_std
    normed = (standard * norm_gain + norm_bias).astype(jnp.bfloat16)
    return (standard, inv_std, normed)


def contract_tokens(left_rows, right_rows):
    return lax.dot_general(
        left_rows, right_rows, (((0,), (0,)), ((), ())), preferred_element_type=jnp.float32
    )


def contract_last(left_rows, right_rows):
    return lax.dot_general(
        left_rows, right_rows, (((1,), (1,)), ((), ())), preferred_element_type=jnp.float32
    )


def finish_rows(branch, grad_normed, second_out, grad_first, standard, inv_std, norm_gain):
    second_in = (second_out.astype(jnp.float32) - branch).astype(jnp.bfloat16)
    grad_std = grad_normed * norm_gain
    grad_rows = inv_std * (
        grad_std
        - jnp.mean(grad_std, axis=-1, keepdims=True)
        - standard * jnp.mean(grad_std * standard, axis=-1, keepdims=True)
    )
    grad_first_in = grad_first.astype(jnp.float32) + grad_rows
    local_stats = jnp.stack([jnp.sum(grad_normed * standard, axis=0), jnp.sum(grad_normed, axis=0)])
    return second_in, grad_first_in, local_stats


def gather_weights_body(
    first_out, second_out, grad_first, grad_second, w_up, w_down, norm_gain, norm_bias
):
    own_rows = first_out.shape[0]
    up_full = lax.all_gather(w_up, "dp", axis=0, tiled=True)
    down_full = lax.all_gather(w_down, "dp", axis=1, tiled=True)
    first_all = lax.all_gather(first_out, "tensor", axis=0, tiled=True)
    grad_all = lax.all_gather(grad_second, "tensor", axis=0, tiled=True)
    standard_all, inv_std_all, normed = normalize(first_all, norm_gain, norm_bias)
    offset = lax.axis_index("tensor") * own_rows
    standard = lax.dynamic_slice_in_dim(standard_all, offset, own_rows, 0)
    inv_std = lax.dynamic_slice_in_dim(inv_std_all, offset, own_rows, 0)
    preact = jnp.dot(normed, up_full, preferred_element_type=jnp.float32)
    hidden = jax.nn.gelu(preact).astype(jnp.bfloat16)
    branch = lax.psum_scatter(
        jnp.dot(hidden, down_full, preferred_element_type=jnp.float32).astype(jnp.bfloat16),
        "tensor",
        scatter_dimension=0,
        tiled=True,
    ).astype(jnp.float32)
    tokens = own_rows * lax.axis_size("tensor") * lax.axis_size("dp")
    grad_scale = tokens ** (-0.5)
    grad_down_part = contract_tokens(hidden, grad_all)
    grad_down = (
        lax.psum_scatter(
            grad_down_part.astype(jnp.bfloat16), "dp", scatter_dimension=1, tiled=True
        ).astype(jnp.float32)
        * grad_scale
    )
    grad_hidden = contract_last(grad_all, down_full)
    grad_pre = jax.vjp(jax.nn.gelu, preact)[1](grad_hidden)[0].astype(jnp.bfloat16)
    grad_up_part = contract_tokens(normed, grad_pre)
    grad_up = (
        lax.psum_scatter(
            grad_up_part.astype(jnp.bfloat16), "dp", scatter_dimension=0, tiled=True
        ).astype(jnp.float32)
        * grad_scale
    )
    grad_normed = lax.psum_scatter(
        contract_last(grad_pre, up_full).astype(jnp.bfloat16),
        "tensor",
        scatter_dimension=0,
        tiled=True,
    ).astype(jnp.float32)
    second_in, grad_first_in, local_stats = finish_rows(
        branch, grad_normed, second_out, grad_first, standard, inv_std, norm_gain
    )
    grad_norm = lax.psum(local_stats, ("tensor", "dp")) * grad_scale
    return (second_in, grad_first_in, grad_up, grad_down, grad_norm)


def swap(values, axis, mask):
    return lax.ppermute(values, axis, [(i, i ^ mask) for i in range(lax.axis_size(axis))])


def bits_of(size):
    return [1 << b for b in reversed(range(size.bit_length() - 1))]


def pack_weights(w_up, w_down, mates):
    n_dp = lax.axis_size("dp")
    depth, units = w_up.shape[0], w_up.shape[1] // n_dp
    up_rows, down_rows, strips = depth // mates, units // mates, units // depth
    strip_rows = down_rows // strips

    def kernel(up_ref, down_ref, *sends):
        place, mate = lax.axis_index("dp"), lax.rem(lax.axis_index("groups"), mates)
        for k in range(1, n_dp):
            first = pl.multiple_of((place ^ k) * units, units)
            send = sends[k - 1]
            row = pl.multiple_of(mate * up_rows, up_rows)
            send[:up_rows, :] = up_ref[pl.ds(row, up_rows), pl.ds(first, units)]
            for c in range(strips):
                row = pl.multiple_of(first + mate * down_rows + c * strip_rows, strip_rows)
                send[up_rows:, c * depth : (c + 1) * depth] = down_ref[pl.ds(row, strip_rows), :]

    return pl.pallas_call(
        kernel,
        out_shape=[jax.ShapeDtypeStruct((2 * up_rows, units), w_up.dtype)] * (n_dp - 1),
        in_specs=[pl.BlockSpec(memory_space=pltpu.VMEM)] * 2,
        out_specs=[pl.BlockSpec(memory_space=pltpu.VMEM)] * (n_dp - 1),
        cost_estimate=pl.CostEstimate(flops=0, bytes_accessed=8 * w_up.size, transcendentals=0),
        name="pack_weights",
    )(w_up, w_down)


def unpack_weights(w_up, w_down, got, mates):
    n_dp = lax.axis_size("dp")
    depth, units = w_up.shape[0], w_up.shape[1] // n_dp
    up_rows, down_rows, strips = depth // mates, units // mates, units // depth
    strip_rows = down_rows // strips

    def kernel(up_ref, down_ref, *rest):
        pieces, (up_out, down_out, sem) = rest[:-3], rest[-3:]
        place, mate = lax.axis_index("dp"), lax.rem(lax.axis_index("groups"), mates)
        copies = []

        def copy(src, dst):
            one = pltpu.make_async_copy(src, dst, sem.at[len(copies)])
            one.start()
            copies.append(one)

        copy(
            up_ref.at[:, pl.ds(pl.multiple_of(place * units, units), units)],
            up_out.at[pl.ds(pl.multiple_of(place * depth, depth), depth), :],
        )
        copy(
            down_ref.at[pl.ds(pl.multiple_of(place * units, units), units), :],
            down_out.at[:, pl.ds(pl.multiple_of(place * depth, depth), depth)],
        )
        for k in range(1, n_dp):
            first = pl.multiple_of((place ^ k) * depth, depth)
            for j in range(mates):
                piece = pieces[j * (n_dp - 1) + k - 1]
                part = mate ^ j
                row = pl.multiple_of(first + part * up_rows, up_rows)
                copy(piece.at[pl.ds(0, up_rows), :], up_out.at[pl.ds(row, up_rows), :])
                for c in range(strips):
                    row = pl.multiple_of(part * down_rows + c * strip_rows, strip_rows)
                    copy(
                        piece.at[pl.ds(up_rows, strip_rows), pl.ds(c * depth, depth)],
                        down_out.at[pl.ds(row, strip_rows), pl.ds(first, depth)],
                    )
        for one in copies:
            one.wait()

    return pl.pallas_call(
        kernel,
        out_shape=[
            jax.ShapeDtypeStruct((depth * n_dp, units), w_up.dtype),
            jax.ShapeDtypeStruct((units, depth * n_dp), w_down.dtype),
        ],
        in_specs=[pl.BlockSpec(memory_space=pl.ANY)] * (2 + mates * (n_dp - 1)),
        out_specs=[pl.BlockSpec(memory_space=pltpu.VMEM)] * 2,
        scratch_shapes=[pltpu.SemaphoreType.DMA((2 + mates * (n_dp - 1) * (1 + strips),))],
        cost_estimate=pl.CostEstimate(flops=0, bytes_accessed=16 * w_up.size, transcendentals=0),
        name="unpack_weights",
    )(w_up, w_down, *[piece for pieces in got for piece in pieces])


def weight_grads(place, chunks, hiddens, grad_pres, n_dp):
    n_chunks, (_, rows, width), units = len(chunks), chunks[0].shape, hiddens[0].shape[1]
    depth = width // n_dp
    strips = units // depth

    def kernel(place_ref, *refs):
        toks, hids, pres = refs[:n_chunks], refs[n_chunks : 2 * n_chunks], refs[2 * n_chunks : -1]
        out = refs[-1]
        up = down = None
        for tok, hid, pre in zip(toks, hids, pres, strict=True):
            one = contract_tokens(tok[0], pre[...])
            two = contract_tokens(hid[...], tok[1])
            up, down = (one, two) if up is None else (up + one, down + two)
        out[0, :depth, :] = up.astype(out.dtype)
        for c in range(strips):
            out[0, depth:, c * depth : (c + 1) * depth] = down[c * depth : (c + 1) * depth].astype(out.dtype)

    return pl.pallas_call(
        kernel,
        out_shape=jax.ShapeDtypeStruct((n_dp, 2 * depth, units), jnp.bfloat16),
        grid_spec=pltpu.PrefetchScalarGridSpec(
            num_scalar_prefetch=1,
            grid=(n_dp,),
            in_specs=[pl.BlockSpec((2, rows, depth), lambda k, p: (0, 0, p[0] ^ k))] * n_chunks
            + [pl.BlockSpec((rows, units), lambda k, p: (0, 0))] * (2 * n_chunks),
            out_specs=pl.BlockSpec((1, 2 * depth, units), lambda k, p: (k, 0, 0)),
        ),
        compiler_params=pltpu.CompilerParams(vmem_limit_bytes=40 * 1024 * 1024),
        cost_estimate=pl.CostEstimate(
            flops=4 * n_chunks * rows * width * units,
            bytes_accessed=4 * n_chunks * rows * (width + units) + 4 * width * units,
            transcendentals=0,
        ),
        name="weight_grads",
    )(place.reshape(1), *chunks, *hiddens, *grad_pres)


def middle(tokens, up, down):
    (_, rows, width), units = tokens.shape, up.shape[1]
    tile = rows // 2
    slope = (2.0 / math.pi) ** 0.5

    def kernel(tok_ref, up_ref, down_ref, hid_ref, pre_ref, part_ref):
        x = jnp.dot(tok_ref[0], up_ref[...], preferred_element_type=jnp.float32)
        gate = jnp.tanh(slope * (x + 0.044715 * (x * x * x)))
        half = 0.5 + 0.5 * gate
        hidden = (x * half).astype(jnp.bfloat16)
        rise = half + (0.5 * slope) * x * (1.0 - gate * gate) * (1.0 + (3 * 0.044715) * (x * x))
        grad_pre = (contract_last(tok_ref[1], down_ref[...]) * rise).astype(jnp.bfloat16)
        hid_ref[...] = hidden
        pre_ref[...] = grad_pre
        branch = jnp.dot(hidden, down_ref[...], preferred_element_type=jnp.float32)
        part_ref[0] = branch.astype(jnp.bfloat16)
        part_ref[1] = contract_last(grad_pre, up_ref[...]).astype(jnp.bfloat16)

    def both(i):
        return (0, i, 0)

    return pl.pallas_call(
        kernel,
        out_shape=[
            jax.ShapeDtypeStruct((rows, units), jnp.bfloat16),
            jax.ShapeDtypeStruct((rows, units), jnp.bfloat16),
            jax.ShapeDtypeStruct((2, rows, width), jnp.bfloat16),
        ],
        grid=(rows // tile,),
        in_specs=[
            pl.BlockSpec((2, tile, width), both),
            pl.BlockSpec((width, units), lambda i: (0, 0)),
            pl.BlockSpec((units, width), lambda i: (0, 0)),
        ],
        out_specs=[
            pl.BlockSpec((tile, units), lambda i: (i, 0)),
            pl.BlockSpec((tile, units), lambda i: (i, 0)),
            pl.BlockSpec((2, tile, width), both),
        ],
        compiler_params=pltpu.CompilerParams(vmem_limit_bytes=32 * 1024 * 1024),
        cost_estimate=pl.CostEstimate(
            flops=8 * rows * width * units,
            bytes_accessed=8 * rows * width + 4 * rows * units + 4 * width * units,
            transcendentals=rows * units,
        ),
        name="middle",
    )(tokens, up, down)


def after(values, *others):
    return lax.optimization_barrier((values, *others))[0]


def gather_tokens_body(
    first_out, second_out, grad_first, grad_second, w_up, w_down, norm_gain, norm_bias
):
    n_dp, n_tensor, n_groups = (lax.axis_size(axis) for axis in ("dp", "tensor", "groups"))
    own_rows, depth = first_out.shape[0], w_up.shape[0]
    units = w_up.shape[1] // n_dp
    mates = 2 if n_groups % 2 == 0 else 1
    place = lax.axis_index("dp")
    standard, inv_std, normed = normalize(first_out, norm_gain, norm_bias)

    chunks = {0: jnp.stack([normed, grad_second])}
    for bit in bits_of(n_dp):
        chunks.update({k | bit: swap(chunk, "dp", bit) for k, chunk in chunks.items()})
    top = bits_of(n_dp)[0]

    sends = pack_weights(w_up, w_down, mates)
    sends = [after(send, chunks[top]) if k >= top else send for k, send in enumerate(sends, 1)]
    got = [[swap(sends[k - 1], "dp", k) for k in range(1, n_dp)]]
    if mates == 2:
        got.append([swap(piece, "groups", 1) for piece in got[0]])
    up, down = unpack_weights(w_up, w_down, got, mates)

    sums, hiddens, grad_pres = {}, {}, {}
    for k in sorted(chunks):
        chunk = chunks[k]
        for bit in bits_of(n_tensor):
            chunk = jnp.concatenate([chunk, swap(chunk, "tensor", bit)], axis=1)
        chunks[k] = chunk
    order = sorted(chunks, reverse=True)
    last = None
    for k in order:
        tokens = chunks[k] if last is None else after(chunks[k], last)
        hiddens[k], grad_pres[k], part = middle(tokens, up, down)
        last = hiddens[k]
        for bit in reversed(bits_of(n_tensor)):
            half = part.shape[1] // 2
            part = part[:, :half] + swap(part[:, half:], "tensor", bit)
        sums[k] = part
    blocks = weight_grads(
        place, [chunks[k] for k in order], [hiddens[k] for k in order], [grad_pres[k] for k in order], n_dp
    )
    came = {}
    for bit in reversed(bits_of(n_dp)):
        for k in [k for k in order if k & bit and k in sums]:
            came[k] = swap(sums.pop(k), "dp", bit)
            got = came[k].astype(jnp.float32)
            total = sums[k ^ bit].astype(jnp.float32) + got
            sums[k ^ bit] = total if k == top else total.astype(jnp.bfloat16)
    branch, grad_normed = sums[0][0], sums[0][1]
    second_in, grad_first_in, stats = finish_rows(
        branch, grad_normed, second_out, grad_first, standard, inv_std, norm_gain
    )

    grad_scale = (own_rows * n_tensor * n_dp) ** (-0.5)
    grad_up = jnp.zeros(w_up.shape, jnp.float32)
    grad_down = jnp.zeros(w_down.shape, jnp.float32)
    for k in range(n_dp):
        other = place ^ k
        block = blocks[k]
        if k:
            block = swap(block if k == top else after(block, came[k & top or 1]), "dp", k)
        block = block.astype(jnp.float32) * grad_scale
        grad_up = lax.dynamic_update_slice_in_dim(grad_up, block[:depth], other * units, 1)
        strips = [block[depth:, c * depth : (c + 1) * depth] for c in range(units // depth)]
        grad_down = lax.dynamic_update_slice_in_dim(
            grad_down, jnp.concatenate(strips, axis=0), other * units, 0
        )

    for axis in ("dp", "tensor"):
        for bit in bits_of(lax.axis_size(axis)):
            stats = stats + swap(stats, axis, bit)
    return (second_in, grad_first_in, grad_up, grad_down, stats * grad_scale)


def body(first_out, second_out, grad_first, grad_second, w_up, *rest):
    n_dp, n_tensor = lax.axis_size("dp"), lax.axis_size("tensor")
    powers = all(size & (size - 1) == 0 for size in (n_dp, n_tensor))
    few_tokens = first_out.shape[0] * n_tensor < w_up.shape[1]
    units, depth = w_up.shape[1] // n_dp, w_up.shape[0]
    fits = w_up.shape[1] % n_dp == 0 and units % depth == 0 and depth % 128 == 0
    pick = gather_tokens_body if powers and few_tokens and fits else gather_weights_body
    return pick(first_out, second_out, grad_first, grad_second, w_up, *rest)


def solution(mesh):
    in_specs = (
        P(("groups", "tensor", "dp"), None),
        P(("groups", "tensor", "dp"), None),
        P(("groups", "tensor", "dp"), None),
        P(("groups", "tensor", "dp"), None),
        P("dp", "tensor"),
        P("tensor", "dp"),
        P(),
        P(),
    )
    out_specs = (
        P(("groups", "tensor", "dp"), None),
        P(("groups", "tensor", "dp"), None),
        P(("groups", "dp"), "tensor"),
        P(("groups", "tensor"), "dp"),
        P("groups", None),
    )
    return jax.shard_map(body, mesh=mesh, in_specs=in_specs, out_specs=out_specs, check_vma=False)
```

```python
import math

import jax
import jax.numpy as jnp
from jax import lax
from jax.experimental import pallas as pl
from jax.experimental.pallas import tpu as pltpu
from jax.sharding import PartitionSpec as P

epsilon = 1e-06


def normalize(row_data, norm_gain, norm_bias):
    values = row_data.astype(jnp.float32)
    row_mean = jnp.mean(values, axis=-1, keepdims=True)
    centred = values - row_mean
    inv_std = lax.rsqrt(jnp.mean(centred * centred, axis=-1, keepdims=True) + epsilon)
    standard = centred * inv_std
    normed = (standard * norm_gain + norm_bias).astype(jnp.bfloat16)
    return (standard, inv_std, normed)


def contract_tokens(left_rows, right_rows):
    return lax.dot_general(
        left_rows, right_rows, (((0,), (0,)), ((), ())), preferred_element_type=jnp.float32
    )


def contract_last(left_rows, right_rows):
    return lax.dot_general(
        left_rows, right_rows, (((1,), (1,)), ((), ())), preferred_element_type=jnp.float32
    )


def finish_rows(branch, grad_normed, second_out, grad_first, first_out, norm_gain, norm_bias):
    standard, inv_std, _ = normalize(first_out, norm_gain, norm_bias)
    second_in = (second_out.astype(jnp.float32) - branch).astype(jnp.bfloat16)
    grad_std = grad_normed * norm_gain
    grad_rows = inv_std * (
        grad_std
        - jnp.mean(grad_std, axis=-1, keepdims=True)
        - standard * jnp.mean(grad_std * standard, axis=-1, keepdims=True)
    )
    return second_in, grad_first.astype(jnp.float32) + grad_rows


def gather_weights_body(
    first_out, second_out, grad_first, grad_second, w_up, w_down, norm_gain, norm_bias
):
    own_rows = first_out.shape[0]
    up_full = lax.all_gather(w_up, "dp", axis=0, tiled=True)
    down_full = lax.all_gather(w_down, "dp", axis=1, tiled=True)
    first_all = lax.all_gather(first_out, "tensor", axis=0, tiled=True)
    grad_all = lax.all_gather(grad_second, "tensor", axis=0, tiled=True)
    standard_all, _, normed = normalize(first_all, norm_gain, norm_bias)
    offset = lax.axis_index("tensor") * own_rows
    standard = lax.dynamic_slice_in_dim(standard_all, offset, own_rows, 0)
    preact = jnp.dot(normed, up_full, preferred_element_type=jnp.float32)
    hidden = jax.nn.gelu(preact).astype(jnp.bfloat16)
    branch = lax.psum_scatter(
        jnp.dot(hidden, down_full, preferred_element_type=jnp.float32).astype(jnp.bfloat16),
        "tensor",
        scatter_dimension=0,
        tiled=True,
    ).astype(jnp.float32)
    tokens = own_rows * lax.axis_size("tensor") * lax.axis_size("dp")
    grad_scale = tokens ** (-0.5)
    grad_down_part = contract_tokens(hidden, grad_all)
    grad_down = (
        lax.psum_scatter(
            grad_down_part.astype(jnp.bfloat16), "dp", scatter_dimension=1, tiled=True
        ).astype(jnp.float32)
        * grad_scale
    )
    grad_hidden = contract_last(grad_all, down_full)
    grad_pre = jax.vjp(jax.nn.gelu, preact)[1](grad_hidden)[0].astype(jnp.bfloat16)
    grad_up_part = contract_tokens(normed, grad_pre)
    grad_up = (
        lax.psum_scatter(
            grad_up_part.astype(jnp.bfloat16), "dp", scatter_dimension=0, tiled=True
        ).astype(jnp.float32)
        * grad_scale
    )
    grad_normed = lax.psum_scatter(
        contract_last(grad_pre, up_full).astype(jnp.bfloat16),
        "tensor",
        scatter_dimension=0,
        tiled=True,
    ).astype(jnp.float32)
    second_in, grad_first_in = finish_rows(
        branch, grad_normed, second_out, grad_first, first_out, norm_gain, norm_bias
    )
    local_stats = jnp.stack([jnp.sum(grad_normed * standard, axis=0), jnp.sum(grad_normed, axis=0)])
    grad_norm = lax.psum(local_stats, ("tensor", "dp")) * grad_scale
    return (second_in, grad_first_in, grad_up, grad_down, grad_norm)


def swap(values, axis, mask, scope):
    with jax.named_scope(scope):
        return lax.ppermute(values, axis, [(i, i ^ mask) for i in range(lax.axis_size(axis))])


def bits_of(size):
    return [1 << b for b in reversed(range(size.bit_length() - 1))]


def pack(first_out, grad_second, w_up, w_down, mates):
    n_dp = lax.axis_size("dp")
    depth, units = w_up.shape[0], w_up.shape[1] // n_dp
    up_rows, down_rows, strips = depth // mates, units // mates, units // depth
    strip_rows = down_rows // strips

    def kernel(first_ref, grad_ref, up_ref, down_ref, rows_ref, *sends):
        rows_ref[0] = first_ref[...]
        rows_ref[1] = grad_ref[...]
        place, mate = lax.axis_index("dp"), lax.rem(lax.axis_index("groups"), mates)
        for k in range(1, n_dp):
            first = pl.multiple_of((place ^ k) * units, units)
            send = sends[k - 1]
            row = pl.multiple_of(mate * up_rows, up_rows)
            send[:up_rows, :] = up_ref[pl.ds(row, up_rows), pl.ds(first, units)]
            for c in range(strips):
                row = pl.multiple_of(first + mate * down_rows + c * strip_rows, strip_rows)
                send[up_rows:, c * depth : (c + 1) * depth] = down_ref[pl.ds(row, strip_rows), :]

    return pl.pallas_call(
        kernel,
        out_shape=[jax.ShapeDtypeStruct((2, *first_out.shape), first_out.dtype)]
        + [jax.ShapeDtypeStruct((2 * up_rows, units), w_up.dtype)] * (n_dp - 1),
        in_specs=[pl.BlockSpec(memory_space=pltpu.VMEM)] * 4,
        out_specs=[pl.BlockSpec(memory_space=pltpu.VMEM)] * n_dp,
        cost_estimate=pl.CostEstimate(
            flops=0, bytes_accessed=8 * (w_up.size + first_out.size), transcendentals=0
        ),
        name="pack",
    )(first_out, grad_second, w_up, w_down)


def unpack_weights(w_up, w_down, got, mates):
    n_dp = lax.axis_size("dp")
    depth, units = w_up.shape[0], w_up.shape[1] // n_dp
    up_rows, down_rows, strips = depth // mates, units // mates, units // depth
    strip_rows = down_rows // strips

    def kernel(up_ref, down_ref, *rest):
        pieces, (up_out, down_out, sem) = rest[:-3], rest[-3:]
        place, mate = lax.axis_index("dp"), lax.rem(lax.axis_index("groups"), mates)
        copies = []

        def copy(src, dst):
            one = pltpu.make_async_copy(src, dst, sem.at[len(copies)])
            one.start()
            copies.append(one)

        copy(
            up_ref.at[:, pl.ds(pl.multiple_of(place * units, units), units)],
            up_out.at[pl.ds(pl.multiple_of(place * depth, depth), depth), :],
        )
        copy(
            down_ref.at[pl.ds(pl.multiple_of(place * units, units), units), :],
            down_out.at[:, pl.ds(pl.multiple_of(place * depth, depth), depth)],
        )
        for k in range(1, n_dp):
            first = pl.multiple_of((place ^ k) * depth, depth)
            for j in range(mates):
                piece = pieces[j * (n_dp - 1) + k - 1]
                part = mate ^ j
                row = pl.multiple_of(first + part * up_rows, up_rows)
                copy(piece.at[pl.ds(0, up_rows), :], up_out.at[pl.ds(row, up_rows), :])
                for c in range(strips):
                    row = pl.multiple_of(part * down_rows + c * strip_rows, strip_rows)
                    copy(
                        piece.at[pl.ds(up_rows, strip_rows), pl.ds(c * depth, depth)],
                        down_out.at[pl.ds(row, strip_rows), pl.ds(first, depth)],
                    )
        for one in copies:
            one.wait()

    return pl.pallas_call(
        kernel,
        out_shape=[
            jax.ShapeDtypeStruct((depth * n_dp, units), w_up.dtype),
            jax.ShapeDtypeStruct((units, depth * n_dp), w_down.dtype),
        ],
        in_specs=[pl.BlockSpec(memory_space=pl.ANY)] * (2 + mates * (n_dp - 1)),
        out_specs=[pl.BlockSpec(memory_space=pltpu.VMEM)] * 2,
        scratch_shapes=[pltpu.SemaphoreType.DMA((2 + mates * (n_dp - 1) * (1 + strips),))],
        cost_estimate=pl.CostEstimate(flops=0, bytes_accessed=16 * w_up.size, transcendentals=0),
        name="unpack_weights",
    )(w_up, w_down, *[piece for pieces in got for piece in pieces])


def weight_grads(place, first, count, normeds, grads, hiddens, grad_pres, n_dp):
    n_chunks, n_pieces = len(normeds), len(grads)
    (rows, width), units = normeds[0].shape, hiddens[0].shape[1]
    piece_rows, depth = grads[0].shape[1], width // n_dp
    strips = units // depth

    def kernel(place_ref, *refs):
        out = refs[-1]
        norm = jnp.concatenate([ref[...] for ref in refs[:n_chunks]], axis=0)
        refs = refs[n_chunks:]
        grad = jnp.concatenate([ref[0] for ref in refs[:n_pieces]], axis=0)
        refs = refs[n_pieces:]
        hid = jnp.concatenate([ref[...] for ref in refs[:n_chunks]], axis=0)
        pre = jnp.concatenate([ref[...] for ref in refs[n_chunks:-1]], axis=0)
        out[0, :depth, :] = contract_tokens(norm, pre).astype(out.dtype)
        down = contract_tokens(hid, grad).astype(out.dtype)
        for c in range(strips):
            out[0, depth:, c * depth : (c + 1) * depth] = down[c * depth : (c + 1) * depth]

    return pl.pallas_call(
        kernel,
        out_shape=jax.ShapeDtypeStruct((count, 2 * depth, units), jnp.bfloat16),
        grid_spec=pltpu.PrefetchScalarGridSpec(
            num_scalar_prefetch=1,
            grid=(count,),
            in_specs=[pl.BlockSpec((rows, depth), lambda k, p: (0, p[0] ^ (first + k)))] * n_chunks
            + [pl.BlockSpec((1, piece_rows, depth), lambda k, p: (1, 0, p[0] ^ (first + k)))] * n_pieces
            + [pl.BlockSpec((rows, units), lambda k, p: (0, 0))] * (2 * n_chunks),
            out_specs=pl.BlockSpec((1, 2 * depth, units), lambda k, p: (k, 0, 0)),
        ),
        compiler_params=pltpu.CompilerParams(vmem_limit_bytes=40 * 1024 * 1024),
        cost_estimate=pl.CostEstimate(
            flops=4 * n_chunks * rows * depth * count * units,
            bytes_accessed=4 * n_chunks * rows * (depth * count + units),
            transcendentals=0,
        ),
        name="weight_grads",
    )(place.reshape(1), *normeds, *grads, *hiddens, *grad_pres)


def middle(pieces, up, down, gain, bias):
    (_, piece_rows, width), units, n = pieces[0].shape, up.shape[1], len(pieces)
    rows = n * piece_rows
    slope = (2.0 / math.pi) ** 0.5

    def kernel(*refs):
        toks, (up_ref, down_ref, gain_ref, bias_ref) = refs[:n], refs[n : n + 4]
        norm_ref, hid_ref, pre_ref, stat_ref = refs[n + 4 : n + 8]
        parts = refs[n + 8 :]
        half_n = max(n // 2, 1)
        stat_ref[...] = jnp.zeros_like(stat_ref)
        for first in range(0, n, half_n):
            here = range(first, first + half_n)
            span = slice(first * piece_rows, (first + half_n) * piece_rows)
            values = jnp.concatenate([toks[j][0] for j in here], axis=0).astype(jnp.float32)
            centred = values - jnp.mean(values, axis=-1, keepdims=True)
            inv_std = lax.rsqrt(jnp.mean(centred * centred, axis=-1, keepdims=True) + epsilon)
            standard = centred * inv_std
            normed = (standard * gain_ref[...] + bias_ref[...]).astype(jnp.bfloat16)
            grads = jnp.concatenate([toks[j][1] for j in here], axis=0)
            x = jnp.dot(normed, up_ref[...], preferred_element_type=jnp.float32)
            gate = jnp.tanh(slope * (x + 0.044715 * (x * x * x)))
            half = 0.5 + 0.5 * gate
            hidden = (x * half).astype(jnp.bfloat16)
            rise = half + (0.5 * slope) * x * (1.0 - gate * gate) * (1.0 + (3 * 0.044715) * (x * x))
            grad_pre = (contract_last(grads, down_ref[...]) * rise).astype(jnp.bfloat16)
            norm_ref[span, :] = normed
            hid_ref[span, :] = hidden
            pre_ref[span, :] = grad_pre
            branch = jnp.dot(hidden, down_ref[...], preferred_element_type=jnp.float32)
            grad_normed = contract_last(grad_pre, up_ref[...])
            stat_ref[0:1, :] += jnp.sum(grad_normed * standard, axis=0, keepdims=True)
            stat_ref[1:2, :] += jnp.sum(grad_normed, axis=0, keepdims=True)
            for j in here:
                own = slice((j - first) * piece_rows, (j - first + 1) * piece_rows)
                parts[j][0] = branch[own].astype(jnp.bfloat16)
                parts[j][1] = grad_normed[own].astype(jnp.bfloat16)

    out = pl.pallas_call(
        kernel,
        out_shape=[
            jax.ShapeDtypeStruct((rows, width), jnp.bfloat16),
            jax.ShapeDtypeStruct((rows, units), jnp.bfloat16),
            jax.ShapeDtypeStruct((rows, units), jnp.bfloat16),
            jax.ShapeDtypeStruct((2, width), jnp.float32),
        ]
        + [jax.ShapeDtypeStruct((2, piece_rows, width), jnp.bfloat16)] * n,
        in_specs=[pl.BlockSpec(memory_space=pltpu.VMEM)] * (n + 4),
        out_specs=[pl.BlockSpec(memory_space=pltpu.VMEM)] * (n + 4),
        compiler_params=pltpu.CompilerParams(vmem_limit_bytes=32 * 1024 * 1024),
        cost_estimate=pl.CostEstimate(
            flops=8 * rows * width * units,
            bytes_accessed=10 * rows * width + 4 * width * units,
            transcendentals=rows * units,
        ),
        name="middle",
    )(*pieces, up, down, gain.reshape(1, width), bias.reshape(1, width))
    return out[0], out[1], out[2], out[3], dict(enumerate(out[4:]))


def after(values, *others):
    return lax.optimization_barrier((values, *others))[0]


def gather_tokens_body(
    first_out, second_out, grad_first, grad_second, w_up, w_down, norm_gain, norm_bias
):
    n_dp, n_tensor, n_groups = (lax.axis_size(axis) for axis in ("dp", "tensor", "groups"))
    own_rows, depth = first_out.shape[0], w_up.shape[0]
    units = w_up.shape[1] // n_dp
    mates = 2 if n_groups % 2 == 0 else 1
    place = lax.axis_index("dp")
    top = bits_of(n_dp)[0]

    own, *sends = pack(first_out, grad_second, w_up, w_down, mates)
    high, others = bits_of(n_tensor)[0], bits_of(n_tensor)[1:]
    tokens, chunks, got = {0: own}, {}, {}

    def tokens_dp(k, *first):
        tokens[k] = swap(after(tokens[k & (k - 1)], *first), "dp", k & -k, f"tokens_{k}")

    def tokens_tensor(k, *first):
        start = after(tokens[k], *first)
        chunks[k] = {0: tokens[k], high: swap(start, "tensor", high, f"tokens_{k}_{high}")}
        for bit in others:
            for j in list(chunks[k]):
                chunks[k][j | bit] = swap(chunks[k][j], "tensor", bit, f"tokens_{k}_{j | bit}")

    def weights_dp(k, *first):
        got[k] = swap(after(sends[k - 1], *first), "dp", k, f"weights_{k}")

    tokens_tensor(0)
    for bit in bits_of(n_dp):
        tokens_dp(bit)
    tokens_tensor(1, chunks[0][high])
    for bit in reversed(bits_of(n_dp)):
        weights_dp(bit, tokens[1], chunks[0][high])
    for k in range(2, n_dp):
        if k & (k - 1):
            tokens_dp(k, got[1], *chunks[0].values())
            weights_dp(k, tokens[top], got[1], chunks[1][high])
        tokens_tensor(k, chunks[k - 1][high], got[1 if k <= top else top])
    got = [got[k] for k in range(1, n_dp)]
    crossed = []
    if mates == 2:
        for k, piece in enumerate(got, 1):
            first = (*crossed[-1:], *chunks[k - 2].values()) if k > 1 else ()
            crossed.append(swap(after(piece, *first), "groups", 1, f"weights_{k}"))
    got = [got, crossed]
    up, down = unpack_weights(w_up, w_down, got[:mates], mates)

    order = sorted(chunks, reverse=True)
    normeds, hiddens, grad_pres, all_stats, ready = [], [], [], [], []
    for i, k in enumerate(order):
        pieces = [chunks[k][j] for j in range(n_tensor)]
        if i >= 1:
            pieces[0] = after(pieces[0], hiddens[-1], *(ready[i - 2] if i >= 2 else ()))
        normed, hidden, grad_pre, stats, parts = middle(pieces, up, down, norm_gain, norm_bias)
        normeds.append(normed)
        hiddens.append(hidden)
        grad_pres.append(grad_pre)
        all_stats.append(stats)
        for bit in reversed(others):
            for j in sorted((j for j in parts if j & bit), reverse=True):
                parts[j ^ bit] = parts[j ^ bit] + swap(parts.pop(j), "tensor", bit, f"sums_{k}_{j}")
        ready.append((parts[0], parts[high]))
    high_came = []
    for i, k in enumerate(order):
        part = after(ready[i][1], ready[i][0], *high_came[:i][-1:])
        high_came.append(swap(part, "tensor", high, f"sums_{k}_{high}"))
    grads = [chunks[k][j] for k in order for j in range(n_tensor)]
    grads[0] = after(grads[0], *ready[-2])
    far = weight_grads(place, top, n_dp - top, normeds, grads, hiddens, grad_pres, n_dp)
    grads[0] = after(grads[0], far)
    near = weight_grads(place, 0, top, normeds, grads, hiddens, grad_pres, n_dp)
    blocks = {k: near[k] if k < top else far[k - top] for k in range(n_dp)}
    blocks[top] = swap(blocks[top], "dp", top, f"grads_{top}")

    sums, came = {}, {}
    for i, k in enumerate(order):
        sums[k] = ready[i][0] + after(high_came[i], far, *sums.values())
        if i == 0 and k != top:
            sums[k] = after(sums[k], near)
            came[k] = swap(sums[k], "dp", k & -k, f"sums_{k}")
            sums[k] = came[k]
    for bit in bits_of(n_dp)[::-1]:
        inner = [k for k in order if k & bit and k in sums and k != bit]
        for k in inner:
            if k not in came:
                came[k] = swap(sums[k], "dp", bit, f"sums_{k}")
            del sums[k]
            sums[k ^ bit] = (sums[k ^ bit].astype(jnp.float32) + came[k]).astype(jnp.bfloat16)
    last = sums[top]
    came[top] = swap(last, "dp", top, f"sums_{top}")
    for bit in bits_of(n_dp)[:0:-1]:
        came[bit] = swap(after(sums[bit], last), "dp", bit, f"sums_{bit}")
    total = sums[0].astype(jnp.float32)
    for bit in bits_of(n_dp)[::-1]:
        total = total + came[bit].astype(jnp.float32)
    sums = {0: total}
    for k in range(1, n_dp):
        if k < top:
            blocks[k] = swap(after(blocks[k], last), "dp", k, f"grads_{k}")
        elif k > top:
            blocks[k] = swap(after(blocks[k], blocks[top], last), "dp", k, f"grads_{k}")
    blocks[top] = after(blocks[top], last)
    branch, grad_normed = sums[0][0], sums[0][1]
    second_in, grad_first_in = finish_rows(
        branch, grad_normed, second_out, grad_first, first_out, norm_gain, norm_bias
    )

    stats = after(sum(all_stats), blocks[top], came[1])
    for axis in ("tensor", "dp"):
        for bit in bits_of(lax.axis_size(axis)):
            stats = stats + swap(stats, axis, bit, "stats")
    blocks[n_dp - 1] = after(blocks[n_dp - 1], stats)

    grad_scale = (own_rows * n_tensor * n_dp) ** (-0.5)
    grad_up = jnp.zeros(w_up.shape, jnp.float32)
    grad_down = jnp.zeros(w_down.shape, jnp.float32)
    for k in range(n_dp):
        other = place ^ k
        block = blocks[k].astype(jnp.float32) * grad_scale
        grad_up = lax.dynamic_update_slice_in_dim(grad_up, block[:depth], other * units, 1)
        strips = [block[depth:, c * depth : (c + 1) * depth] for c in range(units // depth)]
        grad_down = lax.dynamic_update_slice_in_dim(
            grad_down, jnp.concatenate(strips, axis=0), other * units, 0
        )

    return (second_in, grad_first_in, grad_up, grad_down, stats * grad_scale)


def body(first_out, second_out, grad_first, grad_second, w_up, *rest):
    n_dp, n_tensor = lax.axis_size("dp"), lax.axis_size("tensor")
    powers = all(size > 1 and size & (size - 1) == 0 for size in (n_dp, n_tensor))
    few_tokens = first_out.shape[0] * n_tensor < w_up.shape[1]
    units, depth = w_up.shape[1] // n_dp, w_up.shape[0]
    fits = w_up.shape[1] % n_dp == 0 and units % depth == 0 and depth % 128 == 0
    pick = gather_tokens_body if powers and few_tokens and fits else gather_weights_body
    return pick(first_out, second_out, grad_first, grad_second, w_up, *rest)


def solution(mesh):
    in_specs = (
        P(("groups", "tensor", "dp"), None),
        P(("groups", "tensor", "dp"), None),
        P(("groups", "tensor", "dp"), None),
        P(("groups", "tensor", "dp"), None),
        P("dp", "tensor"),
        P("tensor", "dp"),
        P(),
        P(),
    )
    out_specs = (
        P(("groups", "tensor", "dp"), None),
        P(("groups", "tensor", "dp"), None),
        P(("groups", "dp"), "tensor"),
        P(("groups", "tensor"), "dp"),
        P("groups", None),
    )
    return jax.shard_map(body, mesh=mesh, in_specs=in_specs, out_specs=out_specs, check_vma=False)
```

```python
import math

import jax
import jax.numpy as jnp
from jax import lax
from jax.experimental import pallas as pl
from jax.experimental.pallas import tpu as pltpu
from jax.sharding import PartitionSpec as P

epsilon = 1e-06


def normalize(row_data, norm_gain, norm_bias):
    values = row_data.astype(jnp.float32)
    row_mean = jnp.mean(values, axis=-1, keepdims=True)
    centred = values - row_mean
    inv_std = lax.rsqrt(jnp.mean(centred * centred, axis=-1, keepdims=True) + epsilon)
    standard = centred * inv_std
    normed = (standard * norm_gain + norm_bias).astype(jnp.bfloat16)
    return (standard, inv_std, normed)


def contract_tokens(left_rows, right_rows):
    return lax.dot_general(
        left_rows, right_rows, (((0,), (0,)), ((), ())), preferred_element_type=jnp.float32
    )


def contract_last(left_rows, right_rows):
    return lax.dot_general(
        left_rows, right_rows, (((1,), (1,)), ((), ())), preferred_element_type=jnp.float32
    )


def finish_rows(branch, grad_normed, second_out, grad_first, first_out, norm_gain, norm_bias):
    standard, inv_std, _ = normalize(first_out, norm_gain, norm_bias)
    second_in = (second_out.astype(jnp.float32) - branch).astype(jnp.bfloat16)
    grad_std = grad_normed * norm_gain
    grad_rows = inv_std * (
        grad_std
        - jnp.mean(grad_std, axis=-1, keepdims=True)
        - standard * jnp.mean(grad_std * standard, axis=-1, keepdims=True)
    )
    return second_in, grad_first.astype(jnp.float32) + grad_rows


def gather_weights_body(
    first_out, second_out, grad_first, grad_second, w_up, w_down, norm_gain, norm_bias
):
    own_rows = first_out.shape[0]
    up_full = lax.all_gather(w_up, "dp", axis=0, tiled=True)
    down_full = lax.all_gather(w_down, "dp", axis=1, tiled=True)
    first_all = lax.all_gather(first_out, "tensor", axis=0, tiled=True)
    grad_all = lax.all_gather(grad_second, "tensor", axis=0, tiled=True)
    standard_all, _, normed = normalize(first_all, norm_gain, norm_bias)
    offset = lax.axis_index("tensor") * own_rows
    standard = lax.dynamic_slice_in_dim(standard_all, offset, own_rows, 0)
    preact = jnp.dot(normed, up_full, preferred_element_type=jnp.float32)
    hidden = jax.nn.gelu(preact).astype(jnp.bfloat16)
    branch = lax.psum_scatter(
        jnp.dot(hidden, down_full, preferred_element_type=jnp.float32).astype(jnp.bfloat16),
        "tensor",
        scatter_dimension=0,
        tiled=True,
    ).astype(jnp.float32)
    tokens = own_rows * lax.axis_size("tensor") * lax.axis_size("dp")
    grad_scale = tokens ** (-0.5)
    grad_down_part = contract_tokens(hidden, grad_all)
    grad_down = (
        lax.psum_scatter(
            grad_down_part.astype(jnp.bfloat16), "dp", scatter_dimension=1, tiled=True
        ).astype(jnp.float32)
        * grad_scale
    )
    grad_hidden = contract_last(grad_all, down_full)
    grad_pre = jax.vjp(jax.nn.gelu, preact)[1](grad_hidden)[0].astype(jnp.bfloat16)
    grad_up_part = contract_tokens(normed, grad_pre)
    grad_up = (
        lax.psum_scatter(
            grad_up_part.astype(jnp.bfloat16), "dp", scatter_dimension=0, tiled=True
        ).astype(jnp.float32)
        * grad_scale
    )
    grad_normed = lax.psum_scatter(
        contract_last(grad_pre, up_full).astype(jnp.bfloat16),
        "tensor",
        scatter_dimension=0,
        tiled=True,
    ).astype(jnp.float32)
    second_in, grad_first_in = finish_rows(
        branch, grad_normed, second_out, grad_first, first_out, norm_gain, norm_bias
    )
    local_stats = jnp.stack([jnp.sum(grad_normed * standard, axis=0), jnp.sum(grad_normed, axis=0)])
    grad_norm = lax.psum(local_stats, ("tensor", "dp")) * grad_scale
    return (second_in, grad_first_in, grad_up, grad_down, grad_norm)


def swap(values, axis, mask, scope):
    with jax.named_scope(scope):
        return lax.ppermute(values, axis, [(i, i ^ mask) for i in range(lax.axis_size(axis))])


def bits_of(size):
    return [1 << b for b in reversed(range(size.bit_length() - 1))]


def pack_weights(w_up, w_down, mates):
    n_dp = lax.axis_size("dp")
    depth, units = w_up.shape[0], w_up.shape[1] // n_dp
    up_rows, down_rows, strips = depth // mates, units // mates, units // depth
    strip_rows = down_rows // strips

    def kernel(up_ref, down_ref, *sends):
        place, mate = lax.axis_index("dp"), lax.rem(lax.axis_index("groups"), mates)
        for k in range(1, n_dp):
            first = pl.multiple_of((place ^ k) * units, units)
            send = sends[k - 1]
            row = pl.multiple_of(mate * up_rows, up_rows)
            send[:up_rows, :] = up_ref[pl.ds(row, up_rows), pl.ds(first, units)]
            for c in range(strips):
                row = pl.multiple_of(first + mate * down_rows + c * strip_rows, strip_rows)
                send[up_rows:, c * depth : (c + 1) * depth] = down_ref[pl.ds(row, strip_rows), :]

    return pl.pallas_call(
        kernel,
        out_shape=[jax.ShapeDtypeStruct((2 * up_rows, units), w_up.dtype)] * (n_dp - 1),
        in_specs=[pl.BlockSpec(memory_space=pltpu.VMEM)] * 2,
        out_specs=[pl.BlockSpec(memory_space=pltpu.VMEM)] * (n_dp - 1),
        cost_estimate=pl.CostEstimate(flops=0, bytes_accessed=8 * w_up.size, transcendentals=0),
        name="pack_weights",
    )(w_up, w_down)


def unpack_weights(w_up, w_down, got, mates):
    n_dp = lax.axis_size("dp")
    depth, units = w_up.shape[0], w_up.shape[1] // n_dp
    up_rows, down_rows, strips = depth // mates, units // mates, units // depth
    strip_rows = down_rows // strips

    def kernel(up_ref, down_ref, *rest):
        pieces, (up_out, down_out, sem) = rest[:-3], rest[-3:]
        place, mate = lax.axis_index("dp"), lax.rem(lax.axis_index("groups"), mates)
        copies = []

        def copy(src, dst):
            one = pltpu.make_async_copy(src, dst, sem.at[len(copies)])
            one.start()
            copies.append(one)

        copy(
            up_ref.at[:, pl.ds(pl.multiple_of(place * units, units), units)],
            up_out.at[pl.ds(pl.multiple_of(place * depth, depth), depth), :],
        )
        copy(
            down_ref.at[pl.ds(pl.multiple_of(place * units, units), units), :],
            down_out.at[:, pl.ds(pl.multiple_of(place * depth, depth), depth)],
        )
        for k in range(1, n_dp):
            first = pl.multiple_of((place ^ k) * depth, depth)
            for j in range(mates):
                piece = pieces[j * (n_dp - 1) + k - 1]
                part = mate ^ j
                row = pl.multiple_of(first + part * up_rows, up_rows)
                copy(piece.at[pl.ds(0, up_rows), :], up_out.at[pl.ds(row, up_rows), :])
                for c in range(strips):
                    row = pl.multiple_of(part * down_rows + c * strip_rows, strip_rows)
                    copy(
                        piece.at[pl.ds(up_rows, strip_rows), pl.ds(c * depth, depth)],
                        down_out.at[pl.ds(row, strip_rows), pl.ds(first, depth)],
                    )
        for one in copies:
            one.wait()

    return pl.pallas_call(
        kernel,
        out_shape=[
            jax.ShapeDtypeStruct((depth * n_dp, units), w_up.dtype),
            jax.ShapeDtypeStruct((units, depth * n_dp), w_down.dtype),
        ],
        in_specs=[pl.BlockSpec(memory_space=pl.ANY)] * (2 + mates * (n_dp - 1)),
        out_specs=[pl.BlockSpec(memory_space=pltpu.VMEM)] * 2,
        scratch_shapes=[pltpu.SemaphoreType.DMA((2 + mates * (n_dp - 1) * (1 + strips),))],
        cost_estimate=pl.CostEstimate(flops=0, bytes_accessed=16 * w_up.size, transcendentals=0),
        name="unpack_weights",
    )(w_up, w_down, *[piece for pieces in got for piece in pieces])


def core(chunks, up, down, gain, bias, n_dp):
    n_chunks, n = len(chunks), len(chunks[0])
    (_, piece_rows, width), units = chunks[0][0].shape, up.shape[1]
    depth = width // n_dp
    strips, pair = units // depth, 2 * piece_rows
    slope = (2.0 / math.pi) ** 0.5
    dtype = up.dtype

    def kernel(*refs):
        toks, refs = refs[: n_chunks * n], refs[n_chunks * n :]
        (up_hbm, down_hbm, gain_ref, bias_ref), refs = refs[:4], refs[4:]
        outs, blocks, stat_ref = refs[: 2 * n_chunks], refs[2 * n_chunks : 2 * n_chunks + n_dp], refs[2 * n_chunks + n_dp]
        tok, norm, hid, pre, part, block, up_ref, down_ref, in_sem, w_sem, out_sem, b_sem = refs[2 * n_chunks + n_dp + 1 :]
        place = lax.axis_index("dp")
        weights = [
            pltpu.make_async_copy(up_hbm, up_ref, w_sem.at[0]),
            pltpu.make_async_copy(down_hbm, down_ref, w_sem.at[1]),
        ]
        reads = [pltpu.make_async_copy(ref, tok.at[i], in_sem.at[i]) for i, ref in enumerate(toks)]
        for one in weights[:1] + reads[:n] + weights[1:] + reads[n:]:
            one.start()
        stat_ref[...] = jnp.zeros_like(stat_ref)
        writes = []
        for i in range(n_chunks):
            for one in reads[i * n : (i + 1) * n] + (weights if i == 0 else []):
                one.wait()

            @pl.loop(0, n // 2)
            def _(t):
                at = i * n + 2 * t
                span = pl.ds(pl.multiple_of(at * piece_rows, pair), pair)
                values = tok[pl.ds(at, 2), 0].reshape(pair, width).astype(jnp.float32)
                centred = values - jnp.mean(values, axis=-1, keepdims=True)
                inv_std = lax.rsqrt(jnp.mean(centred * centred, axis=-1, keepdims=True) + epsilon)
                standard = centred * inv_std
                normed = (standard * gain_ref[...] + bias_ref[...]).astype(dtype)
                norm[span, :] = normed
                x = jnp.dot(normed, up_ref[...], preferred_element_type=jnp.float32)
                gate = jnp.tanh(slope * (x + 0.044715 * (x * x * x)))
                half = 0.5 + 0.5 * gate
                hidden = (x * half).astype(dtype)
                hid[span, :] = hidden
                rise = half + (0.5 * slope) * x * (1.0 - gate * gate) * (1.0 + (3 * 0.044715) * (x * x))
                grads = tok[pl.ds(at, 2), 1].reshape(pair, width)
                grad_pre = (contract_last(grads, down_ref[...]) * rise).astype(dtype)
                pre[span, :] = grad_pre
                branch = jnp.dot(hidden, down_ref[...], preferred_element_type=jnp.float32)
                grad_normed = contract_last(grad_pre, up_ref[...])
                stat_ref[0:1, :] += jnp.sum(grad_normed * standard, axis=0, keepdims=True)
                stat_ref[1:2, :] += jnp.sum(grad_normed, axis=0, keepdims=True)
                for odd in range(2):
                    own = slice(odd * piece_rows, (odd + 1) * piece_rows)
                    part[2 * i + odd, t, 0] = branch[own].astype(dtype)
                    part[2 * i + odd, t, 1] = grad_normed[own].astype(dtype)

            for odd in (1, 0):
                at = 2 * i + odd
                writes.append(pltpu.make_async_copy(part.at[at], outs[at], out_sem.at[at]))
                writes[-1].start()
        top = bits_of(n_dp)[0]
        for k in sorted(range(n_dp), key=lambda k: (k < top, k)):
            columns = pl.ds(pl.multiple_of((place ^ k) * depth, depth), depth)
            block[k, :depth, :] = contract_tokens(norm[:, columns], pre[...]).astype(dtype)
            grads = tok[:, 1, :, columns].reshape(n_chunks * n * piece_rows, depth)
            down_block = contract_tokens(hid[...], grads).astype(dtype)
            for c in range(strips):
                block[k, depth:, c * depth : (c + 1) * depth] = down_block[c * depth : (c + 1) * depth]
            writes.append(pltpu.make_async_copy(block.at[k], blocks[k], b_sem.at[k]))
            writes[-1].start()
        for one in writes:
            one.wait()

    rows = n_chunks * n * piece_rows
    half = jax.ShapeDtypeStruct((n // 2, 2, piece_rows, width), dtype)
    far = pl.BlockSpec(memory_space=pl.ANY)
    near = pl.BlockSpec(memory_space=pltpu.VMEM)
    out = pl.pallas_call(
        kernel,
        out_shape=[half] * (2 * n_chunks)
        + [jax.ShapeDtypeStruct((2 * depth, units), dtype)] * n_dp
        + [jax.ShapeDtypeStruct((2, width), jnp.float32)],
        in_specs=[far] * (n_chunks * n + 2) + [near] * 2,
        out_specs=[far] * (2 * n_chunks + n_dp) + [near],
        scratch_shapes=[
            pltpu.VMEM((n_chunks * n, 2, piece_rows, width), dtype),
            pltpu.VMEM((rows, width), dtype),
            pltpu.VMEM((rows, units), dtype),
            pltpu.VMEM((rows, units), dtype),
            pltpu.VMEM((2 * n_chunks, n // 2, 2, piece_rows, width), dtype),
            pltpu.VMEM((n_dp, 2 * depth, units), dtype),
            pltpu.VMEM((width, units), dtype),
            pltpu.VMEM((units, width), dtype),
            pltpu.SemaphoreType.DMA((n_chunks * n,)),
            pltpu.SemaphoreType.DMA((2,)),
            pltpu.SemaphoreType.DMA((2 * n_chunks,)),
            pltpu.SemaphoreType.DMA((n_dp,)),
        ],
        compiler_params=pltpu.CompilerParams(vmem_limit_bytes=56 * 1024 * 1024),
        cost_estimate=pl.CostEstimate(
            flops=10 * rows * width * units,
            bytes_accessed=8 * rows * width + 8 * width * units,
            transcendentals=rows * units,
        ),
        name="core",
    )(
        *[piece for chunk in chunks for piece in chunk],
        up,
        down,
        gain.reshape(1, width),
        bias.reshape(1, width),
    )
    halves = [out[2 * i : 2 * i + 2] for i in range(n_chunks)]
    return halves, list(out[2 * n_chunks : -1]), out[-1]


def after(values, *others):
    return lax.optimization_barrier((values, *others))[0]


def gather_tokens_body(
    first_out, second_out, grad_first, grad_second, w_up, w_down, norm_gain, norm_bias
):
    n_dp, n_tensor, n_groups = (lax.axis_size(axis) for axis in ("dp", "tensor", "groups"))
    own_rows, depth = first_out.shape[0], w_up.shape[0]
    units = w_up.shape[1] // n_dp
    mates = 2 if n_groups % 2 == 0 else 1
    place = lax.axis_index("dp")
    top = bits_of(n_dp)[0]

    high, others = bits_of(n_tensor)[0], bits_of(n_tensor)[1:]
    own = jnp.stack([first_out, grad_second])
    tokens, chunks, got, crossed = {0: own}, {}, {}, {}

    def tokens_dp(k, *first):
        tokens[k] = swap(after(tokens[k & (k - 1)], *first), "dp", k & -k, f"tokens_{k}")

    def tokens_tensor(k, *first):
        start = after(tokens[k], *first)
        chunks[k] = {0: tokens[k], high: swap(start, "tensor", high, f"tokens_{k}_{high}")}
        for bit in others:
            for j in list(chunks[k]):
                chunks[k][j | bit] = swap(chunks[k][j], "tensor", bit, f"tokens_{k}_{j | bit}")

    def weights_dp(k, *first):
        got[k] = swap(after(sends[k - 1], *first), "dp", k, f"weights_{k}")

    def weights_groups(k, *first):
        crossed[k] = swap(after(got[k], *first), "groups", 1, f"weights_{k}")

    tokens_tensor(0)
    for bit in bits_of(n_dp)[:0:-1]:
        tokens_dp(bit)
    sends = pack_weights(w_up, w_down, mates)
    tokens_dp(top, sends[0])
    stage = [tokens[1], chunks[0][high]]
    tokens_tensor(1, *stage)
    for bit in reversed(bits_of(n_dp)):
        weights_dp(bit, *stage)
    stage = [tokens[top], chunks[1][high], *got.values(), *chunks[0].values()]
    for k in range(2, n_dp):
        if k & (k - 1):
            tokens_dp(k, *stage)
            weights_dp(k, *stage)
            stage = [tokens[k], got[k], chunks[k - 1][high]]
        if mates == 2:
            for other in (k - 1, k):
                if other & (other - 1) == 0 and other not in crossed:
                    weights_groups(other, *stage)
        tokens_tensor(k, *stage)
    for k in range(1, n_dp):
        if mates == 2 and k not in crossed:
            weights_groups(k, *stage, *chunks[1].values())
    got = [[pieces[k] for k in range(1, n_dp)] for pieces in (got, crossed)[:mates]]
    up, down = unpack_weights(w_up, w_down, got, mates)

    order = sorted(chunks, reverse=True)
    halves, blocks, stats = core(
        [[chunks[k][j] for j in range(n_tensor)] for k in order], up, down, norm_gain, norm_bias, n_dp
    )
    blocks = dict(enumerate(blocks))
    blocks[top] = swap(blocks[top], "dp", top, f"grads_{top}")
    stats = jnp.sum(lax.all_gather(stats, ("tensor", "dp")), axis=0)

    sums, behind = {}, ()
    for k, (even, odd) in zip(order, halves, strict=True):
        part = even + swap(odd, "tensor", 1, f"sums_{k}_1")
        for bit in reversed(bits_of(n_tensor)[:-1]):
            send = after(part[1::2], *behind)
            came = swap(send, "tensor", bit, f"sums_{k}_{bit}")
            part = part[0::2] + came
            behind = (came,)
        sums[k] = part[0]
    came = {}
    for bit in bits_of(n_dp)[::-1]:
        for k in [k for k in order if k & bit and k in sums and k != bit]:
            came[k] = swap(sums.pop(k), "dp", bit, f"sums_{k}")
            sums[k ^ bit] = (sums[k ^ bit].astype(jnp.float32) + came[k]).astype(jnp.bfloat16)
    last = sums[top]
    came[top] = swap(last, "dp", top, f"sums_{top}")
    for bit in bits_of(n_dp)[:0:-1]:
        came[bit] = swap(after(sums[bit], last), "dp", bit, f"sums_{bit}")
    total = sums[0].astype(jnp.float32)
    for bit in bits_of(n_dp)[::-1]:
        total = total + came[bit].astype(jnp.float32)
    sums = {0: total}
    for k in range(1, n_dp):
        if k < top:
            blocks[k] = swap(after(blocks[k], last), "dp", k, f"grads_{k}")
        elif k > top:
            blocks[k] = swap(after(blocks[k], blocks[top], last), "dp", k, f"grads_{k}")
    for k in range(1, n_dp):
        blocks[k] = after(blocks[k], last if k == top else total)
    branch, grad_normed = sums[0][0], sums[0][1]
    second_in, grad_first_in = finish_rows(
        branch, grad_normed, second_out, grad_first, first_out, norm_gain, norm_bias
    )

    grad_scale = (own_rows * n_tensor * n_dp) ** (-0.5)
    grad_up = jnp.zeros(w_up.shape, jnp.float32)
    grad_down = jnp.zeros(w_down.shape, jnp.float32)
    for k in range(n_dp):
        other = place ^ k
        block = blocks[k].astype(jnp.float32) * grad_scale
        grad_up = lax.dynamic_update_slice_in_dim(grad_up, block[:depth], other * units, 1)
        strips = [block[depth:, c * depth : (c + 1) * depth] for c in range(units // depth)]
        grad_down = lax.dynamic_update_slice_in_dim(
            grad_down, jnp.concatenate(strips, axis=0), other * units, 0
        )

    return (second_in, grad_first_in, grad_up, grad_down, stats * grad_scale)


def body(first_out, second_out, grad_first, grad_second, w_up, *rest):
    n_dp, n_tensor = lax.axis_size("dp"), lax.axis_size("tensor")
    powers = all(size > 1 and size & (size - 1) == 0 for size in (n_dp, n_tensor))
    few_tokens = first_out.shape[0] * n_tensor < w_up.shape[1]
    units, depth = w_up.shape[1] // n_dp, w_up.shape[0]
    fits = w_up.shape[1] % n_dp == 0 and units % depth == 0 and depth % 128 == 0
    pick = gather_tokens_body if powers and few_tokens and fits else gather_weights_body
    return pick(first_out, second_out, grad_first, grad_second, w_up, *rest)


def solution(mesh):
    in_specs = (
        P(("groups", "tensor", "dp"), None),
        P(("groups", "tensor", "dp"), None),
        P(("groups", "tensor", "dp"), None),
        P(("groups", "tensor", "dp"), None),
        P("dp", "tensor"),
        P("tensor", "dp"),
        P(),
        P(),
    )
    out_specs = (
        P(("groups", "tensor", "dp"), None),
        P(("groups", "tensor", "dp"), None),
        P(("groups", "dp"), "tensor"),
        P(("groups", "tensor"), "dp"),
        P("groups", None),
    )
    return jax.shard_map(body, mesh=mesh, in_specs=in_specs, out_specs=out_specs, check_vma=False)
```

```python
import math

import jax
import jax.numpy as jnp
from jax import lax
from jax.experimental import pallas as pl
from jax.experimental.pallas import tpu as pltpu
from jax.sharding import PartitionSpec as P

epsilon = 1e-06


def normalize(row_data, norm_gain, norm_bias):
    values = row_data.astype(jnp.float32)
    row_mean = jnp.mean(values, axis=-1, keepdims=True)
    centred = values - row_mean
    inv_std = lax.rsqrt(jnp.mean(centred * centred, axis=-1, keepdims=True) + epsilon)
    standard = centred * inv_std
    normed = (standard * norm_gain + norm_bias).astype(jnp.bfloat16)
    return (standard, inv_std, normed)


def contract_tokens(left_rows, right_rows):
    return lax.dot_general(
        left_rows, right_rows, (((0,), (0,)), ((), ())), preferred_element_type=jnp.float32
    )


def contract_last(left_rows, right_rows):
    return lax.dot_general(
        left_rows, right_rows, (((1,), (1,)), ((), ())), preferred_element_type=jnp.float32
    )


def finish_rows(branch, grad_normed, second_out, grad_first, first_out, norm_gain, norm_bias):
    standard, inv_std, _ = normalize(first_out, norm_gain, norm_bias)
    second_in = (second_out.astype(jnp.float32) - branch).astype(jnp.bfloat16)
    grad_std = grad_normed * norm_gain
    grad_rows = inv_std * (
        grad_std
        - jnp.mean(grad_std, axis=-1, keepdims=True)
        - standard * jnp.mean(grad_std * standard, axis=-1, keepdims=True)
    )
    return second_in, grad_first.astype(jnp.float32) + grad_rows


def gather_weights_body(
    first_out, second_out, grad_first, grad_second, w_up, w_down, norm_gain, norm_bias
):
    own_rows = first_out.shape[0]
    up_full = lax.all_gather(w_up, "dp", axis=0, tiled=True)
    down_full = lax.all_gather(w_down, "dp", axis=1, tiled=True)
    first_all = lax.all_gather(first_out, "tensor", axis=0, tiled=True)
    grad_all = lax.all_gather(grad_second, "tensor", axis=0, tiled=True)
    standard_all, _, normed = normalize(first_all, norm_gain, norm_bias)
    offset = lax.axis_index("tensor") * own_rows
    standard = lax.dynamic_slice_in_dim(standard_all, offset, own_rows, 0)
    preact = jnp.dot(normed, up_full, preferred_element_type=jnp.float32)
    hidden = jax.nn.gelu(preact).astype(jnp.bfloat16)
    branch = lax.psum_scatter(
        jnp.dot(hidden, down_full, preferred_element_type=jnp.float32).astype(jnp.bfloat16),
        "tensor",
        scatter_dimension=0,
        tiled=True,
    ).astype(jnp.float32)
    tokens = own_rows * lax.axis_size("tensor") * lax.axis_size("dp")
    grad_scale = tokens ** (-0.5)
    grad_down_part = contract_tokens(hidden, grad_all)
    grad_down = (
        lax.psum_scatter(
            grad_down_part.astype(jnp.bfloat16), "dp", scatter_dimension=1, tiled=True
        ).astype(jnp.float32)
        * grad_scale
    )
    grad_hidden = contract_last(grad_all, down_full)
    grad_pre = jax.vjp(jax.nn.gelu, preact)[1](grad_hidden)[0].astype(jnp.bfloat16)
    grad_up_part = contract_tokens(normed, grad_pre)
    grad_up = (
        lax.psum_scatter(
            grad_up_part.astype(jnp.bfloat16), "dp", scatter_dimension=0, tiled=True
        ).astype(jnp.float32)
        * grad_scale
    )
    grad_normed = lax.psum_scatter(
        contract_last(grad_pre, up_full).astype(jnp.bfloat16),
        "tensor",
        scatter_dimension=0,
        tiled=True,
    ).astype(jnp.float32)
    second_in, grad_first_in = finish_rows(
        branch, grad_normed, second_out, grad_first, first_out, norm_gain, norm_bias
    )
    local_stats = jnp.stack([jnp.sum(grad_normed * standard, axis=0), jnp.sum(grad_normed, axis=0)])
    grad_norm = lax.psum(local_stats, ("tensor", "dp")) * grad_scale
    return (second_in, grad_first_in, grad_up, grad_down, grad_norm)


def swap(values, axis, mask, scope):
    with jax.named_scope(scope):
        return lax.ppermute(values, axis, [(i, i ^ mask) for i in range(lax.axis_size(axis))])


def bits_of(size):
    return [1 << b for b in reversed(range(size.bit_length() - 1))]


def share(k, n_dp, mates):
    return mates if k >= bits_of(n_dp)[0] else 1


def pack_weights(w_up, w_down, mates):
    n_dp = lax.axis_size("dp")
    depth, units = w_up.shape[0], w_up.shape[1] // n_dp
    strips = units // depth

    def kernel(up_ref, down_ref, *sends):
        place, mate = lax.axis_index("dp"), lax.rem(lax.axis_index("groups"), mates)
        for k in range(1, n_dp):
            n = share(k, n_dp, mates)
            part = mate if n > 1 else 0
            rows = depth // n
            first = pl.multiple_of((place ^ k) * units, units)
            send = sends[k - 1]
            send[:rows, :] = up_ref[pl.ds(pl.multiple_of(part * rows, rows), rows), pl.ds(first, units)]
            for c in range(strips):
                row = pl.multiple_of(first + part * (units // n) + c * rows, rows)
                send[rows:, c * depth : (c + 1) * depth] = down_ref[pl.ds(row, rows), :]

    return pl.pallas_call(
        kernel,
        out_shape=[
            jax.ShapeDtypeStruct((2 * depth // share(k, n_dp, mates), units), w_up.dtype)
            for k in range(1, n_dp)
        ],
        in_specs=[pl.BlockSpec(memory_space=pltpu.VMEM)] * 2,
        out_specs=[pl.BlockSpec(memory_space=pltpu.VMEM)] * (n_dp - 1),
        cost_estimate=pl.CostEstimate(flops=0, bytes_accessed=8 * w_up.size, transcendentals=0),
        name="pack_weights",
    )(w_up, w_down)


def unpack_weights(w_up, w_down, got, mates):
    n_dp = lax.axis_size("dp")
    depth, units = w_up.shape[0], w_up.shape[1] // n_dp
    strips = units // depth
    n_copies = 2 + sum(len(got[k]) * (1 + strips) for k in got)

    def kernel(up_ref, down_ref, *rest):
        pieces, (up_out, down_out, sem) = list(rest[:-3]), rest[-3:]
        place, mate = lax.axis_index("dp"), lax.rem(lax.axis_index("groups"), mates)
        copies = []

        def copy(src, dst):
            one = pltpu.make_async_copy(src, dst, sem.at[len(copies)])
            one.start()
            copies.append(one)

        copy(
            up_ref.at[:, pl.ds(pl.multiple_of(place * units, units), units)],
            up_out.at[pl.ds(pl.multiple_of(place * depth, depth), depth), :],
        )
        copy(
            down_ref.at[pl.ds(pl.multiple_of(place * units, units), units), :],
            down_out.at[:, pl.ds(pl.multiple_of(place * depth, depth), depth)],
        )
        for k in range(1, n_dp):
            first = pl.multiple_of((place ^ k) * depth, depth)
            n = len(got[k])
            rows = depth // n
            for j in range(n):
                piece = pieces.pop(0)
                part = mate ^ j if n > 1 else 0
                row = pl.multiple_of(first + part * rows, rows)
                copy(piece.at[pl.ds(0, rows), :], up_out.at[pl.ds(row, rows), :])
                for c in range(strips):
                    row = pl.multiple_of(part * (units // n) + c * rows, rows)
                    copy(
                        piece.at[pl.ds(rows, rows), pl.ds(c * depth, depth)],
                        down_out.at[pl.ds(row, rows), pl.ds(first, depth)],
                    )
        for one in copies:
            one.wait()

    return pl.pallas_call(
        kernel,
        out_shape=[
            jax.ShapeDtypeStruct((depth * n_dp, units), w_up.dtype),
            jax.ShapeDtypeStruct((units, depth * n_dp), w_down.dtype),
        ],
        in_specs=[pl.BlockSpec(memory_space=pl.ANY)] * (2 + sum(len(got[k]) for k in got)),
        out_specs=[pl.BlockSpec(memory_space=pltpu.VMEM)] * 2,
        scratch_shapes=[pltpu.SemaphoreType.DMA((n_copies,))],
        cost_estimate=pl.CostEstimate(flops=0, bytes_accessed=16 * w_up.size, transcendentals=0),
        name="unpack_weights",
    )(w_up, w_down, *[piece for k in range(1, n_dp) for piece in got[k]])


def core(chunks, up, down, gain, bias, n_dp):
    n_chunks, n = len(chunks), len(chunks[0])
    (_, piece_rows, width), units = chunks[0][0].shape, up.shape[1]
    depth = width // n_dp
    strips, pair = units // depth, 2 * piece_rows
    slope = (2.0 / math.pi) ** 0.5
    dtype = up.dtype

    def kernel(*refs):
        toks, refs = refs[: n_chunks * n], refs[n_chunks * n :]
        (up_hbm, down_hbm, gain_ref, bias_ref), refs = refs[:4], refs[4:]
        outs, blocks, stat_ref = refs[: 2 * n_chunks], refs[2 * n_chunks : 2 * n_chunks + n_dp], refs[2 * n_chunks + n_dp]
        tok, norm, hid, pre, part, block, up_ref, down_ref, in_sem, w_sem, out_sem, b_sem = refs[2 * n_chunks + n_dp + 1 :]
        place = lax.axis_index("dp")
        weights = [
            pltpu.make_async_copy(up_hbm, up_ref, w_sem.at[0]),
            pltpu.make_async_copy(down_hbm, down_ref, w_sem.at[1]),
        ]
        reads = [pltpu.make_async_copy(ref, tok.at[i], in_sem.at[i]) for i, ref in enumerate(toks)]
        for one in weights[:1] + reads[:n] + weights[1:] + reads[n:]:
            one.start()
        stat_ref[...] = jnp.zeros_like(stat_ref)
        writes = []
        for i in range(n_chunks):
            for one in reads[i * n : (i + 1) * n] + (weights if i == 0 else []):
                one.wait()

            @pl.loop(0, n // 2)
            def _(t):
                at = i * n + 2 * t
                span = pl.ds(pl.multiple_of(at * piece_rows, pair), pair)
                values = tok[pl.ds(at, 2), 0].reshape(pair, width).astype(jnp.float32)
                centred = values - jnp.mean(values, axis=-1, keepdims=True)
                inv_std = lax.rsqrt(jnp.mean(centred * centred, axis=-1, keepdims=True) + epsilon)
                standard = centred * inv_std
                normed = (standard * gain_ref[...] + bias_ref[...]).astype(dtype)
                norm[span, :] = normed
                x = jnp.dot(normed, up_ref[...], preferred_element_type=jnp.float32)
                gate = jnp.tanh(slope * (x + 0.044715 * (x * x * x)))
                half = 0.5 + 0.5 * gate
                hidden = (x * half).astype(dtype)
                hid[span, :] = hidden
                rise = half + (0.5 * slope) * x * (1.0 - gate * gate) * (1.0 + (3 * 0.044715) * (x * x))
                grads = tok[pl.ds(at, 2), 1].reshape(pair, width)
                grad_pre = (contract_last(grads, down_ref[...]) * rise).astype(dtype)
                pre[span, :] = grad_pre
                branch = jnp.dot(hidden, down_ref[...], preferred_element_type=jnp.float32)
                grad_normed = contract_last(grad_pre, up_ref[...])
                stat_ref[0:1, :] += jnp.sum(grad_normed * standard, axis=0, keepdims=True)
                stat_ref[1:2, :] += jnp.sum(grad_normed, axis=0, keepdims=True)
                for odd in range(2):
                    own = slice(odd * piece_rows, (odd + 1) * piece_rows)
                    part[2 * i + odd, t, 0] = branch[own].astype(dtype)
                    part[2 * i + odd, t, 1] = grad_normed[own].astype(dtype)

            for odd in (1, 0):
                at = 2 * i + odd
                writes.append(pltpu.make_async_copy(part.at[at], outs[at], out_sem.at[at]))
                writes[-1].start()
        top = bits_of(n_dp)[0]
        for k in sorted(range(n_dp), key=lambda k: (k < top, k)):
            columns = pl.ds(pl.multiple_of((place ^ k) * depth, depth), depth)
            block[k, :depth, :] = contract_tokens(norm[:, columns], pre[...]).astype(dtype)
            grads = tok[:, 1, :, columns].reshape(n_chunks * n * piece_rows, depth)
            down_block = contract_tokens(hid[...], grads).astype(dtype)
            for c in range(strips):
                block[k, depth:, c * depth : (c + 1) * depth] = down_block[c * depth : (c + 1) * depth]
            writes.append(pltpu.make_async_copy(block.at[k], blocks[k], b_sem.at[k]))
            writes[-1].start()
        for one in writes:
            one.wait()

    rows = n_chunks * n * piece_rows
    half = jax.ShapeDtypeStruct((n // 2, 2, piece_rows, width), dtype)
    far = pl.BlockSpec(memory_space=pl.ANY)
    near = pl.BlockSpec(memory_space=pltpu.VMEM)
    out = pl.pallas_call(
        kernel,
        out_shape=[half] * (2 * n_chunks)
        + [jax.ShapeDtypeStruct((2 * depth, units), dtype)] * n_dp
        + [jax.ShapeDtypeStruct((2, width), jnp.float32)],
        in_specs=[far] * (n_chunks * n + 2) + [near] * 2,
        out_specs=[far] * (2 * n_chunks + n_dp) + [near],
        scratch_shapes=[
            pltpu.VMEM((n_chunks * n, 2, piece_rows, width), dtype),
            pltpu.VMEM((rows, width), dtype),
            pltpu.VMEM((rows, units), dtype),
            pltpu.VMEM((rows, units), dtype),
            pltpu.VMEM((2 * n_chunks, n // 2, 2, piece_rows, width), dtype),
            pltpu.VMEM((n_dp, 2 * depth, units), dtype),
            pltpu.VMEM((width, units), dtype),
            pltpu.VMEM((units, width), dtype),
            pltpu.SemaphoreType.DMA((n_chunks * n,)),
            pltpu.SemaphoreType.DMA((2,)),
            pltpu.SemaphoreType.DMA((2 * n_chunks,)),
            pltpu.SemaphoreType.DMA((n_dp,)),
        ],
        compiler_params=pltpu.CompilerParams(vmem_limit_bytes=56 * 1024 * 1024),
        cost_estimate=pl.CostEstimate(
            flops=10 * rows * width * units,
            bytes_accessed=8 * rows * width + 8 * width * units,
            transcendentals=rows * units,
        ),
        name="core",
    )(
        *[piece for chunk in chunks for piece in chunk],
        up,
        down,
        gain.reshape(1, width),
        bias.reshape(1, width),
    )
    halves = [out[2 * i : 2 * i + 2] for i in range(n_chunks)]
    return halves, list(out[2 * n_chunks : -1]), out[-1]


def after(values, *others):
    return lax.optimization_barrier((values, *others))[0]


def gather_tokens_body(
    first_out, second_out, grad_first, grad_second, w_up, w_down, norm_gain, norm_bias
):
    n_dp, n_tensor, n_groups = (lax.axis_size(axis) for axis in ("dp", "tensor", "groups"))
    own_rows, depth = first_out.shape[0], w_up.shape[0]
    units = w_up.shape[1] // n_dp
    mates = 2 if n_groups % 2 == 0 else 1
    place = lax.axis_index("dp")
    top = bits_of(n_dp)[0]

    high, others = bits_of(n_tensor)[0], bits_of(n_tensor)[1:]
    own = jnp.stack([first_out, grad_second])
    tokens, chunks, got, crossed = {0: own}, {}, {}, {}

    def tokens_dp(k, *first):
        tokens[k] = swap(after(tokens[k & (k - 1)], *first), "dp", k & -k, f"tokens_{k}")

    def tokens_tensor(k, *first):
        start = after(tokens[k], *first)
        chunks[k] = {0: tokens[k], high: swap(start, "tensor", high, f"tokens_{k}_{high}")}
        for bit in others:
            for j in list(chunks[k]):
                chunks[k][j | bit] = swap(chunks[k][j], "tensor", bit, f"tokens_{k}_{j | bit}")

    def weights_dp(k, *first):
        got[k] = swap(after(sends[k - 1], *first), "dp", k, f"weights_{k}")

    def weights_groups(k, *first):
        crossed[k] = swap(after(got[k], *first), "groups", 1, f"weights_{k}")

    tokens_tensor(0)
    for bit in bits_of(n_dp)[:0:-1]:
        tokens_dp(bit)
    sends = pack_weights(w_up, w_down, mates)
    tokens_dp(top)
    stage = [tokens[1], *chunks[0].values()]
    tokens_tensor(1, tokens[1], chunks[0][high])
    weights_dp(top, *stage)
    stage = [tokens[top], got[top], chunks[1][high], *chunks[0].values()]
    for k in range(2, n_dp):
        if k & (k - 1):
            tokens_dp(k, *stage)
            weights_dp(k, *stage)
            stage = [tokens[k], got[k], *chunks[k - 2].values(), chunks[k - 1][high]]
        tokens_tensor(k, *stage)
    for k in range(1, n_dp):
        if k < top:
            weights_dp(k, *stage)
        elif mates == 2:
            weights_groups(k, *stage)
    got = {k: [got[k]] + ([crossed[k]] if k in crossed else []) for k in got}
    up, down = unpack_weights(w_up, w_down, got, mates)

    order = sorted(chunks, reverse=True)
    halves, blocks, stats = core(
        [[chunks[k][j] for j in range(n_tensor)] for k in order], up, down, norm_gain, norm_bias, n_dp
    )
    blocks = dict(enumerate(blocks))
    blocks[top] = swap(blocks[top], "dp", top, f"grads_{top}")

    sums, behind = {}, ()
    for k, (even, odd) in zip(order, halves, strict=True):
        came = swap(odd, "tensor", 1, f"sums_{k}_1")
        parts = {2 * j: (even[j], came[j]) for j in range(n_tensor // 2)}
        for bit in reversed(bits_of(n_tensor)[:-1]):
            for j in [j for j in parts if j & bit]:
                send = after(sum(parts.pop(j)), *behind)
                parts[j ^ bit] += (swap(send, "tensor", bit, f"sums_{k}_{j}"),)
                behind = parts[j ^ bit][-1:]
        sums[k] = parts[0]

    def add(terms, dtype=jnp.bfloat16):
        return sum(term.astype(jnp.float32) for term in terms).astype(dtype)

    came = {}
    for bit in bits_of(n_dp)[::-1]:
        for k in [k for k in order if k & bit and k in sums and k != bit]:
            came[k] = swap(add(sums.pop(k)), "dp", bit, f"sums_{k}")
            sums[k ^ bit] += (came[k],)
    last = add(sums[top])
    came[top] = swap(last, "dp", top, f"sums_{top}")
    stats = after(stats, came[order[0]])
    for bit in bits_of(n_tensor):
        stats = stats + swap(stats, "tensor", bit, "stats")
    stats = after(stats, last)
    for bit in bits_of(n_dp):
        stats = stats + swap(stats, "dp", bit, "stats")
        if bit == top:
            first = stats
    for bit in bits_of(n_dp)[:0:-1]:
        came[bit] = swap(after(add(sums[bit]), last, first), "dp", bit, f"sums_{bit}")
    total = add((*sums[0], *(came[bit] for bit in bits_of(n_dp)[::-1])), jnp.float32)
    sums = {0: total}
    for k in range(1, n_dp):
        if k < top:
            blocks[k] = swap(after(blocks[k], last, first), "dp", k, f"grads_{k}")
        elif k > top:
            blocks[k] = swap(after(blocks[k], blocks[top], last), "dp", k, f"grads_{k}")
    for k in range(n_dp):
        blocks[k] = after(blocks[k], last if k in (0, top) else total)
    branch, grad_normed = sums[0][0], sums[0][1]
    second_in, grad_first_in = finish_rows(
        branch, grad_normed, second_out, grad_first, first_out, norm_gain, norm_bias
    )

    grad_scale = (own_rows * n_tensor * n_dp) ** (-0.5)
    grad_up = jnp.zeros(w_up.shape, jnp.float32)
    grad_down = jnp.zeros(w_down.shape, jnp.float32)
    for k in range(n_dp):
        other = place ^ k
        block = blocks[k].astype(jnp.float32) * grad_scale
        grad_up = lax.dynamic_update_slice_in_dim(grad_up, block[:depth], other * units, 1)
        strips = [block[depth:, c * depth : (c + 1) * depth] for c in range(units // depth)]
        grad_down = lax.dynamic_update_slice_in_dim(
            grad_down, jnp.concatenate(strips, axis=0), other * units, 0
        )

    return (second_in, grad_first_in, grad_up, grad_down, stats * grad_scale)


def body(first_out, second_out, grad_first, grad_second, w_up, *rest):
    n_dp, n_tensor = lax.axis_size("dp"), lax.axis_size("tensor")
    powers = all(size > 1 and size & (size - 1) == 0 for size in (n_dp, n_tensor))
    few_tokens = first_out.shape[0] * n_tensor < w_up.shape[1]
    units, depth = w_up.shape[1] // n_dp, w_up.shape[0]
    fits = w_up.shape[1] % n_dp == 0 and units % depth == 0 and depth % 128 == 0
    pick = gather_tokens_body if powers and few_tokens and fits else gather_weights_body
    return pick(first_out, second_out, grad_first, grad_second, w_up, *rest)


def solution(mesh):
    in_specs = (
        P(("groups", "tensor", "dp"), None),
        P(("groups", "tensor", "dp"), None),
        P(("groups", "tensor", "dp"), None),
        P(("groups", "tensor", "dp"), None),
        P("dp", "tensor"),
        P("tensor", "dp"),
        P(),
        P(),
    )
    out_specs = (
        P(("groups", "tensor", "dp"), None),
        P(("groups", "tensor", "dp"), None),
        P(("groups", "dp"), "tensor"),
        P(("groups", "tensor"), "dp"),
        P("groups", None),
    )
    return jax.shard_map(body, mesh=mesh, in_specs=in_specs, out_specs=out_specs, check_vma=False)
```

```python
import math

import jax
import jax.numpy as jnp
from jax import lax
from jax.experimental import pallas as pl
from jax.experimental.pallas import tpu as pltpu
from jax.sharding import PartitionSpec as P

epsilon = 1e-06


def normalize(row_data, norm_gain, norm_bias):
    values = row_data.astype(jnp.float32)
    row_mean = jnp.mean(values, axis=-1, keepdims=True)
    centred = values - row_mean
    inv_std = lax.rsqrt(jnp.mean(centred * centred, axis=-1, keepdims=True) + epsilon)
    standard = centred * inv_std
    normed = (standard * norm_gain + norm_bias).astype(jnp.bfloat16)
    return (standard, inv_std, normed)


def contract_tokens(left_rows, right_rows):
    return lax.dot_general(
        left_rows, right_rows, (((0,), (0,)), ((), ())), preferred_element_type=jnp.float32
    )


def contract_last(left_rows, right_rows):
    return lax.dot_general(
        left_rows, right_rows, (((1,), (1,)), ((), ())), preferred_element_type=jnp.float32
    )


def finish_rows(branch, grad_normed, second_out, grad_first, first_out, norm_gain, norm_bias):
    standard, inv_std, _ = normalize(first_out, norm_gain, norm_bias)
    second_in = (second_out.astype(jnp.float32) - branch).astype(jnp.bfloat16)
    grad_std = grad_normed * norm_gain
    grad_rows = inv_std * (
        grad_std
        - jnp.mean(grad_std, axis=-1, keepdims=True)
        - standard * jnp.mean(grad_std * standard, axis=-1, keepdims=True)
    )
    return second_in, grad_first.astype(jnp.float32) + grad_rows


def gather_weights_body(
    first_out, second_out, grad_first, grad_second, w_up, w_down, norm_gain, norm_bias
):
    own_rows = first_out.shape[0]
    up_full = lax.all_gather(w_up, "dp", axis=0, tiled=True)
    down_full = lax.all_gather(w_down, "dp", axis=1, tiled=True)
    first_all = lax.all_gather(first_out, "tensor", axis=0, tiled=True)
    grad_all = lax.all_gather(grad_second, "tensor", axis=0, tiled=True)
    standard_all, _, normed = normalize(first_all, norm_gain, norm_bias)
    offset = lax.axis_index("tensor") * own_rows
    standard = lax.dynamic_slice_in_dim(standard_all, offset, own_rows, 0)
    preact = jnp.dot(normed, up_full, preferred_element_type=jnp.float32)
    hidden = jax.nn.gelu(preact).astype(jnp.bfloat16)
    branch = lax.psum_scatter(
        jnp.dot(hidden, down_full, preferred_element_type=jnp.float32).astype(jnp.bfloat16),
        "tensor",
        scatter_dimension=0,
        tiled=True,
    ).astype(jnp.float32)
    tokens = own_rows * lax.axis_size("tensor") * lax.axis_size("dp")
    grad_scale = tokens ** (-0.5)
    grad_down_part = contract_tokens(hidden, grad_all)
    grad_down = (
        lax.psum_scatter(
            grad_down_part.astype(jnp.bfloat16), "dp", scatter_dimension=1, tiled=True
        ).astype(jnp.float32)
        * grad_scale
    )
    grad_hidden = contract_last(grad_all, down_full)
    grad_pre = jax.vjp(jax.nn.gelu, preact)[1](grad_hidden)[0].astype(jnp.bfloat16)
    grad_up_part = contract_tokens(normed, grad_pre)
    grad_up = (
        lax.psum_scatter(
            grad_up_part.astype(jnp.bfloat16), "dp", scatter_dimension=0, tiled=True
        ).astype(jnp.float32)
        * grad_scale
    )
    grad_normed = lax.psum_scatter(
        contract_last(grad_pre, up_full).astype(jnp.bfloat16),
        "tensor",
        scatter_dimension=0,
        tiled=True,
    ).astype(jnp.float32)
    second_in, grad_first_in = finish_rows(
        branch, grad_normed, second_out, grad_first, first_out, norm_gain, norm_bias
    )
    local_stats = jnp.stack([jnp.sum(grad_normed * standard, axis=0), jnp.sum(grad_normed, axis=0)])
    grad_norm = lax.psum(local_stats, ("tensor", "dp")) * grad_scale
    return (second_in, grad_first_in, grad_up, grad_down, grad_norm)


def swap(values, axis, mask, scope):
    with jax.named_scope(scope):
        return lax.ppermute(values, axis, [(i, i ^ mask) for i in range(lax.axis_size(axis))])


def bits_of(size):
    return [1 << b for b in reversed(range(size.bit_length() - 1))]


def share(k, n_dp, mates):
    return mates if k >= bits_of(n_dp)[0] else 1


def pack_weights(w_up, w_down, mates):
    n_dp = lax.axis_size("dp")
    depth, units = w_up.shape[0], w_up.shape[1] // n_dp
    strips = units // depth

    def kernel(up_ref, down_ref, *sends):
        place, mate = lax.axis_index("dp"), lax.rem(lax.axis_index("groups"), mates)
        for k in range(1, n_dp):
            n = share(k, n_dp, mates)
            part = mate if n > 1 else 0
            rows = depth // n
            first = pl.multiple_of((place ^ k) * units, units)
            send = sends[k - 1]
            send[:rows, :] = up_ref[pl.ds(pl.multiple_of(part * rows, rows), rows), pl.ds(first, units)]
            for c in range(strips):
                row = pl.multiple_of(first + part * (units // n) + c * rows, rows)
                send[rows:, c * depth : (c + 1) * depth] = down_ref[pl.ds(row, rows), :]

    return pl.pallas_call(
        kernel,
        out_shape=[
            jax.ShapeDtypeStruct((2 * depth // share(k, n_dp, mates), units), w_up.dtype)
            for k in range(1, n_dp)
        ],
        in_specs=[pl.BlockSpec(memory_space=pltpu.VMEM)] * 2,
        out_specs=[pl.BlockSpec(memory_space=pltpu.VMEM)] * (n_dp - 1),
        cost_estimate=pl.CostEstimate(flops=0, bytes_accessed=8 * w_up.size, transcendentals=0),
        name="pack_weights",
    )(w_up, w_down)


def unpack_weights(w_up, w_down, got, mates):
    n_dp = lax.axis_size("dp")
    depth, units = w_up.shape[0], w_up.shape[1] // n_dp
    strips = units // depth
    n_copies = 2 + sum(len(got[k]) * (1 + strips) for k in got)

    def kernel(up_ref, down_ref, *rest):
        pieces, (up_out, down_out, sem) = list(rest[:-3]), rest[-3:]
        place, mate = lax.axis_index("dp"), lax.rem(lax.axis_index("groups"), mates)
        copies = []

        def copy(src, dst):
            one = pltpu.make_async_copy(src, dst, sem.at[len(copies)])
            one.start()
            copies.append(one)

        copy(
            up_ref.at[:, pl.ds(pl.multiple_of(place * units, units), units)],
            up_out.at[pl.ds(pl.multiple_of(place * depth, depth), depth), :],
        )
        copy(
            down_ref.at[pl.ds(pl.multiple_of(place * units, units), units), :],
            down_out.at[:, pl.ds(pl.multiple_of(place * depth, depth), depth)],
        )
        for k in range(1, n_dp):
            first = pl.multiple_of((place ^ k) * depth, depth)
            n = len(got[k])
            rows = depth // n
            for j in range(n):
                piece = pieces.pop(0)
                part = mate ^ j if n > 1 else 0
                row = pl.multiple_of(first + part * rows, rows)
                copy(piece.at[pl.ds(0, rows), :], up_out.at[pl.ds(row, rows), :])
                for c in range(strips):
                    row = pl.multiple_of(part * (units // n) + c * rows, rows)
                    copy(
                        piece.at[pl.ds(rows, rows), pl.ds(c * depth, depth)],
                        down_out.at[pl.ds(row, rows), pl.ds(first, depth)],
                    )
        for one in copies:
            one.wait()

    return pl.pallas_call(
        kernel,
        out_shape=[
            jax.ShapeDtypeStruct((depth * n_dp, units), w_up.dtype),
            jax.ShapeDtypeStruct((units, depth * n_dp), w_down.dtype),
        ],
        in_specs=[pl.BlockSpec(memory_space=pl.ANY)] * (2 + sum(len(got[k]) for k in got)),
        out_specs=[pl.BlockSpec(memory_space=pltpu.VMEM)] * 2,
        scratch_shapes=[pltpu.SemaphoreType.DMA((n_copies,))],
        cost_estimate=pl.CostEstimate(flops=0, bytes_accessed=16 * w_up.size, transcendentals=0),
        name="unpack_weights",
    )(w_up, w_down, *[piece for k in range(1, n_dp) for piece in got[k]])


def core(chunks, up, down, gain, bias, n_dp):
    n_chunks, n = len(chunks), len(chunks[0])
    (_, piece_rows, width), units = chunks[0][0].shape, up.shape[1]
    depth = width // n_dp
    strips, pair = units // depth, 2 * piece_rows
    slope = (2.0 / math.pi) ** 0.5
    dtype = up.dtype

    def kernel(*refs):
        toks, refs = refs[: n_chunks * n], refs[n_chunks * n :]
        (up_hbm, down_hbm, gain_ref, bias_ref), refs = refs[:4], refs[4:]
        outs, blocks, stat_ref = refs[: 2 * n_chunks], refs[2 * n_chunks : 2 * n_chunks + n_dp], refs[2 * n_chunks + n_dp]
        tok, norm, hid, pre, part, block, up_ref, down_ref, in_sem, w_sem, out_sem, b_sem = refs[2 * n_chunks + n_dp + 1 :]
        place = lax.axis_index("dp")
        weights = [
            pltpu.make_async_copy(up_hbm, up_ref, w_sem.at[0]),
            pltpu.make_async_copy(down_hbm, down_ref, w_sem.at[1]),
        ]
        reads = [pltpu.make_async_copy(ref, tok.at[i], in_sem.at[i]) for i, ref in enumerate(toks)]
        for one in weights[:1] + reads[:n] + weights[1:] + reads[n:]:
            one.start()
        stat_ref[...] = jnp.zeros_like(stat_ref)
        writes = []
        for i in range(n_chunks):
            for one in reads[i * n : (i + 1) * n] + (weights if i == 0 else []):
                one.wait()

            @pl.loop(0, n // 2)
            def _(t):
                at = i * n + 2 * t
                span = pl.ds(pl.multiple_of(at * piece_rows, pair), pair)
                values = tok[pl.ds(at, 2), 0].reshape(pair, width).astype(jnp.float32)
                centred = values - jnp.mean(values, axis=-1, keepdims=True)
                inv_std = lax.rsqrt(jnp.mean(centred * centred, axis=-1, keepdims=True) + epsilon)
                standard = centred * inv_std
                normed = (standard * gain_ref[...] + bias_ref[...]).astype(dtype)
                norm[span, :] = normed
                x = jnp.dot(normed, up_ref[...], preferred_element_type=jnp.float32)
                gate = jnp.tanh(slope * (x + 0.044715 * (x * x * x)))
                half = 0.5 + 0.5 * gate
                hidden = (x * half).astype(dtype)
                hid[span, :] = hidden
                rise = half + (0.5 * slope) * x * (1.0 - gate * gate) * (1.0 + (3 * 0.044715) * (x * x))
                grads = tok[pl.ds(at, 2), 1].reshape(pair, width)
                grad_pre = (contract_last(grads, down_ref[...]) * rise).astype(dtype)
                pre[span, :] = grad_pre
                branch = jnp.dot(hidden, down_ref[...], preferred_element_type=jnp.float32)
                grad_normed = contract_last(grad_pre, up_ref[...])
                stat_ref[0:1, :] += jnp.sum(grad_normed * standard, axis=0, keepdims=True)
                stat_ref[1:2, :] += jnp.sum(grad_normed, axis=0, keepdims=True)
                for odd in range(2):
                    own = slice(odd * piece_rows, (odd + 1) * piece_rows)
                    part[2 * i + odd, t, 0] = branch[own].astype(dtype)
                    part[2 * i + odd, t, 1] = grad_normed[own].astype(dtype)

            for odd in (1, 0):
                at = 2 * i + odd
                writes.append(pltpu.make_async_copy(part.at[at], outs[at], out_sem.at[at]))
                writes[-1].start()
        top = bits_of(n_dp)[0]
        for k in sorted(range(n_dp), key=lambda k: (k < top, k)):
            columns = pl.ds(pl.multiple_of((place ^ k) * depth, depth), depth)
            block[k, :depth, :] = contract_tokens(norm[:, columns], pre[...]).astype(dtype)
            grads = tok[:, 1, :, columns].reshape(n_chunks * n * piece_rows, depth)
            down_block = contract_tokens(hid[...], grads).astype(dtype)
            for c in range(strips):
                block[k, depth:, c * depth : (c + 1) * depth] = down_block[c * depth : (c + 1) * depth]
            writes.append(pltpu.make_async_copy(block.at[k], blocks[k], b_sem.at[k]))
            writes[-1].start()
        for one in writes:
            one.wait()

    rows = n_chunks * n * piece_rows
    half = jax.ShapeDtypeStruct((n // 2, 2, piece_rows, width), dtype)
    far = pl.BlockSpec(memory_space=pl.ANY)
    near = pl.BlockSpec(memory_space=pltpu.VMEM)
    out = pl.pallas_call(
        kernel,
        out_shape=[half] * (2 * n_chunks)
        + [jax.ShapeDtypeStruct((2 * depth, units), dtype)] * n_dp
        + [jax.ShapeDtypeStruct((2, width), jnp.float32)],
        in_specs=[far] * (n_chunks * n + 2) + [near] * 2,
        out_specs=[far] * (2 * n_chunks + n_dp) + [near],
        scratch_shapes=[
            pltpu.VMEM((n_chunks * n, 2, piece_rows, width), dtype),
            pltpu.VMEM((rows, width), dtype),
            pltpu.VMEM((rows, units), dtype),
            pltpu.VMEM((rows, units), dtype),
            pltpu.VMEM((2 * n_chunks, n // 2, 2, piece_rows, width), dtype),
            pltpu.VMEM((n_dp, 2 * depth, units), dtype),
            pltpu.VMEM((width, units), dtype),
            pltpu.VMEM((units, width), dtype),
            pltpu.SemaphoreType.DMA((n_chunks * n,)),
            pltpu.SemaphoreType.DMA((2,)),
            pltpu.SemaphoreType.DMA((2 * n_chunks,)),
            pltpu.SemaphoreType.DMA((n_dp,)),
        ],
        compiler_params=pltpu.CompilerParams(vmem_limit_bytes=56 * 1024 * 1024),
        cost_estimate=pl.CostEstimate(
            flops=10 * rows * width * units,
            bytes_accessed=8 * rows * width + 8 * width * units,
            transcendentals=rows * units,
        ),
        name="core",
    )(
        *[piece for chunk in chunks for piece in chunk],
        up,
        down,
        gain.reshape(1, width),
        bias.reshape(1, width),
    )
    halves = [out[2 * i : 2 * i + 2] for i in range(n_chunks)]
    return halves, list(out[2 * n_chunks : -1]), out[-1]


def after(values, *others):
    return lax.optimization_barrier((values, *others))[0]


def gather_tokens_body(
    first_out, second_out, grad_first, grad_second, w_up, w_down, norm_gain, norm_bias
):
    n_dp, n_tensor, n_groups = (lax.axis_size(axis) for axis in ("dp", "tensor", "groups"))
    own_rows, depth = first_out.shape[0], w_up.shape[0]
    units = w_up.shape[1] // n_dp
    mates = 2 if n_groups % 2 == 0 else 1
    place = lax.axis_index("dp")
    top = bits_of(n_dp)[0]

    high, others = bits_of(n_tensor)[0], bits_of(n_tensor)[1:]
    own = jnp.stack([first_out, grad_second])
    tokens, chunks, got, crossed = {0: own}, {}, {}, {}

    def tokens_dp(k, *first):
        tokens[k] = swap(after(tokens[k & (k - 1)], *first), "dp", k & -k, f"tokens_{k}")

    def tokens_tensor(k, *first):
        start = after(tokens[k], *first)
        chunks[k] = {0: tokens[k], high: swap(start, "tensor", high, f"tokens_{k}_{high}")}

    def weights_dp(k, *first):
        got[k] = swap(after(sends[k - 1], *first), "dp", k, f"weights_{k}")

    def weights_groups(k, *first):
        crossed[k] = swap(after(got[k], *first), "groups", 1, f"weights_{k}")

    def tokens_rest(k, *first):
        for bit in others:
            for j in list(chunks[k]):
                piece = after(chunks[k][j], *first)
                chunks[k][j | bit] = swap(piece, "tensor", bit, f"tokens_{k}_{j | bit}")

    tokens_tensor(0)
    for bit in reversed(bits_of(n_dp)):
        tokens_dp(bit)
    sends = pack_weights(w_up, w_down, mates)
    for bit in bits_of(n_dp):
        weights_dp(bit)
    tokens_tensor(1, tokens[1], chunks[0][high])
    stage = [*tokens.values(), *got.values(), chunks[0][high]]
    tokens_rest(0, *stage)
    for k in range(2, n_dp):
        if k & (k - 1):
            tokens_dp(k, *stage)
            weights_dp(k, *stage)
            stage = [tokens[k], got[k], chunks[k - 1][high], *chunks[0].values()]
        tokens_tensor(k, *stage, chunks[k - 1][high])
        tokens_rest(k - 1, *stage)
    tokens_rest(n_dp - 1)
    if mates == 2:
        for k in range(top, n_dp):
            weights_groups(k, *(stage if k == top else []))
    got = {k: [got[k]] + ([crossed[k]] if k in crossed else []) for k in got}
    up, down = unpack_weights(w_up, w_down, got, mates)

    order = sorted(chunks, reverse=True)
    halves, blocks, stats = core(
        [[chunks[k][j] for j in range(n_tensor)] for k in order], up, down, norm_gain, norm_bias, n_dp
    )
    blocks = dict(enumerate(blocks))
    blocks[top] = swap(blocks[top], "dp", top, f"grads_{top}")

    sums, behind, hops = {}, (), []
    for k, (even, odd) in zip(order, halves, strict=True):
        came = swap(odd, "tensor", 1, f"sums_{k}_1")
        parts = {2 * j: (even[j], came[j]) for j in range(n_tensor // 2)}
        for bit in reversed(bits_of(n_tensor)[:-1]):
            for j in [j for j in parts if j & bit]:
                send = after(sum(parts.pop(j)), *behind)
                parts[j ^ bit] += (swap(send, "tensor", bit, f"sums_{k}_{j}"),)
                behind = parts[j ^ bit][-1:]
                hops += behind
        sums[k] = parts[0]

    def add(terms, dtype=jnp.bfloat16):
        return sum(term.astype(jnp.float32) for term in terms).astype(dtype)

    for bit in bits_of(n_tensor):
        stats = stats + swap(stats, "tensor", bit, "stats")
    stats = {0: stats.astype(jnp.bfloat16)}
    extra = 16

    came = {}
    for bit in bits_of(n_dp)[::-1]:
        for k in [k for k in order if k & bit and k in sums and k != bit]:
            came[k] = swap(add(sums.pop(k)), "dp", bit, f"sums_{k}")
            sums[k ^ bit] += (came[k],)
    last = add(sums[top])
    rows = jnp.pad(stats[0][:, None], ((0, 0), (0, extra - 1), (0, 0)))
    last = jnp.concatenate([last, rows], axis=1)
    came[top] = swap(last, "dp", top, f"sums_{top}")
    came[top], stats[top] = came[top][:, :own_rows], came[top][:, own_rows]
    rows = stats[0].reshape(-1, units)
    rows = jnp.pad(rows, ((0, extra - rows.shape[0]), (0, 0)))
    for k in range(1, n_dp):
        if k != top:
            block = jnp.concatenate([blocks[k], rows])
            first = [last] if k < top else [blocks[top], *hops[1:2]]
            block = swap(after(block, *first), "dp", k, f"grads_{k}")
            blocks[k], rest = block[: 2 * depth], block[2 * depth :]
            stats[k] = rest[: stats[0].size // units].reshape(stats[0].shape)
    for bit in bits_of(n_dp)[:0:-1]:
        came[bit] = swap(after(add(sums[bit]), last), "dp", bit, f"sums_{bit}")
    total = add((*sums[0], *(came[bit] for bit in bits_of(n_dp)[::-1])), jnp.float32)
    sums = {0: total}
    for k in range(n_dp):
        blocks[k] = after(blocks[k], last if k in (0, top) else hops[-1])
    stats = [stats[k].astype(jnp.float32) for k in range(n_dp)]
    while len(stats) > 1:
        stats = [one + two for one, two in zip(stats[0::2], stats[1::2], strict=True)]
    stats = stats[0]
    branch, grad_normed = sums[0][0], sums[0][1]
    second_in, grad_first_in = finish_rows(
        branch, grad_normed, second_out, grad_first, first_out, norm_gain, norm_bias
    )

    grad_scale = (own_rows * n_tensor * n_dp) ** (-0.5)
    grad_up = jnp.zeros(w_up.shape, jnp.float32)
    grad_down = jnp.zeros(w_down.shape, jnp.float32)
    for k in range(n_dp):
        other = place ^ k
        block = blocks[k].astype(jnp.float32) * grad_scale
        grad_up = lax.dynamic_update_slice_in_dim(grad_up, block[:depth], other * units, 1)
        strips = [block[depth:, c * depth : (c + 1) * depth] for c in range(units // depth)]
        grad_down = lax.dynamic_update_slice_in_dim(
            grad_down, jnp.concatenate(strips, axis=0), other * units, 0
        )

    return (second_in, grad_first_in, grad_up, grad_down, stats * grad_scale)


def body(first_out, second_out, grad_first, grad_second, w_up, *rest):
    n_dp, n_tensor = lax.axis_size("dp"), lax.axis_size("tensor")
    powers = all(size > 1 and size & (size - 1) == 0 for size in (n_dp, n_tensor))
    few_tokens = first_out.shape[0] * n_tensor < w_up.shape[1]
    units, depth = w_up.shape[1] // n_dp, w_up.shape[0]
    fits = w_up.shape[1] % n_dp == 0 and units % depth == 0 and depth % 128 == 0
    fits = fits and first_out.shape[1] % units == 0 and first_out.shape[1] <= 8 * units
    pick = gather_tokens_body if powers and few_tokens and fits else gather_weights_body
    return pick(first_out, second_out, grad_first, grad_second, w_up, *rest)


def solution(mesh):
    in_specs = (
        P(("groups", "tensor", "dp"), None),
        P(("groups", "tensor", "dp"), None),
        P(("groups", "tensor", "dp"), None),
        P(("groups", "tensor", "dp"), None),
        P("dp", "tensor"),
        P("tensor", "dp"),
        P(),
        P(),
    )
    out_specs = (
        P(("groups", "tensor", "dp"), None),
        P(("groups", "tensor", "dp"), None),
        P(("groups", "dp"), "tensor"),
        P(("groups", "tensor"), "dp"),
        P("groups", None),
    )
    return jax.shard_map(body, mesh=mesh, in_specs=in_specs, out_specs=out_specs, check_vma=False)
```

```python
import math

import jax
import jax.numpy as jnp
from jax import lax
from jax.experimental import pallas as pl
from jax.experimental.pallas import tpu as pltpu
from jax.sharding import PartitionSpec as P

epsilon = 1e-06


def normalize(row_data, norm_gain, norm_bias):
    values = row_data.astype(jnp.float32)
    row_mean = jnp.mean(values, axis=-1, keepdims=True)
    centred = values - row_mean
    inv_std = lax.rsqrt(jnp.mean(centred * centred, axis=-1, keepdims=True) + epsilon)
    standard = centred * inv_std
    normed = (standard * norm_gain + norm_bias).astype(jnp.bfloat16)
    return (standard, inv_std, normed)


def contract_tokens(left_rows, right_rows):
    return lax.dot_general(
        left_rows, right_rows, (((0,), (0,)), ((), ())), preferred_element_type=jnp.float32
    )


def contract_last(left_rows, right_rows):
    return lax.dot_general(
        left_rows, right_rows, (((1,), (1,)), ((), ())), preferred_element_type=jnp.float32
    )


def finish_rows(branch, grad_normed, second_out, grad_first, first_out, norm_gain, norm_bias):
    standard, inv_std, _ = normalize(first_out, norm_gain, norm_bias)
    second_in = (second_out.astype(jnp.float32) - branch).astype(jnp.bfloat16)
    grad_std = grad_normed * norm_gain
    grad_rows = inv_std * (
        grad_std
        - jnp.mean(grad_std, axis=-1, keepdims=True)
        - standard * jnp.mean(grad_std * standard, axis=-1, keepdims=True)
    )
    return second_in, grad_first.astype(jnp.float32) + grad_rows


def gather_weights_body(
    first_out, second_out, grad_first, grad_second, w_up, w_down, norm_gain, norm_bias
):
    own_rows = first_out.shape[0]
    up_full = lax.all_gather(w_up, "dp", axis=0, tiled=True)
    down_full = lax.all_gather(w_down, "dp", axis=1, tiled=True)
    first_all = lax.all_gather(first_out, "tensor", axis=0, tiled=True)
    grad_all = lax.all_gather(grad_second, "tensor", axis=0, tiled=True)
    standard_all, _, normed = normalize(first_all, norm_gain, norm_bias)
    offset = lax.axis_index("tensor") * own_rows
    standard = lax.dynamic_slice_in_dim(standard_all, offset, own_rows, 0)
    preact = jnp.dot(normed, up_full, preferred_element_type=jnp.float32)
    hidden = jax.nn.gelu(preact).astype(jnp.bfloat16)
    branch = lax.psum_scatter(
        jnp.dot(hidden, down_full, preferred_element_type=jnp.float32).astype(jnp.bfloat16),
        "tensor",
        scatter_dimension=0,
        tiled=True,
    ).astype(jnp.float32)
    tokens = own_rows * lax.axis_size("tensor") * lax.axis_size("dp")
    grad_scale = tokens ** (-0.5)
    grad_down_part = contract_tokens(hidden, grad_all)
    grad_down = (
        lax.psum_scatter(
            grad_down_part.astype(jnp.bfloat16), "dp", scatter_dimension=1, tiled=True
        ).astype(jnp.float32)
        * grad_scale
    )
    grad_hidden = contract_last(grad_all, down_full)
    grad_pre = jax.vjp(jax.nn.gelu, preact)[1](grad_hidden)[0].astype(jnp.bfloat16)
    grad_up_part = contract_tokens(normed, grad_pre)
    grad_up = (
        lax.psum_scatter(
            grad_up_part.astype(jnp.bfloat16), "dp", scatter_dimension=0, tiled=True
        ).astype(jnp.float32)
        * grad_scale
    )
    grad_normed = lax.psum_scatter(
        contract_last(grad_pre, up_full).astype(jnp.bfloat16),
        "tensor",
        scatter_dimension=0,
        tiled=True,
    ).astype(jnp.float32)
    second_in, grad_first_in = finish_rows(
        branch, grad_normed, second_out, grad_first, first_out, norm_gain, norm_bias
    )
    local_stats = jnp.stack([jnp.sum(grad_normed * standard, axis=0), jnp.sum(grad_normed, axis=0)])
    grad_norm = lax.psum(local_stats, ("tensor", "dp")) * grad_scale
    return (second_in, grad_first_in, grad_up, grad_down, grad_norm)


def swap(values, axis, mask, scope):
    with jax.named_scope(scope):
        return lax.ppermute(values, axis, [(i, i ^ mask) for i in range(lax.axis_size(axis))])


def bits_of(size):
    return [1 << b for b in reversed(range(size.bit_length() - 1))]


def share(k, n_dp, mates):
    return mates if k >= bits_of(n_dp)[0] else 1


def pack_weights(w_up, w_down, mates):
    n_dp = lax.axis_size("dp")
    depth, units = w_up.shape[0], w_up.shape[1] // n_dp
    strips = units // depth

    def kernel(up_ref, down_ref, *sends):
        place, mate = lax.axis_index("dp"), lax.rem(lax.axis_index("groups"), mates)
        for k in range(1, n_dp):
            n = share(k, n_dp, mates)
            part = mate if n > 1 else 0
            rows = depth // n
            first = pl.multiple_of((place ^ k) * units, units)
            send = sends[k - 1]
            send[:, :units] = up_ref[pl.ds(pl.multiple_of(part * rows, rows), rows), pl.ds(first, units)]
            for c in range(strips):
                row = pl.multiple_of(first + part * (units // n) + c * rows, rows)
                send[:, units + c * depth : units + (c + 1) * depth] = down_ref[pl.ds(row, rows), :]

    return pl.pallas_call(
        kernel,
        out_shape=[
            jax.ShapeDtypeStruct((depth // share(k, n_dp, mates), 2 * units), w_up.dtype)
            for k in range(1, n_dp)
        ],
        in_specs=[pl.BlockSpec(memory_space=pltpu.VMEM)] * 2,
        out_specs=[pl.BlockSpec(memory_space=pltpu.VMEM)] * (n_dp - 1),
        cost_estimate=pl.CostEstimate(flops=0, bytes_accessed=8 * w_up.size, transcendentals=0),
        name="pack_weights",
    )(w_up, w_down)


def core(chunks, w_up, w_down, got, mates, gain, bias):
    n_chunks, n, n_dp = len(chunks), len(chunks[0]), lax.axis_size("dp")
    (piece_rows, width), units = chunks[0][0].shape, w_up.shape[1] // n_dp
    piece_rows //= 2
    depth = width // n_dp
    strips, pair = units // depth, 2 * piece_rows
    slope = (2.0 / math.pi) ** 0.5
    dtype = w_up.dtype
    pieces_of_weights = [piece for k in range(1, n_dp) for piece in got[k]]
    n_got = len(pieces_of_weights)

    def kernel(*refs):
        toks, refs = refs[: n_chunks * n], refs[n_chunks * n :]
        (own_up, own_down), weights, (gain_ref, bias_ref), refs = (
            refs[:2],
            list(refs[2 : 2 + n_got]),
            refs[2 + n_got : 4 + n_got],
            refs[4 + n_got :],
        )
        outs, blocks, stat_ref = refs[: 2 * n_chunks], refs[2 * n_chunks : 2 * n_chunks + n_dp], refs[2 * n_chunks + n_dp]
        tok, norm, hid, pre, part, block, up_ref, down_ref, in_sem, w_sem, out_sem, b_sem = refs[2 * n_chunks + n_dp + 1 :]
        place, mate = lax.axis_index("dp"), lax.rem(lax.axis_index("groups"), mates)
        reads, loads, writes = [], [], []

        def load(src, dst):
            loads.append(pltpu.make_async_copy(src, dst, w_sem.at[len(loads)]))
            loads[-1].start()

        for i, ref in enumerate(toks):
            reads.append(pltpu.make_async_copy(ref, tok.at[i], in_sem.at[i]))
            if i < n:
                reads[-1].start()
        mine = pl.ds(pl.multiple_of(place * units, units), units)
        rows = pl.ds(pl.multiple_of(place * depth, depth), depth)
        load(own_up.at[:, mine], up_ref.at[rows, :])
        load(own_down.at[mine, :], down_ref.at[:, rows])
        for k in range(1, n_dp):
            first = pl.multiple_of((place ^ k) * depth, depth)
            many = len(got[k])
            rows = depth // many
            for j in range(many):
                piece = weights.pop(0)
                which = mate ^ j if many > 1 else 0
                row = pl.multiple_of(first + which * rows, rows)
                load(piece.at[:, pl.ds(0, units)], up_ref.at[pl.ds(row, rows), :])
                for c in range(strips):
                    row = pl.multiple_of(which * (units // many) + c * rows, rows)
                    load(
                        piece.at[:, pl.ds(units + c * depth, depth)],
                        down_ref.at[pl.ds(row, rows), pl.ds(first, depth)],
                    )
        for one in reads[n:]:
            one.start()
        stat_ref[...] = jnp.zeros_like(stat_ref)
        for i in range(n_chunks):
            for one in reads[i * n : (i + 1) * n] + (loads if i == 0 else []):
                one.wait()

            @pl.loop(0, n // 2)
            def _(t):
                at = i * n + 2 * t
                span = pl.ds(pl.multiple_of(at * piece_rows, pair), pair)
                values = tok[pl.ds(at, 2), :piece_rows].reshape(pair, width).astype(jnp.float32)
                centred = values - jnp.mean(values, axis=-1, keepdims=True)
                inv_std = lax.rsqrt(jnp.mean(centred * centred, axis=-1, keepdims=True) + epsilon)
                standard = centred * inv_std
                normed = (standard * gain_ref[...] + bias_ref[...]).astype(dtype)
                norm[span, :] = normed
                x = jnp.dot(normed, up_ref[...], preferred_element_type=jnp.float32)
                gate = jnp.tanh(slope * (x + 0.044715 * (x * x * x)))
                half = 0.5 + 0.5 * gate
                hidden = (x * half).astype(dtype)
                hid[span, :] = hidden
                rise = half + (0.5 * slope) * x * (1.0 - gate * gate) * (1.0 + (3 * 0.044715) * (x * x))
                grads = tok[pl.ds(at, 2), piece_rows:].reshape(pair, width)
                grad_pre = (contract_last(grads, down_ref[...]) * rise).astype(dtype)
                pre[span, :] = grad_pre
                branch = jnp.dot(hidden, down_ref[...], preferred_element_type=jnp.float32)
                grad_normed = contract_last(grad_pre, up_ref[...])
                stat_ref[0:1, :] += jnp.sum(grad_normed * standard, axis=0, keepdims=True)
                stat_ref[1:2, :] += jnp.sum(grad_normed, axis=0, keepdims=True)
                row = pl.multiple_of(t * pair, pair)
                for odd in range(2):
                    own = slice(odd * piece_rows, (odd + 1) * piece_rows)
                    part[2 * i + odd, pl.ds(row, piece_rows), :] = branch[own].astype(dtype)
                    part[2 * i + odd, pl.ds(row + piece_rows, piece_rows), :] = grad_normed[own].astype(dtype)

            for odd in (1, 0):
                at = 2 * i + odd
                writes.append(pltpu.make_async_copy(part.at[at], outs[at], out_sem.at[at]))
                writes[-1].start()
        top = bits_of(n_dp)[0]
        for k in sorted(range(n_dp), key=lambda k: (k < top, k)):
            columns = pl.ds(pl.multiple_of((place ^ k) * depth, depth), depth)
            block[k, :depth, :] = contract_tokens(norm[:, columns], pre[...]).astype(dtype)
            grads = tok[:, piece_rows:, columns].reshape(n_chunks * n * piece_rows, depth)
            down_block = contract_tokens(hid[...], grads).astype(dtype)
            for c in range(strips):
                block[k, depth:, c * depth : (c + 1) * depth] = down_block[c * depth : (c + 1) * depth]
            writes.append(pltpu.make_async_copy(block.at[k], blocks[k], b_sem.at[k]))
            writes[-1].start()
        for one in writes:
            one.wait()

    rows = n_chunks * n * piece_rows
    half = (n // 2 * pair, width)
    far = pl.BlockSpec(memory_space=pl.ANY)
    near = pl.BlockSpec(memory_space=pltpu.VMEM)
    out = pl.pallas_call(
        kernel,
        out_shape=[jax.ShapeDtypeStruct(half, dtype)] * (2 * n_chunks)
        + [jax.ShapeDtypeStruct((2 * depth, units), dtype)] * n_dp
        + [jax.ShapeDtypeStruct((2, width), jnp.float32)],
        in_specs=[far] * (n_chunks * n + 2 + n_got) + [near] * 2,
        out_specs=[far] * (2 * n_chunks + n_dp) + [near],
        scratch_shapes=[
            pltpu.VMEM((n_chunks * n, pair, width), dtype),
            pltpu.VMEM((rows, width), dtype),
            pltpu.VMEM((rows, units), dtype),
            pltpu.VMEM((rows, units), dtype),
            pltpu.VMEM((2 * n_chunks, *half), dtype),
            pltpu.VMEM((n_dp, 2 * depth, units), dtype),
            pltpu.VMEM((width, units), dtype),
            pltpu.VMEM((units, width), dtype),
            pltpu.SemaphoreType.DMA((n_chunks * n,)),
            pltpu.SemaphoreType.DMA((2 + n_got * (1 + strips),)),
            pltpu.SemaphoreType.DMA((2 * n_chunks,)),
            pltpu.SemaphoreType.DMA((n_dp,)),
        ],
        compiler_params=pltpu.CompilerParams(vmem_limit_bytes=56 * 1024 * 1024),
        cost_estimate=pl.CostEstimate(
            flops=10 * rows * width * units,
            bytes_accessed=8 * rows * width + 8 * width * units,
            transcendentals=rows * units,
        ),
        name="core",
    )(
        *[piece for chunk in chunks for piece in chunk],
        w_up,
        w_down,
        *pieces_of_weights,
        gain.reshape(1, width),
        bias.reshape(1, width),
    )
    halves = [out[2 * i : 2 * i + 2] for i in range(n_chunks)]
    return halves, list(out[2 * n_chunks : -1]), out[-1]


def finish(blocks, terms, own_stats, first_out, second_out, grad_first, gain, bias, w_shapes, scale):
    (rows, width), n_dp = first_out.shape, len(blocks)
    depth, units = w_shapes[0][0], w_shapes[0][1] // n_dp
    strips, top, n_terms = units // depth, bits_of(n_dp)[0], len(terms)

    def kernel(*refs):
        parts, adds, (stat_ref, first_ref, second_ref, grad_ref, gain_ref, bias_ref), outs = (
            refs[:n_dp],
            refs[n_dp : n_dp + n_terms],
            refs[n_dp + n_terms : n_dp + n_terms + 6],
            refs[n_dp + n_terms + 6 :],
        )
        second_in, grad_in, up_out, down_out, norm_out = outs
        place = lax.axis_index("dp")
        for k in range(n_dp):
            first = pl.multiple_of((place ^ k) * units, units)
            up_out[:, pl.ds(first, units)] = parts[k][:depth, :].astype(jnp.float32) * scale
            for c in range(strips):
                block = parts[k][depth : 2 * depth, c * depth : (c + 1) * depth]
                row = pl.multiple_of(first + c * depth, depth)
                down_out[pl.ds(row, depth), :] = block.astype(jnp.float32) * scale
        total = sum(ref[: 2 * rows, :].astype(jnp.float32) for ref in adds)
        second_in[...] = (second_ref[...].astype(jnp.float32) - total[:rows]).astype(second_in.dtype)
        values = first_ref[...].astype(jnp.float32)
        centred = values - jnp.mean(values, axis=-1, keepdims=True)
        inv_std = lax.rsqrt(jnp.mean(centred * centred, axis=-1, keepdims=True) + epsilon)
        standard = centred * inv_std
        grad_std = total[rows:] * gain_ref[...]
        grad_rows = inv_std * (
            grad_std
            - jnp.mean(grad_std, axis=-1, keepdims=True)
            - standard * jnp.mean(grad_std * standard, axis=-1, keepdims=True)
        )
        grad_in[...] = grad_ref[...].astype(jnp.float32) + grad_rows
        stats = []
        for k in range(n_dp):
            if k == 0:
                one = stat_ref[...].astype(jnp.float32)
            elif k == top:
                one = adds[-1][2 * rows :, :].astype(jnp.float32)[:2]
            else:
                tail = parts[k][2 * depth :, :].astype(jnp.float32)
                per = width // units
                one = jnp.concatenate(
                    [
                        jnp.concatenate([tail[i * per + j : i * per + j + 1] for j in range(per)], axis=1)
                        for i in range(2)
                    ],
                    axis=0,
                )
            stats.append(one)
        while len(stats) > 1:
            stats = [one + two for one, two in zip(stats[0::2], stats[1::2], strict=True)]
        norm_out[...] = stats[0] * scale

    def whole(x):
        return pl.BlockSpec(x.shape, lambda i: (0, 0))

    arrays = [*blocks, *terms, own_stats, first_out, second_out, grad_first, gain.reshape(1, width), bias.reshape(1, width)]
    in_specs = [whole(x) for x in arrays]
    for i in range(n_terms - 1):
        in_specs[n_dp + i] = pl.BlockSpec((2 * rows, width), lambda i: (0, 0))
    out_shape = [
        jax.ShapeDtypeStruct((rows, width), second_out.dtype),
        jax.ShapeDtypeStruct((rows, width), jnp.float32),
        jax.ShapeDtypeStruct(w_shapes[0], jnp.float32),
        jax.ShapeDtypeStruct(w_shapes[1], jnp.float32),
        jax.ShapeDtypeStruct((2, width), jnp.float32),
    ]
    return pl.pallas_call(
        kernel,
        out_shape=out_shape,
        grid=(1,),
        in_specs=in_specs,
        out_specs=[whole(x) for x in out_shape],
        compiler_params=pltpu.CompilerParams(vmem_limit_bytes=48 * 1024 * 1024),
        cost_estimate=pl.CostEstimate(
            flops=0, bytes_accessed=12 * w_shapes[0][0] * w_shapes[0][1], transcendentals=0
        ),
        name="finish",
    )(*arrays)


def after(values, *others):
    return lax.optimization_barrier((values, *others))[0]


def gather_tokens_body(
    first_out, second_out, grad_first, grad_second, w_up, w_down, norm_gain, norm_bias
):
    n_dp, n_tensor, n_groups = (lax.axis_size(axis) for axis in ("dp", "tensor", "groups"))
    own_rows, depth = first_out.shape[0], w_up.shape[0]
    units = w_up.shape[1] // n_dp
    mates = 2 if n_groups % 2 == 0 else 1
    place = lax.axis_index("dp")
    top = bits_of(n_dp)[0]

    high, others = bits_of(n_tensor)[0], bits_of(n_tensor)[1:]
    own = jnp.concatenate([first_out, grad_second])
    tokens, chunks, got, crossed = {0: own}, {}, {}, {}

    def tokens_dp(k, *first):
        tokens[k] = swap(after(tokens[k & (k - 1)], *first), "dp", k & -k, f"tokens_{k}")

    def tokens_tensor(k, *first):
        start = after(tokens[k], *first)
        chunks[k] = {0: tokens[k], high: swap(start, "tensor", high, f"tokens_{k}_{high}")}

    def tokens_rest(k, *first):
        for bit in others:
            for j in list(chunks[k]):
                piece = after(chunks[k][j], *first)
                chunks[k][j | bit] = swap(piece, "tensor", bit, f"tokens_{k}_{j | bit}")

    def weights_dp(k, *first):
        got[k] = swap(after(sends[k - 1], *first), "dp", k, f"weights_{k}")

    def weights_groups(k, *first):
        crossed[k] = swap(after(got[k], *first), "groups", 1, f"weights_{k}")

    tokens_tensor(0)
    for bit in bits_of(n_dp)[:0:-1]:
        tokens_dp(bit)
    sends = pack_weights(w_up, w_down, mates)
    both = swap(jnp.concatenate([own, sends[top - 1]]), "dp", top, f"tokens_weights_{top}")
    tokens[top], got[top] = both[: 2 * own_rows], both[2 * own_rows :]
    for bit in bits_of(n_dp)[1:]:
        weights_dp(bit)
    tokens_tensor(1, tokens[1], chunks[0][high])
    stage = [*tokens.values(), *got.values(), chunks[0][high]]
    tokens_rest(0, *stage)
    for k in range(2, n_dp):
        if k & (k - 1):
            tokens_dp(k, *stage)
            weights_dp(k, *stage)
            if mates == 2 and top not in crossed:
                weights_groups(top, *stage)
            stage = [tokens[k], got[k], *crossed.values(), chunks[k - 1][high], *chunks[0].values()]
        tokens_tensor(k, *stage, chunks[k - 1][high])
        tokens_rest(k - 1, *stage)
    tokens_rest(n_dp - 1)
    if mates == 2:
        for k in range(top, n_dp):
            if k not in crossed:
                weights_groups(k)
    got = {k: [got[k]] + ([crossed[k]] if k in crossed else []) for k in got}

    order = sorted(chunks, reverse=True)
    halves, blocks, stats = core(
        [[chunks[k][j] for j in range(n_tensor)] for k in order], w_up, w_down, got, mates, norm_gain, norm_bias
    )
    blocks = dict(enumerate(blocks))
    blocks[top] = swap(blocks[top], "dp", top, f"grads_{top}")

    sums, behind, hops = {}, (), []
    for k, (even, odd) in zip(order, halves, strict=True):
        came = swap(odd, "tensor", 1, f"sums_{k}_1")
        spans = [slice(j * 2 * own_rows, (j + 1) * 2 * own_rows) for j in range(n_tensor // 2)]
        parts = {2 * j: (even[span], came[span]) for j, span in enumerate(spans)}
        parts[0] = (even, came)
        for bit in reversed(bits_of(n_tensor)[:-1]):
            for j in [j for j in parts if j & bit]:
                send = after(sum(parts.pop(j)), *behind)
                if not hops:
                    stats = after(stats, send)
                parts[j ^ bit] += (swap(send, "tensor", bit, f"sums_{k}_{j}"),)
                behind = parts[j ^ bit][-1:]
                hops += behind
        sums[k] = parts[0]

    def add(terms):
        return sum(term[: 2 * own_rows].astype(jnp.float32) for term in terms).astype(jnp.bfloat16)

    for bit in bits_of(n_tensor):
        stats = stats + swap(stats, "tensor", bit, "stats")
    stats = stats.astype(jnp.bfloat16)
    extra = 16

    came = {}
    for bit in bits_of(n_dp)[::-1]:
        for k in [k for k in order if k & bit and k in sums and k != bit]:
            came[k] = swap(add(sums.pop(k)), "dp", bit, f"sums_{k}")
            sums[k ^ bit] += (came[k],)
    last = jnp.concatenate([add(sums[top]), jnp.pad(stats, ((0, extra - 2), (0, 0)))])
    came[top] = swap(last, "dp", top, f"sums_{top}")
    rows = stats.reshape(-1, units)
    rows = jnp.pad(rows, ((0, extra - rows.shape[0]), (0, 0)))
    for k in range(1, n_dp):
        if k != top:
            block = jnp.concatenate([blocks[k], rows])
            first = [last] if k < top else [blocks[top], *hops[:1]]
            blocks[k] = swap(after(block, *first), "dp", k, f"grads_{k}")
    for bit in bits_of(n_dp)[:0:-1]:
        came[bit] = swap(after(add(sums[bit]), last), "dp", bit, f"sums_{bit}")

    scale = (own_rows * n_tensor * n_dp) ** (-0.5)
    terms = [*sums[0], *(came[bit] for bit in bits_of(n_dp)[::-1])]
    return tuple(
        finish(
            [blocks[k] for k in range(n_dp)],
            terms,
            stats,
            first_out,
            second_out,
            grad_first,
            norm_gain,
            norm_bias,
            (w_up.shape, w_down.shape),
            scale,
        )
    )


def body(first_out, second_out, grad_first, grad_second, w_up, *rest):
    n_dp, n_tensor = lax.axis_size("dp"), lax.axis_size("tensor")
    powers = all(size > 1 and size & (size - 1) == 0 for size in (n_dp, n_tensor))
    few_tokens = first_out.shape[0] * n_tensor < w_up.shape[1]
    units, depth = w_up.shape[1] // n_dp, w_up.shape[0]
    fits = w_up.shape[1] % n_dp == 0 and units % depth == 0 and depth % 128 == 0
    fits = fits and first_out.shape[1] == 2 * units and n_dp > 2 and n_tensor > 2
    pick = gather_tokens_body if powers and few_tokens and fits else gather_weights_body
    return pick(first_out, second_out, grad_first, grad_second, w_up, *rest)


def solution(mesh):
    in_specs = (
        P(("groups", "tensor", "dp"), None),
        P(("groups", "tensor", "dp"), None),
        P(("groups", "tensor", "dp"), None),
        P(("groups", "tensor", "dp"), None),
        P("dp", "tensor"),
        P("tensor", "dp"),
        P(),
        P(),
    )
    out_specs = (
        P(("groups", "tensor", "dp"), None),
        P(("groups", "tensor", "dp"), None),
        P(("groups", "dp"), "tensor"),
        P(("groups", "tensor"), "dp"),
        P("groups", None),
    )
    return jax.shard_map(body, mesh=mesh, in_specs=in_specs, out_specs=out_specs, check_vma=False)
```

```python
import math

import jax
import jax.numpy as jnp
from jax import lax
from jax.experimental import pallas as pl
from jax.experimental.pallas import tpu as pltpu
from jax.sharding import PartitionSpec as P

epsilon = 1e-06
EXTRA = 16


def normalize(row_data, norm_gain, norm_bias):
    values = row_data.astype(jnp.float32)
    row_mean = jnp.mean(values, axis=-1, keepdims=True)
    centred = values - row_mean
    inv_std = lax.rsqrt(jnp.mean(centred * centred, axis=-1, keepdims=True) + epsilon)
    standard = centred * inv_std
    normed = (standard * norm_gain + norm_bias).astype(jnp.bfloat16)
    return (standard, inv_std, normed)


def contract_tokens(left_rows, right_rows):
    return lax.dot_general(
        left_rows, right_rows, (((0,), (0,)), ((), ())), preferred_element_type=jnp.float32
    )


def contract_last(left_rows, right_rows):
    return lax.dot_general(
        left_rows, right_rows, (((1,), (1,)), ((), ())), preferred_element_type=jnp.float32
    )


def finish_rows(branch, grad_normed, second_out, grad_first, first_out, norm_gain, norm_bias):
    standard, inv_std, _ = normalize(first_out, norm_gain, norm_bias)
    second_in = (second_out.astype(jnp.float32) - branch).astype(jnp.bfloat16)
    grad_std = grad_normed * norm_gain
    grad_rows = inv_std * (
        grad_std
        - jnp.mean(grad_std, axis=-1, keepdims=True)
        - standard * jnp.mean(grad_std * standard, axis=-1, keepdims=True)
    )
    return second_in, grad_first.astype(jnp.float32) + grad_rows


def gather_weights_body(
    first_out, second_out, grad_first, grad_second, w_up, w_down, norm_gain, norm_bias
):
    own_rows = first_out.shape[0]
    up_full = lax.all_gather(w_up, "dp", axis=0, tiled=True)
    down_full = lax.all_gather(w_down, "dp", axis=1, tiled=True)
    first_all = lax.all_gather(first_out, "tensor", axis=0, tiled=True)
    grad_all = lax.all_gather(grad_second, "tensor", axis=0, tiled=True)
    standard_all, _, normed = normalize(first_all, norm_gain, norm_bias)
    offset = lax.axis_index("tensor") * own_rows
    standard = lax.dynamic_slice_in_dim(standard_all, offset, own_rows, 0)
    preact = jnp.dot(normed, up_full, preferred_element_type=jnp.float32)
    hidden = jax.nn.gelu(preact).astype(jnp.bfloat16)
    branch = lax.psum_scatter(
        jnp.dot(hidden, down_full, preferred_element_type=jnp.float32).astype(jnp.bfloat16),
        "tensor",
        scatter_dimension=0,
        tiled=True,
    ).astype(jnp.float32)
    tokens = own_rows * lax.axis_size("tensor") * lax.axis_size("dp")
    grad_scale = tokens ** (-0.5)
    grad_down_part = contract_tokens(hidden, grad_all)
    grad_down = (
        lax.psum_scatter(
            grad_down_part.astype(jnp.bfloat16), "dp", scatter_dimension=1, tiled=True
        ).astype(jnp.float32)
        * grad_scale
    )
    grad_hidden = contract_last(grad_all, down_full)
    grad_pre = jax.vjp(jax.nn.gelu, preact)[1](grad_hidden)[0].astype(jnp.bfloat16)
    grad_up_part = contract_tokens(normed, grad_pre)
    grad_up = (
        lax.psum_scatter(
            grad_up_part.astype(jnp.bfloat16), "dp", scatter_dimension=0, tiled=True
        ).astype(jnp.float32)
        * grad_scale
    )
    grad_normed = lax.psum_scatter(
        contract_last(grad_pre, up_full).astype(jnp.bfloat16),
        "tensor",
        scatter_dimension=0,
        tiled=True,
    ).astype(jnp.float32)
    second_in, grad_first_in = finish_rows(
        branch, grad_normed, second_out, grad_first, first_out, norm_gain, norm_bias
    )
    local_stats = jnp.stack([jnp.sum(grad_normed * standard, axis=0), jnp.sum(grad_normed, axis=0)])
    grad_norm = lax.psum(local_stats, ("tensor", "dp")) * grad_scale
    return (second_in, grad_first_in, grad_up, grad_down, grad_norm)


def swap(values, axis, mask, scope):
    with jax.named_scope(scope):
        return lax.ppermute(values, axis, [(i, i ^ mask) for i in range(lax.axis_size(axis))])


def bits_of(size):
    return [1 << b for b in reversed(range(size.bit_length() - 1))]


def pack(first_out, grad_second, w_up, w_down, mates):
    n_dp, (own_rows, width) = lax.axis_size("dp"), first_out.shape
    depth, units = w_up.shape[0], w_up.shape[1] // n_dp
    strips, rows = units // depth, depth // mates

    def kernel(first_ref, grad_ref, up_ref, down_ref, own, *sends):
        place, mate = lax.axis_index("dp"), lax.rem(lax.axis_index("groups"), mates)
        for ref in [own] + [sends[bit - 1] for bit in bits_of(n_dp)]:
            ref[:own_rows, :] = first_ref[...]
            ref[own_rows : 2 * own_rows, :] = grad_ref[...]
        for k in range(1, n_dp):
            first = pl.multiple_of((place ^ k) * units, units)
            send, skip = sends[k - 1], 0 if k & (k - 1) else 2 * own_rows
            span = slice(skip, skip + rows)
            send[span, :units] = up_ref[pl.ds(pl.multiple_of(mate * rows, rows), rows), pl.ds(first, units)]
            for c in range(strips):
                row = pl.multiple_of(first + mate * (units // mates) + c * rows, rows)
                send[span, units + c * depth : units + (c + 1) * depth] = down_ref[pl.ds(row, rows), :]

    return pl.pallas_call(
        kernel,
        out_shape=[jax.ShapeDtypeStruct((2 * own_rows, width), w_up.dtype)]
        + [
            jax.ShapeDtypeStruct((rows + (0 if k & (k - 1) else 2 * own_rows), width), w_up.dtype)
            for k in range(1, n_dp)
        ],
        in_specs=[pl.BlockSpec(memory_space=pltpu.VMEM)] * 4,
        out_specs=[pl.BlockSpec(memory_space=pltpu.VMEM)] * n_dp,
        cost_estimate=pl.CostEstimate(flops=0, bytes_accessed=8 * w_up.size, transcendentals=0),
        name="pack",
    )(first_out, grad_second, w_up, w_down)


def core(chunks, w_up, w_down, got, mates, gain, bias):
    n_chunks, n, n_dp = len(chunks), len(chunks[0]), lax.axis_size("dp")
    (piece_rows, width), units = chunks[0][0].shape, w_up.shape[1] // n_dp
    piece_rows //= 2
    depth = width // n_dp
    strips, pair = units // depth, 2 * piece_rows
    slope = (2.0 / math.pi) ** 0.5
    dtype = w_up.dtype
    pieces_of_weights = [piece for k in range(1, n_dp) for piece in got[k]]
    n_got = len(pieces_of_weights)

    def kernel(*refs):
        toks, refs = refs[: n_chunks * n], refs[n_chunks * n :]
        (own_up, own_down), weights, (gain_ref, bias_ref), refs = (
            refs[:2],
            list(refs[2 : 2 + n_got]),
            refs[2 + n_got : 4 + n_got],
            refs[4 + n_got :],
        )
        outs, blocks, stat_ref = refs[: 2 * n_chunks], refs[2 * n_chunks : 2 * n_chunks + n_dp], refs[2 * n_chunks + n_dp]
        scratch = refs[2 * n_chunks + n_dp + 1 :]
        tok, norm, hid, pre, part, block, up_ref, down_ref, total, in_sem, w_sem, out_sem, b_sem = scratch
        place, mate = lax.axis_index("dp"), lax.rem(lax.axis_index("groups"), mates)
        reads, loads, writes = [], [], []

        def load(src, dst):
            loads.append(pltpu.make_async_copy(src, dst, w_sem.at[len(loads)]))
            loads[-1].start()

        for i, ref in enumerate(toks):
            reads.append(pltpu.make_async_copy(ref, tok.at[i], in_sem.at[i]))
            if i < n:
                reads[-1].start()
        mine = pl.ds(pl.multiple_of(place * units, units), units)
        rows = pl.ds(pl.multiple_of(place * depth, depth), depth)
        load(own_up.at[:, mine], up_ref.at[rows, :])
        load(own_down.at[mine, :], down_ref.at[:, rows])
        for k in range(1, n_dp):
            first = pl.multiple_of((place ^ k) * depth, depth)
            many = len(got[k])
            rows = depth // many
            for j in range(many):
                piece = weights.pop(0)
                which = mate ^ j if many > 1 else 0
                row = pl.multiple_of(first + which * rows, rows)
                load(piece.at[:, pl.ds(0, units)], up_ref.at[pl.ds(row, rows), :])
                for c in range(strips):
                    row = pl.multiple_of(which * (units // many) + c * rows, rows)
                    load(
                        piece.at[:, pl.ds(units + c * depth, depth)],
                        down_ref.at[pl.ds(row, rows), pl.ds(first, depth)],
                    )
        for one in reads[n:]:
            one.start()
        total[...] = jnp.zeros_like(total)
        for i in range(n_chunks):
            for one in reads[i * n : (i + 1) * n] + (loads if i == 0 else []):
                one.wait()

            @pl.loop(0, n // 2)
            def _(t):
                at = i * n + 2 * t
                span = pl.ds(pl.multiple_of(at * piece_rows, pair), pair)
                values = tok[pl.ds(at, 2), :piece_rows].reshape(pair, width).astype(jnp.float32)
                centred = values - jnp.mean(values, axis=-1, keepdims=True)
                inv_std = lax.rsqrt(jnp.mean(centred * centred, axis=-1, keepdims=True) + epsilon)
                standard = centred * inv_std
                normed = (standard * gain_ref[...] + bias_ref[...]).astype(dtype)
                norm[span, :] = normed
                x = jnp.dot(normed, up_ref[...], preferred_element_type=jnp.float32)
                gate = jnp.tanh(slope * (x + 0.044715 * (x * x * x)))
                half = 0.5 + 0.5 * gate
                hidden = (x * half).astype(dtype)
                hid[span, :] = hidden
                rise = half + (0.5 * slope) * x * (1.0 - gate * gate) * (1.0 + (3 * 0.044715) * (x * x))
                grads = tok[pl.ds(at, 2), piece_rows:].reshape(pair, width)
                grad_pre = (contract_last(grads, down_ref[...]) * rise).astype(dtype)
                pre[span, :] = grad_pre
                branch = jnp.dot(hidden, down_ref[...], preferred_element_type=jnp.float32)
                grad_normed = contract_last(grad_pre, up_ref[...])
                total[0:1, :] += jnp.sum(grad_normed * standard, axis=0, keepdims=True)
                total[1:2, :] += jnp.sum(grad_normed, axis=0, keepdims=True)
                row = pl.multiple_of(t * pair, pair)
                for odd in range(2):
                    own = slice(odd * piece_rows, (odd + 1) * piece_rows)
                    part[2 * i + odd, pl.ds(row, piece_rows), :] = branch[own].astype(dtype)
                    part[2 * i + odd, pl.ds(row + piece_rows, piece_rows), :] = grad_normed[own].astype(dtype)

            for odd in (1, 0):
                at = 2 * i + odd
                out = outs[at].at[pl.ds(0, half[0]), :]
                writes.append(pltpu.make_async_copy(part.at[at], out, out_sem.at[at]))
                writes[-1].start()
        stat_ref[...] = jnp.zeros_like(stat_ref)
        stat_ref[0:2, :] = total[0:2, :].astype(dtype)
        stat_ref[2:4, :] = (total[0:2, :] - stat_ref[0:2, :].astype(jnp.float32)).astype(dtype)
        tail = outs[1].at[pl.ds(half[0], EXTRA), :]
        writes.append(pltpu.make_async_copy(stat_ref, tail, out_sem.at[2 * n_chunks]))
        writes[-1].start()
        top = bits_of(n_dp)[0]
        for k in sorted(range(n_dp), key=lambda k: (k < top, k)):
            columns = pl.ds(pl.multiple_of((place ^ k) * depth, depth), depth)
            block[k, :depth, :] = contract_tokens(norm[:, columns], pre[...]).astype(dtype)
            grads = tok[:, piece_rows:, columns].reshape(n_chunks * n * piece_rows, depth)
            down_block = contract_tokens(hid[...], grads).astype(dtype)
            for c in range(strips):
                block[k, depth:, c * depth : (c + 1) * depth] = down_block[c * depth : (c + 1) * depth]
            writes.append(pltpu.make_async_copy(block.at[k], blocks[k], b_sem.at[k]))
            writes[-1].start()
        for one in writes:
            one.wait()

    rows = n_chunks * n * piece_rows
    half = (n // 2 * pair, width)
    far = pl.BlockSpec(memory_space=pl.ANY)
    near = pl.BlockSpec(memory_space=pltpu.VMEM)
    out = pl.pallas_call(
        kernel,
        out_shape=[
            jax.ShapeDtypeStruct((half[0] + (EXTRA if at == 1 else 0), width), dtype) for at in range(2 * n_chunks)
        ]
        + [jax.ShapeDtypeStruct((2 * depth, units), dtype)] * n_dp
        + [jax.ShapeDtypeStruct((EXTRA, width), dtype)],
        in_specs=[far] * (n_chunks * n + 2 + n_got) + [near] * 2,
        out_specs=[far] * (2 * n_chunks + n_dp) + [near],
        scratch_shapes=[
            pltpu.VMEM((n_chunks * n, pair, width), dtype),
            pltpu.VMEM((rows, width), dtype),
            pltpu.VMEM((rows, units), dtype),
            pltpu.VMEM((rows, units), dtype),
            pltpu.VMEM((2 * n_chunks, *half), dtype),
            pltpu.VMEM((n_dp, 2 * depth, units), dtype),
            pltpu.VMEM((width, units), dtype),
            pltpu.VMEM((units, width), dtype),
            pltpu.VMEM((EXTRA, width), jnp.float32),
            pltpu.SemaphoreType.DMA((n_chunks * n,)),
            pltpu.SemaphoreType.DMA((2 + n_got * (1 + strips),)),
            pltpu.SemaphoreType.DMA((2 * n_chunks + 1,)),
            pltpu.SemaphoreType.DMA((n_dp,)),
        ],
        compiler_params=pltpu.CompilerParams(vmem_limit_bytes=56 * 1024 * 1024),
        cost_estimate=pl.CostEstimate(
            flops=10 * rows * width * units,
            bytes_accessed=8 * rows * width + 8 * width * units,
            transcendentals=rows * units,
        ),
        name="core",
    )(
        *[piece for chunk in chunks for piece in chunk],
        w_up,
        w_down,
        *pieces_of_weights,
        gain.reshape(1, width),
        bias.reshape(1, width),
    )
    halves = [out[2 * i : 2 * i + 2] for i in range(n_chunks)]
    return halves, list(out[2 * n_chunks : -1]), out[-1]


def finish(blocks, terms, stats, first_out, second_out, grad_first, gain, bias, w_shapes, scale):
    (rows, width), n_dp = first_out.shape, len(blocks)
    depth, units = w_shapes[0][0], w_shapes[0][1] // n_dp
    strips, n_terms = units // depth, len(terms)

    def kernel(*refs):
        parts, adds, (stat_ref, first_ref, second_ref, grad_ref, gain_ref, bias_ref), outs = (
            refs[:n_dp],
            refs[n_dp : n_dp + n_terms],
            refs[n_dp + n_terms : n_dp + n_terms + 6],
            refs[n_dp + n_terms + 6 :],
        )
        second_in, grad_in, up_out, down_out, norm_out = outs
        place = lax.axis_index("dp")
        for k in range(n_dp):
            first = pl.multiple_of((place ^ k) * units, units)
            up_out[:, pl.ds(first, units)] = parts[k][:depth, :].astype(jnp.float32) * scale
            for c in range(strips):
                block = parts[k][depth : 2 * depth, c * depth : (c + 1) * depth]
                row = pl.multiple_of(first + c * depth, depth)
                down_out[pl.ds(row, depth), :] = block.astype(jnp.float32) * scale
        total = sum(ref[: 2 * rows, :].astype(jnp.float32) for ref in adds)
        second_in[...] = (second_ref[...].astype(jnp.float32) - total[:rows]).astype(second_in.dtype)
        values = first_ref[...].astype(jnp.float32)
        centred = values - jnp.mean(values, axis=-1, keepdims=True)
        inv_std = lax.rsqrt(jnp.mean(centred * centred, axis=-1, keepdims=True) + epsilon)
        standard = centred * inv_std
        grad_std = total[rows:] * gain_ref[...]
        grad_rows = inv_std * (
            grad_std
            - jnp.mean(grad_std, axis=-1, keepdims=True)
            - standard * jnp.mean(grad_std * standard, axis=-1, keepdims=True)
        )
        grad_in[...] = grad_ref[...].astype(jnp.float32) + grad_rows
        one, two = stat_ref[...].astype(jnp.float32), adds[-1][2 * rows :, :].astype(jnp.float32)
        norm_out[...] = ((one[0:2] + one[2:4]) + (two[0:2] + two[2:4])) * scale

    def whole(x):
        return pl.BlockSpec(x.shape, lambda i: (0, 0))

    arrays = [*blocks, *terms, stats, first_out, second_out, grad_first, gain.reshape(1, width), bias.reshape(1, width)]
    in_specs = [whole(x) for x in arrays]
    for i in range(n_terms - 1):
        in_specs[n_dp + i] = pl.BlockSpec((2 * rows, width), lambda i: (0, 0))
    out_shape = [
        jax.ShapeDtypeStruct((rows, width), second_out.dtype),
        jax.ShapeDtypeStruct((rows, width), jnp.float32),
        jax.ShapeDtypeStruct(w_shapes[0], jnp.float32),
        jax.ShapeDtypeStruct(w_shapes[1], jnp.float32),
        jax.ShapeDtypeStruct((2, width), jnp.float32),
    ]
    return pl.pallas_call(
        kernel,
        out_shape=out_shape,
        grid=(1,),
        in_specs=in_specs,
        out_specs=[whole(x) for x in out_shape],
        compiler_params=pltpu.CompilerParams(vmem_limit_bytes=48 * 1024 * 1024),
        cost_estimate=pl.CostEstimate(
            flops=0, bytes_accessed=12 * w_shapes[0][0] * w_shapes[0][1], transcendentals=0
        ),
        name="finish",
    )(*arrays)


def join(rows, terms, stats=()):
    width = terms[0][0].shape[1]
    arrays = [*terms, *stats]
    n_terms = len(terms)

    def kernel(*refs):
        out = refs[len(arrays)]
        total = sum(ref[...].astype(jnp.float32) for ref in refs[:n_terms])
        out[:rows, :] = total.astype(out.dtype)
        if stats:
            one, two = (ref[...].astype(jnp.float32) for ref in refs[n_terms : n_terms + 2])
            both = (one[0:2] + one[2:4]) + (two[0:2] + two[2:4])
            tail = refs[-1]
            tail[...] = jnp.zeros_like(tail)
            tail[0:2, :] = both.astype(tail.dtype)
            tail[2:4, :] = (both - tail[0:2, :].astype(jnp.float32)).astype(tail.dtype)
            out[rows:, :] = tail[...]

    def spec(height, place):
        return pl.BlockSpec((height, width), lambda i: (place, 0))

    out_shape = [jax.ShapeDtypeStruct((rows + (EXTRA if stats else 0), width), jnp.bfloat16)]
    out_specs = [spec(out_shape[0].shape[0], 0)]
    if stats:
        out_shape.append(jax.ShapeDtypeStruct((EXTRA, width), jnp.bfloat16))
        out_specs.append(spec(EXTRA, 0))
    out = pl.pallas_call(
        kernel,
        out_shape=out_shape,
        grid=(1,),
        in_specs=[spec(rows, place) for _, place in terms] + [spec(EXTRA, place) for _, place in stats],
        out_specs=out_specs,
        cost_estimate=pl.CostEstimate(
            flops=0, bytes_accessed=2 * (len(terms) + 1) * rows * width, transcendentals=0
        ),
        name="join",
    )(*(x for x, _ in arrays))
    return out if stats else out[0]


def after(values, *others):
    return lax.optimization_barrier((values, *others))[0]


def gather_tokens_body(
    first_out, second_out, grad_first, grad_second, w_up, w_down, norm_gain, norm_bias
):
    n_dp, n_tensor, n_groups = (lax.axis_size(axis) for axis in ("dp", "tensor", "groups"))
    own_rows, depth = first_out.shape[0], w_up.shape[0]
    units = w_up.shape[1] // n_dp
    mates = 2 if n_groups % 2 == 0 else 1
    place = lax.axis_index("dp")
    top = bits_of(n_dp)[0]

    high, others = bits_of(n_tensor)[0], bits_of(n_tensor)[1:]
    own, *sends = pack(first_out, grad_second, w_up, w_down, mates)
    tokens, chunks, got, crossed = {0: own}, {}, {}, {}

    def tokens_dp(k, *first):
        tokens[k] = swap(after(tokens[k & (k - 1)], *first), "dp", k & -k, f"tokens_{k}")

    def tokens_tensor(k, *first):
        start = after(tokens[k], *first)
        chunks[k] = {0: tokens[k], high: swap(start, "tensor", high, f"tokens_{k}_{high}")}

    def tokens_rest(k, *first):
        for bit in others:
            for j in list(chunks[k]):
                piece = after(chunks[k][j], *first)
                chunks[k][j | bit] = swap(piece, "tensor", bit, f"tokens_{k}_{j | bit}")

    def weights_groups(k, *first):
        if mates == 2:
            crossed[k] = swap(after(got[k], *first), "groups", 1, f"weights_{k}")

    tokens_tensor(0)
    tokens_rest(0)
    for bit in reversed(bits_of(n_dp)):
        both = swap(sends[bit - 1], "dp", bit, f"tokens_weights_{bit}")
        tokens[bit], got[bit] = both[: 2 * own_rows], both[2 * own_rows :]
    tokens_tensor(1, tokens[1], chunks[0][high])
    stage = [*tokens.values(), *got.values(), *chunks[0].values()]
    for bit in reversed(bits_of(n_dp)):
        weights_groups(bit, *stage)
    for k in range(2, n_dp):
        if k & (k - 1):
            tokens_dp(k, *stage)
            got[k] = swap(after(sends[k - 1], *stage, chunks[1][high]), "dp", k, f"weights_{k}")
            stage = [tokens[k], got[k], *crossed.values()]
        tokens_rest(k - 1)
        tokens_tensor(k, *stage, *(chunks[k - 2].values() if k > top else ()), chunks[k - 1][high])
        if k & (k - 1):
            weights_groups(k)
    tokens_rest(n_dp - 1, *crossed.values())
    got = {k: [got[k]] + ([crossed[k]] if k in crossed else []) for k in got}

    order = sorted(chunks, reverse=True)
    halves, blocks, stats = core(
        [[chunks[k][j] for j in range(n_tensor)] for k in order], w_up, w_down, got, mates, norm_gain, norm_bias
    )
    blocks = dict(enumerate(blocks))
    blocks[top] = swap(blocks[top], "dp", top, f"grads_{top}")

    for k in range(top + 1, n_dp):
        blocks[k] = swap(blocks[k], "dp", k, f"grads_{k}")

    sums, behind, span, waiting = {}, (), 2 * own_rows, None
    for k, (even, odd) in zip(order, halves, strict=True):
        came = swap(odd, "tensor", 1, f"sums_{k}_1")
        if k == order[0]:
            waiting = (came, even.shape[0] // EXTRA)
        parts = {2 * j: [(x, j) for x in (even, came)] for j in range(n_tensor // 2)}
        for bit in reversed(bits_of(n_tensor)[:-1]):
            for j in [j for j in parts if j & bit]:
                if k == order[0] and j == bit:
                    send, stats = join(span, parts.pop(j), [(stats, 0), waiting])
                else:
                    send = join(span, parts.pop(j))
                if k < 2:
                    behind += (blocks[n_dp - 1 if k == 0 else top],)
                came = swap(after(send, *behind), "tensor", bit, f"sums_{k}_{j}")
                if k == order[0] and j == bit:
                    waiting = (came, span // EXTRA)
                parts[j ^ bit].append((came, 0))
                behind = (came,)
        sums[k] = parts[0]
    came = {}
    for bit in bits_of(n_dp)[::-1]:
        for k in [k for k in order if k & bit and k in sums and k != bit]:
            if k == (n_dp - 1) & -bit:
                send, stats = join(span, sums.pop(k), [(stats, 0), waiting])
            else:
                send = join(span, sums.pop(k))
            came[k] = swap(send, "dp", bit, f"sums_{k}")
            if k == (n_dp - 1) & -bit:
                waiting = (came[k], span // EXTRA)
            sums[k ^ bit].append((came[k], 0))
    last, stats = join(span, sums[top], [(stats, 0), waiting])
    came[top] = swap(last, "dp", top, f"sums_{top}")
    for bit in bits_of(n_dp)[:0:-1]:
        came[bit] = swap(after(join(span, sums[bit]), last), "dp", bit, f"sums_{bit}")
    for k in range(1, top):
        blocks[k] = swap(after(blocks[k], last), "dp", k, f"grads_{k}")

    scale = (own_rows * n_tensor * n_dp) ** (-0.5)
    terms = [*(x for x, _ in sums[0]), *(came[bit] for bit in bits_of(n_dp)[::-1])]
    return tuple(
        finish(
            [blocks[k] for k in range(n_dp)],
            terms,
            stats,
            first_out,
            second_out,
            grad_first,
            norm_gain,
            norm_bias,
            (w_up.shape, w_down.shape),
            scale,
        )
    )


def body(first_out, second_out, grad_first, grad_second, w_up, *rest):
    n_dp, n_tensor = lax.axis_size("dp"), lax.axis_size("tensor")
    powers = all(size > 1 and size & (size - 1) == 0 for size in (n_dp, n_tensor))
    few_tokens = first_out.shape[0] * n_tensor < w_up.shape[1]
    units, depth = w_up.shape[1] // n_dp, w_up.shape[0]
    fits = w_up.shape[1] % n_dp == 0 and units % depth == 0 and depth % 128 == 0
    fits = fits and first_out.shape[1] == 2 * units and n_dp > 2 and n_tensor > 2
    pick = gather_tokens_body if powers and few_tokens and fits else gather_weights_body
    return pick(first_out, second_out, grad_first, grad_second, w_up, *rest)


def solution(mesh):
    in_specs = (
        P(("groups", "tensor", "dp"), None),
        P(("groups", "tensor", "dp"), None),
        P(("groups", "tensor", "dp"), None),
        P(("groups", "tensor", "dp"), None),
        P("dp", "tensor"),
        P("tensor", "dp"),
        P(),
        P(),
    )
    out_specs = (
        P(("groups", "tensor", "dp"), None),
        P(("groups", "tensor", "dp"), None),
        P(("groups", "dp"), "tensor"),
        P(("groups", "tensor"), "dp"),
        P("groups", None),
    )
    return jax.shard_map(body, mesh=mesh, in_specs=in_specs, out_specs=out_specs, check_vma=False)
```

```python
import math

import jax
import jax.numpy as jnp
from jax import lax
from jax.experimental import pallas as pl
from jax.experimental.pallas import tpu as pltpu
from jax.sharding import PartitionSpec as P

epsilon = 1e-06
EXTRA = 16


def normalize(row_data, norm_gain, norm_bias):
    values = row_data.astype(jnp.float32)
    row_mean = jnp.mean(values, axis=-1, keepdims=True)
    centred = values - row_mean
    inv_std = lax.rsqrt(jnp.mean(centred * centred, axis=-1, keepdims=True) + epsilon)
    standard = centred * inv_std
    normed = (standard * norm_gain + norm_bias).astype(jnp.bfloat16)
    return (standard, inv_std, normed)


def contract_tokens(left_rows, right_rows):
    return lax.dot_general(
        left_rows, right_rows, (((0,), (0,)), ((), ())), preferred_element_type=jnp.float32
    )


def contract_last(left_rows, right_rows):
    return lax.dot_general(
        left_rows, right_rows, (((1,), (1,)), ((), ())), preferred_element_type=jnp.float32
    )


def finish_rows(branch, grad_normed, second_out, grad_first, first_out, norm_gain, norm_bias):
    standard, inv_std, _ = normalize(first_out, norm_gain, norm_bias)
    second_in = (second_out.astype(jnp.float32) - branch).astype(jnp.bfloat16)
    grad_std = grad_normed * norm_gain
    grad_rows = inv_std * (
        grad_std
        - jnp.mean(grad_std, axis=-1, keepdims=True)
        - standard * jnp.mean(grad_std * standard, axis=-1, keepdims=True)
    )
    return second_in, grad_first.astype(jnp.float32) + grad_rows


def gather_weights_body(
    first_out, second_out, grad_first, grad_second, w_up, w_down, norm_gain, norm_bias
):
    own_rows = first_out.shape[0]
    up_full = lax.all_gather(w_up, "dp", axis=0, tiled=True)
    down_full = lax.all_gather(w_down, "dp", axis=1, tiled=True)
    first_all = lax.all_gather(first_out, "tensor", axis=0, tiled=True)
    grad_all = lax.all_gather(grad_second, "tensor", axis=0, tiled=True)
    standard_all, _, normed = normalize(first_all, norm_gain, norm_bias)
    offset = lax.axis_index("tensor") * own_rows
    standard = lax.dynamic_slice_in_dim(standard_all, offset, own_rows, 0)
    preact = jnp.dot(normed, up_full, preferred_element_type=jnp.float32)
    hidden = jax.nn.gelu(preact).astype(jnp.bfloat16)
    branch = lax.psum_scatter(
        jnp.dot(hidden, down_full, preferred_element_type=jnp.float32).astype(jnp.bfloat16),
        "tensor",
        scatter_dimension=0,
        tiled=True,
    ).astype(jnp.float32)
    tokens = own_rows * lax.axis_size("tensor") * lax.axis_size("dp")
    grad_scale = tokens ** (-0.5)
    grad_down_part = contract_tokens(hidden, grad_all)
    grad_down = (
        lax.psum_scatter(
            grad_down_part.astype(jnp.bfloat16), "dp", scatter_dimension=1, tiled=True
        ).astype(jnp.float32)
        * grad_scale
    )
    grad_hidden = contract_last(grad_all, down_full)
    grad_pre = jax.vjp(jax.nn.gelu, preact)[1](grad_hidden)[0].astype(jnp.bfloat16)
    grad_up_part = contract_tokens(normed, grad_pre)
    grad_up = (
        lax.psum_scatter(
            grad_up_part.astype(jnp.bfloat16), "dp", scatter_dimension=0, tiled=True
        ).astype(jnp.float32)
        * grad_scale
    )
    grad_normed = lax.psum_scatter(
        contract_last(grad_pre, up_full).astype(jnp.bfloat16),
        "tensor",
        scatter_dimension=0,
        tiled=True,
    ).astype(jnp.float32)
    second_in, grad_first_in = finish_rows(
        branch, grad_normed, second_out, grad_first, first_out, norm_gain, norm_bias
    )
    local_stats = jnp.stack([jnp.sum(grad_normed * standard, axis=0), jnp.sum(grad_normed, axis=0)])
    grad_norm = lax.psum(local_stats, ("tensor", "dp")) * grad_scale
    return (second_in, grad_first_in, grad_up, grad_down, grad_norm)


def swap(values, axis, mask, scope):
    with jax.named_scope(scope):
        return lax.ppermute(values, axis, [(i, i ^ mask) for i in range(lax.axis_size(axis))])


def bits_of(size):
    return [1 << b for b in reversed(range(size.bit_length() - 1))]


def pack(first_out, grad_second, w_up, w_down, mates):
    n_dp, (own_rows, width) = lax.axis_size("dp"), first_out.shape
    depth, units = w_up.shape[0], w_up.shape[1] // n_dp
    strips, rows = units // depth, depth // mates

    def kernel(first_ref, grad_ref, up_ref, down_ref, own, *sends):
        place, mate = lax.axis_index("dp"), lax.rem(lax.axis_index("groups"), mates)
        own[:own_rows, :] = first_ref[...]
        own[own_rows:, :] = grad_ref[...]
        for k in range(1, n_dp):
            first = pl.multiple_of((place ^ k) * units, units)
            send = sends[k - 1]
            send[:, :units] = up_ref[pl.ds(pl.multiple_of(mate * rows, rows), rows), pl.ds(first, units)]
            for c in range(strips):
                row = pl.multiple_of(first + mate * (units // mates) + c * rows, rows)
                send[:, units + c * depth : units + (c + 1) * depth] = down_ref[pl.ds(row, rows), :]

    return pl.pallas_call(
        kernel,
        out_shape=[jax.ShapeDtypeStruct((2 * own_rows, width), w_up.dtype)]
        + [jax.ShapeDtypeStruct((rows, width), w_up.dtype)] * (n_dp - 1),
        in_specs=[pl.BlockSpec(memory_space=pltpu.VMEM)] * 4,
        out_specs=[pl.BlockSpec(memory_space=pltpu.VMEM)] * n_dp,
        cost_estimate=pl.CostEstimate(flops=0, bytes_accessed=8 * w_up.size, transcendentals=0),
        name="pack",
    )(first_out, grad_second, w_up, w_down)


def core(chunks, w_up, w_down, got, mates, gain, bias):
    n_chunks, n, n_dp = len(chunks), len(chunks[0]), lax.axis_size("dp")
    (piece_rows, width), units = chunks[0][0].shape, w_up.shape[1] // n_dp
    piece_rows //= 2
    depth = width // n_dp
    strips, pair = units // depth, 2 * piece_rows
    slope = (2.0 / math.pi) ** 0.5
    dtype = w_up.dtype
    pieces_of_weights = [piece for k in range(1, n_dp) for piece in got[k]]
    n_got = len(pieces_of_weights)

    def kernel(*refs):
        toks, refs = refs[: n_chunks * n], refs[n_chunks * n :]
        (own_up, own_down), weights, (gain_ref, bias_ref), refs = (
            refs[:2],
            list(refs[2 : 2 + n_got]),
            refs[2 + n_got : 4 + n_got],
            refs[4 + n_got :],
        )
        outs, blocks, stat_ref = refs[: 2 * n_chunks], refs[2 * n_chunks : 2 * n_chunks + n_dp], refs[2 * n_chunks + n_dp]
        scratch = refs[2 * n_chunks + n_dp + 1 :]
        tok, norm, hid, pre, part, block, up_ref, down_ref, total, in_sem, w_sem, out_sem, b_sem = scratch
        place, mate = lax.axis_index("dp"), lax.rem(lax.axis_index("groups"), mates)
        reads, loads, writes = [], [], []

        def load(src, dst):
            loads.append(pltpu.make_async_copy(src, dst, w_sem.at[len(loads)]))
            loads[-1].start()

        for i, ref in enumerate(toks):
            reads.append(pltpu.make_async_copy(ref, tok.at[i], in_sem.at[i]))
            if i < n:
                reads[-1].start()
        mine = pl.ds(pl.multiple_of(place * units, units), units)
        rows = pl.ds(pl.multiple_of(place * depth, depth), depth)
        load(own_up.at[:, mine], up_ref.at[rows, :])
        load(own_down.at[mine, :], down_ref.at[:, rows])
        for k in range(1, n_dp):
            first = pl.multiple_of((place ^ k) * depth, depth)
            many = len(got[k])
            rows = depth // many
            for j in range(many):
                piece = weights.pop(0)
                which = mate ^ j if many > 1 else 0
                row = pl.multiple_of(first + which * rows, rows)
                load(piece.at[:, pl.ds(0, units)], up_ref.at[pl.ds(row, rows), :])
                for c in range(strips):
                    row = pl.multiple_of(which * (units // many) + c * rows, rows)
                    load(
                        piece.at[:, pl.ds(units + c * depth, depth)],
                        down_ref.at[pl.ds(row, rows), pl.ds(first, depth)],
                    )
        for one in reads[n:]:
            one.start()
        total[...] = jnp.zeros_like(total)
        for i in range(n_chunks):
            for one in reads[i * n : (i + 1) * n] + (loads if i == 0 else []):
                one.wait()

            @pl.loop(0, n // 2)
            def _(t):
                at = i * n + 2 * t
                span = pl.ds(pl.multiple_of(at * piece_rows, pair), pair)
                values = tok[pl.ds(at, 2), :piece_rows].reshape(pair, width).astype(jnp.float32)
                centred = values - jnp.mean(values, axis=-1, keepdims=True)
                inv_std = lax.rsqrt(jnp.mean(centred * centred, axis=-1, keepdims=True) + epsilon)
                standard = centred * inv_std
                normed = (standard * gain_ref[...] + bias_ref[...]).astype(dtype)
                norm[span, :] = normed
                x = jnp.dot(normed, up_ref[...], preferred_element_type=jnp.float32)
                gate = jnp.tanh(slope * (x + 0.044715 * (x * x * x)))
                half = 0.5 + 0.5 * gate
                hidden = (x * half).astype(dtype)
                hid[span, :] = hidden
                rise = half + (0.5 * slope) * x * (1.0 - gate * gate) * (1.0 + (3 * 0.044715) * (x * x))
                grads = tok[pl.ds(at, 2), piece_rows:].reshape(pair, width)
                grad_pre = (contract_last(grads, down_ref[...]) * rise).astype(dtype)
                pre[span, :] = grad_pre
                branch = jnp.dot(hidden, down_ref[...], preferred_element_type=jnp.float32)
                grad_normed = contract_last(grad_pre, up_ref[...])
                total[0:1, :] += jnp.sum(grad_normed * standard, axis=0, keepdims=True)
                total[1:2, :] += jnp.sum(grad_normed, axis=0, keepdims=True)
                row = pl.multiple_of(t * pair, pair)
                for odd in range(2):
                    own = slice(odd * piece_rows, (odd + 1) * piece_rows)
                    part[2 * i + odd, pl.ds(row, piece_rows), :] = branch[own].astype(dtype)
                    part[2 * i + odd, pl.ds(row + piece_rows, piece_rows), :] = grad_normed[own].astype(dtype)

            for odd in (1, 0):
                at = 2 * i + odd
                out = outs[at].at[pl.ds(0, half[0]), :]
                writes.append(pltpu.make_async_copy(part.at[at], out, out_sem.at[at]))
                writes[-1].start()
        stat_ref[...] = jnp.zeros_like(stat_ref)
        stat_ref[0:2, :] = total[0:2, :].astype(dtype)
        stat_ref[2:4, :] = (total[0:2, :] - stat_ref[0:2, :].astype(jnp.float32)).astype(dtype)
        tail = outs[1].at[pl.ds(half[0], EXTRA), :]
        writes.append(pltpu.make_async_copy(stat_ref, tail, out_sem.at[2 * n_chunks]))
        writes[-1].start()
        top = bits_of(n_dp)[0]
        for k in sorted(range(n_dp), key=lambda k: (k < top, k)):
            columns = pl.ds(pl.multiple_of((place ^ k) * depth, depth), depth)
            block[k, :depth, :] = contract_tokens(norm[:, columns], pre[...]).astype(dtype)
            grads = tok[:, piece_rows:, columns].reshape(n_chunks * n * piece_rows, depth)
            down_block = contract_tokens(hid[...], grads).astype(dtype)
            for c in range(strips):
                block[k, depth:, c * depth : (c + 1) * depth] = down_block[c * depth : (c + 1) * depth]
            writes.append(pltpu.make_async_copy(block.at[k], blocks[k], b_sem.at[k]))
            writes[-1].start()
        for one in writes:
            one.wait()

    rows = n_chunks * n * piece_rows
    half = (n // 2 * pair, width)
    far = pl.BlockSpec(memory_space=pl.ANY)
    near = pl.BlockSpec(memory_space=pltpu.VMEM)
    out = pl.pallas_call(
        kernel,
        out_shape=[
            jax.ShapeDtypeStruct((half[0] + (EXTRA if at == 1 else 0), width), dtype) for at in range(2 * n_chunks)
        ]
        + [jax.ShapeDtypeStruct((2 * depth, units), dtype)] * n_dp
        + [jax.ShapeDtypeStruct((EXTRA, width), dtype)],
        in_specs=[far] * (n_chunks * n + 2 + n_got) + [near] * 2,
        out_specs=[far] * (2 * n_chunks + n_dp) + [near],
        scratch_shapes=[
            pltpu.VMEM((n_chunks * n, pair, width), dtype),
            pltpu.VMEM((rows, width), dtype),
            pltpu.VMEM((rows, units), dtype),
            pltpu.VMEM((rows, units), dtype),
            pltpu.VMEM((2 * n_chunks, *half), dtype),
            pltpu.VMEM((n_dp, 2 * depth, units), dtype),
            pltpu.VMEM((width, units), dtype),
            pltpu.VMEM((units, width), dtype),
            pltpu.VMEM((EXTRA, width), jnp.float32),
            pltpu.SemaphoreType.DMA((n_chunks * n,)),
            pltpu.SemaphoreType.DMA((2 + n_got * (1 + strips),)),
            pltpu.SemaphoreType.DMA((2 * n_chunks + 1,)),
            pltpu.SemaphoreType.DMA((n_dp,)),
        ],
        compiler_params=pltpu.CompilerParams(vmem_limit_bytes=56 * 1024 * 1024),
        cost_estimate=pl.CostEstimate(
            flops=10 * rows * width * units,
            bytes_accessed=8 * rows * width + 8 * width * units,
            transcendentals=rows * units,
        ),
        name="core",
    )(
        *[piece for chunk in chunks for piece in chunk],
        w_up,
        w_down,
        *pieces_of_weights,
        gain.reshape(1, width),
        bias.reshape(1, width),
    )
    halves = [out[2 * i : 2 * i + 2] for i in range(n_chunks)]
    return halves, list(out[2 * n_chunks : -1]), out[-1]


def finish(blocks, terms, stats, first_out, second_out, grad_first, gain, bias, w_shapes, scale):
    (rows, width), n_dp = first_out.shape, len(blocks)
    depth, units = w_shapes[0][0], w_shapes[0][1] // n_dp
    strips, n_terms = units // depth, len(terms)

    def kernel(*refs):
        parts, adds, (stat_ref, first_ref, second_ref, grad_ref, gain_ref, bias_ref), outs = (
            refs[:n_dp],
            refs[n_dp : n_dp + n_terms],
            refs[n_dp + n_terms : n_dp + n_terms + 6],
            refs[n_dp + n_terms + 6 :],
        )
        second_in, grad_in, up_out, down_out, norm_out = outs
        place = lax.axis_index("dp")
        for k in range(n_dp):
            first = pl.multiple_of((place ^ k) * units, units)
            up_out[:, pl.ds(first, units)] = parts[k][:depth, :].astype(jnp.float32) * scale
            for c in range(strips):
                block = parts[k][depth : 2 * depth, c * depth : (c + 1) * depth]
                row = pl.multiple_of(first + c * depth, depth)
                down_out[pl.ds(row, depth), :] = block.astype(jnp.float32) * scale
        total = sum(ref[: 2 * rows, :].astype(jnp.float32) for ref in adds)
        second_in[...] = (second_ref[...].astype(jnp.float32) - total[:rows]).astype(second_in.dtype)
        values = first_ref[...].astype(jnp.float32)
        centred = values - jnp.mean(values, axis=-1, keepdims=True)
        inv_std = lax.rsqrt(jnp.mean(centred * centred, axis=-1, keepdims=True) + epsilon)
        standard = centred * inv_std
        grad_std = total[rows:] * gain_ref[...]
        grad_rows = inv_std * (
            grad_std
            - jnp.mean(grad_std, axis=-1, keepdims=True)
            - standard * jnp.mean(grad_std * standard, axis=-1, keepdims=True)
        )
        grad_in[...] = grad_ref[...].astype(jnp.float32) + grad_rows
        one, two = stat_ref[...].astype(jnp.float32), adds[-1][2 * rows :, :].astype(jnp.float32)
        norm_out[...] = ((one[0:2] + one[2:4]) + (two[0:2] + two[2:4])) * scale

    def whole(x):
        return pl.BlockSpec(x.shape, lambda i: (0, 0))

    arrays = [*blocks, *terms, stats, first_out, second_out, grad_first, gain.reshape(1, width), bias.reshape(1, width)]
    in_specs = [whole(x) for x in arrays]
    for i in range(n_terms - 1):
        in_specs[n_dp + i] = pl.BlockSpec((2 * rows, width), lambda i: (0, 0))
    out_shape = [
        jax.ShapeDtypeStruct((rows, width), second_out.dtype),
        jax.ShapeDtypeStruct((rows, width), jnp.float32),
        jax.ShapeDtypeStruct(w_shapes[0], jnp.float32),
        jax.ShapeDtypeStruct(w_shapes[1], jnp.float32),
        jax.ShapeDtypeStruct((2, width), jnp.float32),
    ]
    return pl.pallas_call(
        kernel,
        out_shape=out_shape,
        grid=(1,),
        in_specs=in_specs,
        out_specs=[whole(x) for x in out_shape],
        compiler_params=pltpu.CompilerParams(vmem_limit_bytes=48 * 1024 * 1024),
        cost_estimate=pl.CostEstimate(
            flops=0, bytes_accessed=12 * w_shapes[0][0] * w_shapes[0][1], transcendentals=0
        ),
        name="finish",
    )(*arrays)


def join(rows, terms, stats=()):
    width = terms[0][0].shape[1]
    arrays = [*terms, *stats]
    n_terms = len(terms)

    def kernel(*refs):
        out = refs[len(arrays)]
        total = sum(ref[...].astype(jnp.float32) for ref in refs[:n_terms])
        out[:rows, :] = total.astype(out.dtype)
        if stats:
            one, two = (ref[...].astype(jnp.float32) for ref in refs[n_terms : n_terms + 2])
            both = (one[0:2] + one[2:4]) + (two[0:2] + two[2:4])
            tail = refs[-1]
            tail[...] = jnp.zeros_like(tail)
            tail[0:2, :] = both.astype(tail.dtype)
            tail[2:4, :] = (both - tail[0:2, :].astype(jnp.float32)).astype(tail.dtype)
            out[rows:, :] = tail[...]

    def spec(height, place):
        return pl.BlockSpec((height, width), lambda i: (place, 0))

    out_shape = [jax.ShapeDtypeStruct((rows + (EXTRA if stats else 0), width), jnp.bfloat16)]
    out_specs = [spec(out_shape[0].shape[0], 0)]
    if stats:
        out_shape.append(jax.ShapeDtypeStruct((EXTRA, width), jnp.bfloat16))
        out_specs.append(spec(EXTRA, 0))
    out = pl.pallas_call(
        kernel,
        out_shape=out_shape,
        grid=(1,),
        in_specs=[spec(rows, place) for _, place in terms] + [spec(EXTRA, place) for _, place in stats],
        out_specs=out_specs,
        cost_estimate=pl.CostEstimate(
            flops=0, bytes_accessed=2 * (len(terms) + 1) * rows * width, transcendentals=0
        ),
        name="join",
    )(*(x for x, _ in arrays))
    return out if stats else out[0]


def after(values, *others):
    return lax.optimization_barrier((values, *others))[0]


def gather_tokens_body(
    first_out, second_out, grad_first, grad_second, w_up, w_down, norm_gain, norm_bias
):
    n_dp, n_tensor, n_groups = (lax.axis_size(axis) for axis in ("dp", "tensor", "groups"))
    own_rows, depth = first_out.shape[0], w_up.shape[0]
    units = w_up.shape[1] // n_dp
    mates = 2 if n_groups % 2 == 0 else 1
    place = lax.axis_index("dp")
    top = bits_of(n_dp)[0]

    high, others = bits_of(n_tensor)[0], bits_of(n_tensor)[1:]
    own, *sends = pack(first_out, grad_second, w_up, w_down, mates)
    tokens, chunks, got, crossed = {0: own}, {}, {}, {}

    def tokens_dp(k, *first):
        tokens[k] = swap(after(tokens[k & (k - 1)], *first), "dp", k & -k, f"tokens_{k}")

    def tokens_tensor(k, *first):
        start = after(tokens[k], *first)
        chunks[k] = {0: tokens[k], high: swap(start, "tensor", high, f"tokens_{k}_{high}")}

    def tokens_rest(k, *first):
        for bit in others:
            for j in list(chunks[k]):
                piece = after(chunks[k][j], *first)
                chunks[k][j | bit] = swap(piece, "tensor", bit, f"tokens_{k}_{j | bit}")

    def weights_groups(k, *first):
        if mates == 2:
            crossed[k] = swap(after(got[k], *first), "groups", 1, f"weights_{k}")

    def weights_dp(k, *first):
        got[k] = swap(after(sends[k - 1], *first), "dp", k, f"weights_{k}")

    for bit in reversed(bits_of(n_dp)):
        tokens_dp(bit)
    tokens_tensor(0)
    tokens_rest(0)
    tokens_tensor(1, tokens[top], chunks[0][high])
    stage = [*tokens.values(), *chunks[0].values()]
    for k in range(2, n_dp):
        if k & (k - 1):
            tokens_dp(k, *stage)
        weights_dp(k, *stage, *([got[top]] if top in got else []))
    for k in range(2, n_dp):
        tokens_rest(k - 1)
        stage = [got[top]]
        if k & (k - 1):
            stage = [tokens[k], *got.values(), *chunks[k - 2].values()]
        tokens_tensor(k, *stage, chunks[k - 1][high])
    weights_dp(1, *stage)
    for k in [*range(2, n_dp), 1]:
        weights_groups(k)
    tokens_rest(n_dp - 1, *crossed.values())
    got = {k: [got[k]] + ([crossed[k]] if k in crossed else []) for k in got}

    order = sorted(chunks, reverse=True)
    halves, blocks, stats = core(
        [[chunks[k][j] for j in range(n_tensor)] for k in order], w_up, w_down, got, mates, norm_gain, norm_bias
    )
    blocks = dict(enumerate(blocks))
    blocks[top] = swap(blocks[top], "dp", top, f"grads_{top}")

    for k in range(1, top):
        blocks[k] = swap(blocks[k], "dp", k, f"grads_{k}")
    for k in range(top + 1, n_dp):
        blocks[k] = swap(after(blocks[k], *(blocks[j] for j in range(1, k))), "dp", k, f"grads_{k}")

    def add(terms):
        spans = (x[place * span : (place + 1) * span].astype(jnp.float32) for x, place in terms)
        return sum(spans).astype(jnp.bfloat16)

    sums, behind, span, waiting = {}, (), 2 * own_rows, None
    for k, (even, odd) in zip(order, halves, strict=True):
        came = swap(odd, "tensor", 1, f"sums_{k}_1")
        if k == order[0]:
            waiting = (came, even.shape[0] // EXTRA)
        parts = {2 * j: [(x, j) for x in (even, came)] for j in range(n_tensor // 2)}
        for bit in reversed(bits_of(n_tensor)[:-1]):
            for j in [j for j in parts if j & bit]:
                if k == order[0] and j == bit:
                    send, stats = join(span, parts.pop(j), [(stats, 0), waiting])
                else:
                    send = add(parts.pop(j))
                if k < 2:
                    behind += (blocks[n_dp - 1 if k == 0 else top],)
                came = swap(after(send, *behind), "tensor", bit, f"sums_{k}_{j}")
                if k == order[0] and j == bit:
                    waiting = (came, span // EXTRA)
                parts[j ^ bit].append((came, 0))
                behind = (came,)
        sums[k] = parts[0]
    came = {}
    for bit in bits_of(n_dp)[::-1]:
        for k in [k for k in order if k & bit and k in sums and k != bit]:
            if k == (n_dp - 1) & -bit:
                send, stats = join(span, sums.pop(k), [(stats, 0), waiting])
            else:
                send = add(sums.pop(k))
            came[k] = swap(send, "dp", bit, f"sums_{k}")
            if k == (n_dp - 1) & -bit:
                waiting = (came[k], span // EXTRA)
            sums[k ^ bit].append((came[k], 0))
    last, stats = join(span, sums[top], [(stats, 0), waiting])
    came[top] = swap(last, "dp", top, f"sums_{top}")
    for bit in bits_of(n_dp)[:0:-1]:
        came[bit] = swap(after(add(sums[bit]), last), "dp", bit, f"sums_{bit}")

    scale = (own_rows * n_tensor * n_dp) ** (-0.5)
    terms = [*(x for x, _ in sums[0]), *(came[bit] for bit in bits_of(n_dp)[::-1])]
    return tuple(
        finish(
            [blocks[k] for k in range(n_dp)],
            terms,
            stats,
            first_out,
            second_out,
            grad_first,
            norm_gain,
            norm_bias,
            (w_up.shape, w_down.shape),
            scale,
        )
    )


def body(first_out, second_out, grad_first, grad_second, w_up, *rest):
    n_dp, n_tensor = lax.axis_size("dp"), lax.axis_size("tensor")
    powers = all(size > 1 and size & (size - 1) == 0 for size in (n_dp, n_tensor))
    few_tokens = first_out.shape[0] * n_tensor < w_up.shape[1]
    units, depth = w_up.shape[1] // n_dp, w_up.shape[0]
    fits = w_up.shape[1] % n_dp == 0 and units % depth == 0 and depth % 128 == 0
    fits = fits and first_out.shape[1] == 2 * units and n_dp > 2 and n_tensor > 2
    pick = gather_tokens_body if powers and few_tokens and fits else gather_weights_body
    return pick(first_out, second_out, grad_first, grad_second, w_up, *rest)


def solution(mesh):
    in_specs = (
        P(("groups", "tensor", "dp"), None),
        P(("groups", "tensor", "dp"), None),
        P(("groups", "tensor", "dp"), None),
        P(("groups", "tensor", "dp"), None),
        P("dp", "tensor"),
        P("tensor", "dp"),
        P(),
        P(),
    )
    out_specs = (
        P(("groups", "tensor", "dp"), None),
        P(("groups", "tensor", "dp"), None),
        P(("groups", "dp"), "tensor"),
        P(("groups", "tensor"), "dp"),
        P("groups", None),
    )
    return jax.shard_map(body, mesh=mesh, in_specs=in_specs, out_specs=out_specs, check_vma=False)
```

```python
import math

import jax
import jax.numpy as jnp
from jax import lax
from jax.experimental import pallas as pl
from jax.experimental.pallas import tpu as pltpu
from jax.sharding import PartitionSpec as P

epsilon = 1e-06
EXTRA = 16


def normalize(row_data, norm_gain, norm_bias):
    values = row_data.astype(jnp.float32)
    row_mean = jnp.mean(values, axis=-1, keepdims=True)
    centred = values - row_mean
    inv_std = lax.rsqrt(jnp.mean(centred * centred, axis=-1, keepdims=True) + epsilon)
    standard = centred * inv_std
    normed = (standard * norm_gain + norm_bias).astype(jnp.bfloat16)
    return (standard, inv_std, normed)


def contract_tokens(left_rows, right_rows):
    return lax.dot_general(
        left_rows, right_rows, (((0,), (0,)), ((), ())), preferred_element_type=jnp.float32
    )


def contract_last(left_rows, right_rows):
    return lax.dot_general(
        left_rows, right_rows, (((1,), (1,)), ((), ())), preferred_element_type=jnp.float32
    )


def finish_rows(branch, grad_normed, second_out, grad_first, first_out, norm_gain, norm_bias):
    standard, inv_std, _ = normalize(first_out, norm_gain, norm_bias)
    second_in = (second_out.astype(jnp.float32) - branch).astype(jnp.bfloat16)
    grad_std = grad_normed * norm_gain
    grad_rows = inv_std * (
        grad_std
        - jnp.mean(grad_std, axis=-1, keepdims=True)
        - standard * jnp.mean(grad_std * standard, axis=-1, keepdims=True)
    )
    return second_in, grad_first.astype(jnp.float32) + grad_rows


def gather_weights_body(
    first_out, second_out, grad_first, grad_second, w_up, w_down, norm_gain, norm_bias
):
    own_rows = first_out.shape[0]
    up_full = lax.all_gather(w_up, "dp", axis=0, tiled=True)
    down_full = lax.all_gather(w_down, "dp", axis=1, tiled=True)
    first_all = lax.all_gather(first_out, "tensor", axis=0, tiled=True)
    grad_all = lax.all_gather(grad_second, "tensor", axis=0, tiled=True)
    standard_all, _, normed = normalize(first_all, norm_gain, norm_bias)
    offset = lax.axis_index("tensor") * own_rows
    standard = lax.dynamic_slice_in_dim(standard_all, offset, own_rows, 0)
    preact = jnp.dot(normed, up_full, preferred_element_type=jnp.float32)
    hidden = jax.nn.gelu(preact).astype(jnp.bfloat16)
    branch = lax.psum_scatter(
        jnp.dot(hidden, down_full, preferred_element_type=jnp.float32).astype(jnp.bfloat16),
        "tensor",
        scatter_dimension=0,
        tiled=True,
    ).astype(jnp.float32)
    tokens = own_rows * lax.axis_size("tensor") * lax.axis_size("dp")
    grad_scale = tokens ** (-0.5)
    grad_down_part = contract_tokens(hidden, grad_all)
    grad_down = (
        lax.psum_scatter(
            grad_down_part.astype(jnp.bfloat16), "dp", scatter_dimension=1, tiled=True
        ).astype(jnp.float32)
        * grad_scale
    )
    grad_hidden = contract_last(grad_all, down_full)
    grad_pre = jax.vjp(jax.nn.gelu, preact)[1](grad_hidden)[0].astype(jnp.bfloat16)
    grad_up_part = contract_tokens(normed, grad_pre)
    grad_up = (
        lax.psum_scatter(
            grad_up_part.astype(jnp.bfloat16), "dp", scatter_dimension=0, tiled=True
        ).astype(jnp.float32)
        * grad_scale
    )
    grad_normed = lax.psum_scatter(
        contract_last(grad_pre, up_full).astype(jnp.bfloat16),
        "tensor",
        scatter_dimension=0,
        tiled=True,
    ).astype(jnp.float32)
    second_in, grad_first_in = finish_rows(
        branch, grad_normed, second_out, grad_first, first_out, norm_gain, norm_bias
    )
    local_stats = jnp.stack([jnp.sum(grad_normed * standard, axis=0), jnp.sum(grad_normed, axis=0)])
    grad_norm = lax.psum(local_stats, ("tensor", "dp")) * grad_scale
    return (second_in, grad_first_in, grad_up, grad_down, grad_norm)


def swap(values, axis, mask, scope):
    with jax.named_scope(scope):
        return lax.ppermute(values, axis, [(i, i ^ mask) for i in range(lax.axis_size(axis))])


def bits_of(size):
    return [1 << b for b in reversed(range(size.bit_length() - 1))]


def pack(first_out, grad_second, w_up, w_down, mates):
    n_dp, (own_rows, width) = lax.axis_size("dp"), first_out.shape
    depth, units = w_up.shape[0], w_up.shape[1] // n_dp
    strips, rows = units // depth, depth // mates

    def kernel(first_ref, grad_ref, up_ref, down_ref, own, *sends):
        place, mate = lax.axis_index("dp"), lax.rem(lax.axis_index("groups"), mates)
        own[:own_rows, :] = first_ref[...]
        own[own_rows:, :] = grad_ref[...]
        for k in range(1, n_dp):
            first = pl.multiple_of((place ^ k) * units, units)
            send = sends[k - 1]
            send[:, :units] = up_ref[pl.ds(pl.multiple_of(mate * rows, rows), rows), pl.ds(first, units)]
            for c in range(strips):
                row = pl.multiple_of(first + mate * (units // mates) + c * rows, rows)
                send[:, units + c * depth : units + (c + 1) * depth] = down_ref[pl.ds(row, rows), :]

    return pl.pallas_call(
        kernel,
        out_shape=[jax.ShapeDtypeStruct((2 * own_rows, width), w_up.dtype)]
        + [jax.ShapeDtypeStruct((rows, width), w_up.dtype)] * (n_dp - 1),
        in_specs=[pl.BlockSpec(memory_space=pltpu.VMEM)] * 4,
        out_specs=[pl.BlockSpec(memory_space=pltpu.VMEM)] * n_dp,
        cost_estimate=pl.CostEstimate(flops=0, bytes_accessed=8 * w_up.size, transcendentals=0),
        name="pack",
    )(first_out, grad_second, w_up, w_down)


def core(chunks, w_up, w_down, got, mates, gain, bias):
    n_chunks, n, n_dp = len(chunks), len(chunks[0]), lax.axis_size("dp")
    (piece_rows, width), units = chunks[0][0].shape, w_up.shape[1] // n_dp
    piece_rows //= 2
    depth = width // n_dp
    strips, pair = units // depth, 2 * piece_rows
    slope = (2.0 / math.pi) ** 0.5
    dtype = w_up.dtype
    pieces_of_weights = [piece for k in range(1, n_dp) for piece in got[k]]
    n_got = len(pieces_of_weights)

    def kernel(*refs):
        toks, refs = refs[: n_chunks * n], refs[n_chunks * n :]
        (own_up, own_down), weights, (gain_ref, bias_ref), refs = (
            refs[:2],
            list(refs[2 : 2 + n_got]),
            refs[2 + n_got : 4 + n_got],
            refs[4 + n_got :],
        )
        outs, blocks, stat_ref = refs[: 2 * n_chunks], refs[2 * n_chunks : 2 * n_chunks + n_dp], refs[2 * n_chunks + n_dp]
        scratch = refs[2 * n_chunks + n_dp + 1 :]
        tok, norm, hid, pre, part, block, up_ref, down_ref, total, in_sem, w_sem, out_sem, b_sem = scratch
        place, mate = lax.axis_index("dp"), lax.rem(lax.axis_index("groups"), mates)
        reads, loads, writes = [], [], []

        def load(src, dst):
            loads.append(pltpu.make_async_copy(src, dst, w_sem.at[len(loads)]))
            loads[-1].start()

        for i, ref in enumerate(toks):
            reads.append(pltpu.make_async_copy(ref, tok.at[i], in_sem.at[i]))
            if i < n:
                reads[-1].start()
        mine = pl.ds(pl.multiple_of(place * units, units), units)
        rows = pl.ds(pl.multiple_of(place * depth, depth), depth)
        load(own_up.at[:, mine], up_ref.at[rows, :])
        load(own_down.at[mine, :], down_ref.at[:, rows])
        for k in range(1, n_dp):
            first = pl.multiple_of((place ^ k) * depth, depth)
            many = len(got[k])
            rows = depth // many
            for j in range(many):
                piece = weights.pop(0)
                which = mate ^ j if many > 1 else 0
                row = pl.multiple_of(first + which * rows, rows)
                load(piece.at[:, pl.ds(0, units)], up_ref.at[pl.ds(row, rows), :])
                for c in range(strips):
                    row = pl.multiple_of(which * (units // many) + c * rows, rows)
                    load(
                        piece.at[:, pl.ds(units + c * depth, depth)],
                        down_ref.at[pl.ds(row, rows), pl.ds(first, depth)],
                    )
        for one in reads[n:]:
            one.start()
        total[...] = jnp.zeros_like(total)
        for i in range(n_chunks):
            for one in reads[i * n : (i + 1) * n] + (loads if i == 0 else []):
                one.wait()

            @pl.loop(0, n // 2)
            def _(t):
                at = i * n + 2 * t
                span = pl.ds(pl.multiple_of(at * piece_rows, pair), pair)
                values = tok[pl.ds(at, 2), :piece_rows].reshape(pair, width).astype(jnp.float32)
                centred = values - jnp.mean(values, axis=-1, keepdims=True)
                inv_std = lax.rsqrt(jnp.mean(centred * centred, axis=-1, keepdims=True) + epsilon)
                standard = centred * inv_std
                normed = (standard * gain_ref[...] + bias_ref[...]).astype(dtype)
                norm[span, :] = normed
                x = jnp.dot(normed, up_ref[...], preferred_element_type=jnp.float32)
                gate = jnp.tanh(slope * (x + 0.044715 * (x * x * x)))
                half = 0.5 + 0.5 * gate
                hidden = (x * half).astype(dtype)
                hid[span, :] = hidden
                rise = half + (0.5 * slope) * x * (1.0 - gate * gate) * (1.0 + (3 * 0.044715) * (x * x))
                grads = tok[pl.ds(at, 2), piece_rows:].reshape(pair, width)
                grad_pre = (contract_last(grads, down_ref[...]) * rise).astype(dtype)
                pre[span, :] = grad_pre
                branch = jnp.dot(hidden, down_ref[...], preferred_element_type=jnp.float32)
                grad_normed = contract_last(grad_pre, up_ref[...])
                total[0:1, :] += jnp.sum(grad_normed * standard, axis=0, keepdims=True)
                total[1:2, :] += jnp.sum(grad_normed, axis=0, keepdims=True)
                row = pl.multiple_of(t * pair, pair)
                for odd in range(2):
                    own = slice(odd * piece_rows, (odd + 1) * piece_rows)
                    part[2 * i + odd, pl.ds(row, piece_rows), :] = branch[own].astype(dtype)
                    part[2 * i + odd, pl.ds(row + piece_rows, piece_rows), :] = grad_normed[own].astype(dtype)

            for odd in (1, 0):
                at = 2 * i + odd
                out = outs[at].at[pl.ds(0, half[0]), :]
                writes.append(pltpu.make_async_copy(part.at[at], out, out_sem.at[at]))
                writes[-1].start()
        stat_ref[...] = jnp.zeros_like(stat_ref)
        stat_ref[0:2, :] = total[0:2, :].astype(dtype)
        stat_ref[2:4, :] = (total[0:2, :] - stat_ref[0:2, :].astype(jnp.float32)).astype(dtype)
        tail = outs[1].at[pl.ds(half[0], EXTRA), :]
        writes.append(pltpu.make_async_copy(stat_ref, tail, out_sem.at[2 * n_chunks]))
        writes[-1].start()
        top = bits_of(n_dp)[0]
        for k in sorted(range(n_dp), key=lambda k: (k < top, k)):
            columns = pl.ds(pl.multiple_of((place ^ k) * depth, depth), depth)
            block[k, :depth, :] = contract_tokens(norm[:, columns], pre[...]).astype(dtype)
            grads = tok[:, piece_rows:, columns].reshape(n_chunks * n * piece_rows, depth)
            down_block = contract_tokens(hid[...], grads).astype(dtype)
            for c in range(strips):
                block[k, depth:, c * depth : (c + 1) * depth] = down_block[c * depth : (c + 1) * depth]
            writes.append(pltpu.make_async_copy(block.at[k], blocks[k], b_sem.at[k]))
            writes[-1].start()
        for one in writes:
            one.wait()

    rows = n_chunks * n * piece_rows
    half = (n // 2 * pair, width)
    far = pl.BlockSpec(memory_space=pl.ANY)
    near = pl.BlockSpec(memory_space=pltpu.VMEM)
    out = pl.pallas_call(
        kernel,
        out_shape=[
            jax.ShapeDtypeStruct((half[0] + (EXTRA if at == 1 else 0), width), dtype) for at in range(2 * n_chunks)
        ]
        + [jax.ShapeDtypeStruct((2 * depth, units), dtype)] * n_dp
        + [jax.ShapeDtypeStruct((EXTRA, width), dtype)],
        in_specs=[far] * (n_chunks * n + 2 + n_got) + [near] * 2,
        out_specs=[far] * (2 * n_chunks + n_dp) + [near],
        scratch_shapes=[
            pltpu.VMEM((n_chunks * n, pair, width), dtype),
            pltpu.VMEM((rows, width), dtype),
            pltpu.VMEM((rows, units), dtype),
            pltpu.VMEM((rows, units), dtype),
            pltpu.VMEM((2 * n_chunks, *half), dtype),
            pltpu.VMEM((n_dp, 2 * depth, units), dtype),
            pltpu.VMEM((width, units), dtype),
            pltpu.VMEM((units, width), dtype),
            pltpu.VMEM((EXTRA, width), jnp.float32),
            pltpu.SemaphoreType.DMA((n_chunks * n,)),
            pltpu.SemaphoreType.DMA((2 + n_got * (1 + strips),)),
            pltpu.SemaphoreType.DMA((2 * n_chunks + 1,)),
            pltpu.SemaphoreType.DMA((n_dp,)),
        ],
        compiler_params=pltpu.CompilerParams(vmem_limit_bytes=56 * 1024 * 1024),
        cost_estimate=pl.CostEstimate(
            flops=10 * rows * width * units,
            bytes_accessed=8 * rows * width + 8 * width * units,
            transcendentals=rows * units,
        ),
        name="core",
    )(
        *[piece for chunk in chunks for piece in chunk],
        w_up,
        w_down,
        *pieces_of_weights,
        gain.reshape(1, width),
        bias.reshape(1, width),
    )
    halves = [out[2 * i : 2 * i + 2] for i in range(n_chunks)]
    return halves, list(out[2 * n_chunks : -1]), out[-1]


def finish(blocks, terms, stats, first_out, second_out, grad_first, gain, bias, w_shapes, scale):
    (rows, width), n_dp = first_out.shape, len(blocks)
    depth, units = w_shapes[0][0], w_shapes[0][1] // n_dp
    strips, n_terms = units // depth, len(terms)

    def kernel(*refs):
        parts, adds, (stat_ref, first_ref, second_ref, grad_ref, gain_ref, bias_ref), outs = (
            refs[:n_dp],
            refs[n_dp : n_dp + n_terms],
            refs[n_dp + n_terms : n_dp + n_terms + 6],
            refs[n_dp + n_terms + 6 :],
        )
        second_in, grad_in, up_out, down_out, norm_out = outs
        place = lax.axis_index("dp")
        for k in range(n_dp):
            first = pl.multiple_of((place ^ k) * units, units)
            up_out[:, pl.ds(first, units)] = parts[k][:depth, :].astype(jnp.float32) * scale
            for c in range(strips):
                block = parts[k][depth : 2 * depth, c * depth : (c + 1) * depth]
                row = pl.multiple_of(first + c * depth, depth)
                down_out[pl.ds(row, depth), :] = block.astype(jnp.float32) * scale
        total = sum(ref[: 2 * rows, :].astype(jnp.float32) for ref in adds)
        second_in[...] = (second_ref[...].astype(jnp.float32) - total[:rows]).astype(second_in.dtype)
        values = first_ref[...].astype(jnp.float32)
        centred = values - jnp.mean(values, axis=-1, keepdims=True)
        inv_std = lax.rsqrt(jnp.mean(centred * centred, axis=-1, keepdims=True) + epsilon)
        standard = centred * inv_std
        grad_std = total[rows:] * gain_ref[...]
        grad_rows = inv_std * (
            grad_std
            - jnp.mean(grad_std, axis=-1, keepdims=True)
            - standard * jnp.mean(grad_std * standard, axis=-1, keepdims=True)
        )
        grad_in[...] = grad_ref[...].astype(jnp.float32) + grad_rows
        one, two = stat_ref[...].astype(jnp.float32), adds[-1][2 * rows :, :].astype(jnp.float32)
        norm_out[...] = ((one[0:2] + one[2:4]) + (two[0:2] + two[2:4])) * scale

    def whole(x):
        return pl.BlockSpec(x.shape, lambda i: (0, 0))

    arrays = [*blocks, *terms, stats, first_out, second_out, grad_first, gain.reshape(1, width), bias.reshape(1, width)]
    in_specs = [whole(x) for x in arrays]
    for i in range(n_terms - 1):
        in_specs[n_dp + i] = pl.BlockSpec((2 * rows, width), lambda i: (0, 0))
    out_shape = [
        jax.ShapeDtypeStruct((rows, width), second_out.dtype),
        jax.ShapeDtypeStruct((rows, width), jnp.float32),
        jax.ShapeDtypeStruct(w_shapes[0], jnp.float32),
        jax.ShapeDtypeStruct(w_shapes[1], jnp.float32),
        jax.ShapeDtypeStruct((2, width), jnp.float32),
    ]
    return pl.pallas_call(
        kernel,
        out_shape=out_shape,
        grid=(1,),
        in_specs=in_specs,
        out_specs=[whole(x) for x in out_shape],
        compiler_params=pltpu.CompilerParams(vmem_limit_bytes=48 * 1024 * 1024),
        cost_estimate=pl.CostEstimate(
            flops=0, bytes_accessed=12 * w_shapes[0][0] * w_shapes[0][1], transcendentals=0
        ),
        name="finish",
    )(*arrays)


def join(rows, terms, stats=()):
    width = terms[0][0].shape[1]
    arrays = [*terms, *stats]
    n_terms = len(terms)

    def kernel(*refs):
        out = refs[len(arrays)]
        total = sum(ref[...].astype(jnp.float32) for ref in refs[:n_terms])
        out[:rows, :] = total.astype(out.dtype)
        if stats:
            one, two = (ref[...].astype(jnp.float32) for ref in refs[n_terms : n_terms + 2])
            both = (one[0:2] + one[2:4]) + (two[0:2] + two[2:4])
            tail = refs[-1]
            tail[...] = jnp.zeros_like(tail)
            tail[0:2, :] = both.astype(tail.dtype)
            tail[2:4, :] = (both - tail[0:2, :].astype(jnp.float32)).astype(tail.dtype)
            out[rows:, :] = tail[...]

    def spec(height, place):
        return pl.BlockSpec((height, width), lambda i: (place, 0))

    out_shape = [jax.ShapeDtypeStruct((rows + (EXTRA if stats else 0), width), jnp.bfloat16)]
    out_specs = [spec(out_shape[0].shape[0], 0)]
    if stats:
        out_shape.append(jax.ShapeDtypeStruct((EXTRA, width), jnp.bfloat16))
        out_specs.append(spec(EXTRA, 0))
    out = pl.pallas_call(
        kernel,
        out_shape=out_shape,
        grid=(1,),
        in_specs=[spec(rows, place) for _, place in terms] + [spec(EXTRA, place) for _, place in stats],
        out_specs=out_specs,
        cost_estimate=pl.CostEstimate(
            flops=0, bytes_accessed=2 * (len(terms) + 1) * rows * width, transcendentals=0
        ),
        name="join",
    )(*(x for x, _ in arrays))
    return out if stats else out[0]


def after(values, *others):
    return lax.optimization_barrier((values, *others))[0]


def gather_tokens_body(
    first_out, second_out, grad_first, grad_second, w_up, w_down, norm_gain, norm_bias
):
    n_dp, n_tensor, n_groups = (lax.axis_size(axis) for axis in ("dp", "tensor", "groups"))
    own_rows, depth = first_out.shape[0], w_up.shape[0]
    units = w_up.shape[1] // n_dp
    mates = 2 if n_groups % 2 == 0 else 1
    place = lax.axis_index("dp")
    top = bits_of(n_dp)[0]

    high, others = bits_of(n_tensor)[0], bits_of(n_tensor)[1:]
    own, *sends = pack(first_out, grad_second, w_up, w_down, mates)
    tokens, chunks, got, crossed = {0: own}, {}, {}, {}

    def tokens_dp(k, *first):
        tokens[k] = swap(after(tokens[k & (k - 1)], *first), "dp", k & -k, f"tokens_{k}")

    def tokens_tensor(k, *first):
        start = after(tokens[k], *first)
        chunks[k] = {0: tokens[k], high: swap(start, "tensor", high, f"tokens_{k}_{high}")}

    def tokens_rest(k, *first):
        for bit in others:
            for j in list(chunks[k]):
                piece = after(chunks[k][j], *first)
                chunks[k][j | bit] = swap(piece, "tensor", bit, f"tokens_{k}_{j | bit}")

    def weights_groups(k, *first):
        if mates == 2:
            crossed[k] = swap(after(got[k], *first), "groups", 1, f"weights_{k}")

    def weights_dp(k, *first):
        got[k] = swap(after(sends[k - 1], *first), "dp", k, f"weights_{k}")

    for bit in reversed(bits_of(n_dp)):
        tokens_dp(bit)
    tokens_tensor(0)
    tokens_rest(0)
    tokens_tensor(1, tokens[top], chunks[0][high])
    stage = [*tokens.values(), *chunks[0].values()]
    for k in range(2, n_dp):
        if k & (k - 1):
            tokens_dp(k, *stage)
        weights_dp(k, *stage, *([got[top]] if top in got else []))
    for k in range(2, n_dp):
        tokens_rest(k - 1)
        stage = [got[top]]
        if k & (k - 1):
            weights_groups(top)
            stage = [tokens[k], *got.values(), *crossed.values(), *chunks[k - 2].values()]
        tokens_tensor(k, *stage, chunks[k - 1][high])
    weights_dp(1, *stage)
    for k in [*range(2, n_dp), 1]:
        if k not in crossed:
            weights_groups(k)
    tokens_rest(n_dp - 1, *crossed.values())
    got = {k: [got[k]] + ([crossed[k]] if k in crossed else []) for k in got}

    order = sorted(chunks, reverse=True)
    halves, blocks, stats = core(
        [[chunks[k][j] for j in range(n_tensor)] for k in order], w_up, w_down, got, mates, norm_gain, norm_bias
    )
    blocks = dict(enumerate(blocks))
    blocks[top] = swap(blocks[top], "dp", top, f"grads_{top}")

    for k in range(1, top):
        blocks[k] = swap(blocks[k], "dp", k, f"grads_{k}")
    third = {}
    for k in range(top + 1, n_dp):
        third[k] = blocks[k]

    def add(terms):
        spans = (x[place * span : (place + 1) * span].astype(jnp.float32) for x, place in terms)
        return sum(spans).astype(jnp.bfloat16)

    sums, behind, span, waiting = {}, (), 2 * own_rows, None
    for k, (even, odd) in zip(order, halves, strict=True):
        came = swap(odd, "tensor", 1, f"sums_{k}_1")
        if k == order[0]:
            waiting = (came, even.shape[0] // EXTRA)
        parts = {2 * j: [(x, j) for x in (even, came)] for j in range(n_tensor // 2)}
        for bit in reversed(bits_of(n_tensor)[:-1]):
            for j in [j for j in parts if j & bit]:
                if k == order[0] and j == bit:
                    send, stats = join(span, parts.pop(j), [(stats, 0), waiting])
                else:
                    send = add(parts.pop(j))
                if behind and k:
                    behind += (blocks[1 if k == top else top],)
                came = swap(after(send, *behind), "tensor", bit, f"sums_{k}_{j}")
                if k == order[0] and j == bit:
                    waiting = (came, span // EXTRA)
                parts[j ^ bit].append((came, 0))
                behind = (came,)
        sums[k] = parts[0]
    came = {}
    for bit in bits_of(n_dp)[::-1]:
        for k in [k for k in order if k & bit and k in sums and k != bit]:
            if k == (n_dp - 1) & -bit:
                send, stats = join(span, sums.pop(k), [(stats, 0), waiting])
            else:
                send = add(sums.pop(k))
            came[k] = swap(send, "dp", bit, f"sums_{k}")
            for j in third:
                blocks[j] = swap(after(third[j], blocks[top], send), "dp", j, f"grads_{j}")
            third = {}
            if k == (n_dp - 1) & -bit:
                waiting = (came[k], span // EXTRA)
            sums[k ^ bit].append((came[k], 0))
    last, stats = join(span, sums[top], [(stats, 0), waiting])
    came[top] = swap(last, "dp", top, f"sums_{top}")
    for bit in bits_of(n_dp)[:0:-1]:
        came[bit] = swap(after(add(sums[bit]), last), "dp", bit, f"sums_{bit}")

    scale = (own_rows * n_tensor * n_dp) ** (-0.5)
    terms = [*(x for x, _ in sums[0]), *(came[bit] for bit in bits_of(n_dp)[::-1])]
    return tuple(
        finish(
            [blocks[k] for k in range(n_dp)],
            terms,
            stats,
            first_out,
            second_out,
            grad_first,
            norm_gain,
            norm_bias,
            (w_up.shape, w_down.shape),
            scale,
        )
    )


def body(first_out, second_out, grad_first, grad_second, w_up, *rest):
    n_dp, n_tensor = lax.axis_size("dp"), lax.axis_size("tensor")
    powers = all(size > 1 and size & (size - 1) == 0 for size in (n_dp, n_tensor))
    few_tokens = first_out.shape[0] * n_tensor < w_up.shape[1]
    units, depth = w_up.shape[1] // n_dp, w_up.shape[0]
    fits = w_up.shape[1] % n_dp == 0 and units % depth == 0 and depth % 128 == 0
    fits = fits and first_out.shape[1] == 2 * units and n_dp > 2 and n_tensor > 2
    pick = gather_tokens_body if powers and few_tokens and fits else gather_weights_body
    return pick(first_out, second_out, grad_first, grad_second, w_up, *rest)


def solution(mesh):
    in_specs = (
        P(("groups", "tensor", "dp"), None),
        P(("groups", "tensor", "dp"), None),
        P(("groups", "tensor", "dp"), None),
        P(("groups", "tensor", "dp"), None),
        P("dp", "tensor"),
        P("tensor", "dp"),
        P(),
        P(),
    )
    out_specs = (
        P(("groups", "tensor", "dp"), None),
        P(("groups", "tensor", "dp"), None),
        P(("groups", "dp"), "tensor"),
        P(("groups", "tensor"), "dp"),
        P("groups", None),
    )
    return jax.shard_map(body, mesh=mesh, in_specs=in_specs, out_specs=out_specs, check_vma=False)
```

```python
import math

import jax
import jax.numpy as jnp
from jax import lax
from jax.experimental import pallas as pl
from jax.experimental.pallas import tpu as pltpu
from jax.sharding import PartitionSpec as P

epsilon = 1e-06
EXTRA = 16


def normalize(row_data, norm_gain, norm_bias):
    values = row_data.astype(jnp.float32)
    row_mean = jnp.mean(values, axis=-1, keepdims=True)
    centred = values - row_mean
    inv_std = lax.rsqrt(jnp.mean(centred * centred, axis=-1, keepdims=True) + epsilon)
    standard = centred * inv_std
    normed = (standard * norm_gain + norm_bias).astype(jnp.bfloat16)
    return (standard, inv_std, normed)


def contract_tokens(left_rows, right_rows):
    return lax.dot_general(
        left_rows, right_rows, (((0,), (0,)), ((), ())), preferred_element_type=jnp.float32
    )


def contract_last(left_rows, right_rows):
    return lax.dot_general(
        left_rows, right_rows, (((1,), (1,)), ((), ())), preferred_element_type=jnp.float32
    )


def finish_rows(branch, grad_normed, second_out, grad_first, first_out, norm_gain, norm_bias):
    standard, inv_std, _ = normalize(first_out, norm_gain, norm_bias)
    second_in = (second_out.astype(jnp.float32) - branch).astype(jnp.bfloat16)
    grad_std = grad_normed * norm_gain
    grad_rows = inv_std * (
        grad_std
        - jnp.mean(grad_std, axis=-1, keepdims=True)
        - standard * jnp.mean(grad_std * standard, axis=-1, keepdims=True)
    )
    return second_in, grad_first.astype(jnp.float32) + grad_rows


def gather_weights_body(
    first_out, second_out, grad_first, grad_second, w_up, w_down, norm_gain, norm_bias
):
    own_rows = first_out.shape[0]
    up_full = lax.all_gather(w_up, "dp", axis=0, tiled=True)
    down_full = lax.all_gather(w_down, "dp", axis=1, tiled=True)
    first_all = lax.all_gather(first_out, "tensor", axis=0, tiled=True)
    grad_all = lax.all_gather(grad_second, "tensor", axis=0, tiled=True)
    standard_all, _, normed = normalize(first_all, norm_gain, norm_bias)
    offset = lax.axis_index("tensor") * own_rows
    standard = lax.dynamic_slice_in_dim(standard_all, offset, own_rows, 0)
    preact = jnp.dot(normed, up_full, preferred_element_type=jnp.float32)
    hidden = jax.nn.gelu(preact).astype(jnp.bfloat16)
    branch = lax.psum_scatter(
        jnp.dot(hidden, down_full, preferred_element_type=jnp.float32).astype(jnp.bfloat16),
        "tensor",
        scatter_dimension=0,
        tiled=True,
    ).astype(jnp.float32)
    tokens = own_rows * lax.axis_size("tensor") * lax.axis_size("dp")
    grad_scale = tokens ** (-0.5)
    grad_down_part = contract_tokens(hidden, grad_all)
    grad_down = (
        lax.psum_scatter(
            grad_down_part.astype(jnp.bfloat16), "dp", scatter_dimension=1, tiled=True
        ).astype(jnp.float32)
        * grad_scale
    )
    grad_hidden = contract_last(grad_all, down_full)
    grad_pre = jax.vjp(jax.nn.gelu, preact)[1](grad_hidden)[0].astype(jnp.bfloat16)
    grad_up_part = contract_tokens(normed, grad_pre)
    grad_up = (
        lax.psum_scatter(
            grad_up_part.astype(jnp.bfloat16), "dp", scatter_dimension=0, tiled=True
        ).astype(jnp.float32)
        * grad_scale
    )
    grad_normed = lax.psum_scatter(
        contract_last(grad_pre, up_full).astype(jnp.bfloat16),
        "tensor",
        scatter_dimension=0,
        tiled=True,
    ).astype(jnp.float32)
    second_in, grad_first_in = finish_rows(
        branch, grad_normed, second_out, grad_first, first_out, norm_gain, norm_bias
    )
    local_stats = jnp.stack([jnp.sum(grad_normed * standard, axis=0), jnp.sum(grad_normed, axis=0)])
    grad_norm = lax.psum(local_stats, ("tensor", "dp")) * grad_scale
    return (second_in, grad_first_in, grad_up, grad_down, grad_norm)


def swap(values, axis, mask, scope):
    with jax.named_scope(scope):
        return lax.ppermute(values, axis, [(i, i ^ mask) for i in range(lax.axis_size(axis))])


def bits_of(size):
    return [1 << b for b in reversed(range(size.bit_length() - 1))]


def pack(first_out, grad_second, w_up, w_down, mates):
    n_dp, (own_rows, width) = lax.axis_size("dp"), first_out.shape
    depth, units = w_up.shape[0], w_up.shape[1] // n_dp
    strips, rows = units // depth, depth // mates

    def kernel(first_ref, grad_ref, up_ref, down_ref, own, *sends):
        place, mate = lax.axis_index("dp"), lax.rem(lax.axis_index("groups"), mates)
        own[:own_rows, :] = first_ref[...]
        own[own_rows:, :] = grad_ref[...]
        for k in range(1, n_dp):
            first = pl.multiple_of((place ^ k) * units, units)
            send = sends[k - 1]
            send[:, :units] = up_ref[pl.ds(pl.multiple_of(mate * rows, rows), rows), pl.ds(first, units)]
            for c in range(strips):
                row = pl.multiple_of(first + mate * (units // mates) + c * rows, rows)
                send[:, units + c * depth : units + (c + 1) * depth] = down_ref[pl.ds(row, rows), :]

    return pl.pallas_call(
        kernel,
        out_shape=[jax.ShapeDtypeStruct((2 * own_rows, width), w_up.dtype)]
        + [jax.ShapeDtypeStruct((rows, width), w_up.dtype)] * (n_dp - 1),
        in_specs=[pl.BlockSpec(memory_space=pltpu.VMEM)] * 4,
        out_specs=[pl.BlockSpec(memory_space=pltpu.VMEM)] * n_dp,
        cost_estimate=pl.CostEstimate(flops=0, bytes_accessed=8 * w_up.size, transcendentals=0),
        name="pack",
    )(first_out, grad_second, w_up, w_down)


def core(chunks, w_up, w_down, got, mates, gain, bias):
    n_chunks, n, n_dp = len(chunks), len(chunks[0]), lax.axis_size("dp")
    (piece_rows, width), units = chunks[0][0].shape, w_up.shape[1] // n_dp
    piece_rows //= 2
    depth = width // n_dp
    strips, pair = units // depth, 2 * piece_rows
    slope = (2.0 / math.pi) ** 0.5
    dtype = w_up.dtype
    pieces_of_weights = [piece for k in range(1, n_dp) for piece in got[k]]
    n_got = len(pieces_of_weights)

    def kernel(*refs):
        toks, refs = refs[: n_chunks * n], refs[n_chunks * n :]
        (own_up, own_down), weights, (gain_ref, bias_ref), refs = (
            refs[:2],
            list(refs[2 : 2 + n_got]),
            refs[2 + n_got : 4 + n_got],
            refs[4 + n_got :],
        )
        outs, blocks, stat_ref = refs[: 2 * n_chunks], refs[2 * n_chunks : 2 * n_chunks + n_dp], refs[2 * n_chunks + n_dp]
        scratch = refs[2 * n_chunks + n_dp + 1 :]
        tok, norm, hid, pre, part, block, up_ref, down_ref, total, in_sem, w_sem, out_sem, b_sem = scratch
        place, mate = lax.axis_index("dp"), lax.rem(lax.axis_index("groups"), mates)
        reads, loads, writes = [], [], []

        def load(src, dst):
            loads.append(pltpu.make_async_copy(src, dst, w_sem.at[len(loads)]))
            loads[-1].start()

        for i, ref in enumerate(toks):
            reads.append(pltpu.make_async_copy(ref, tok.at[i], in_sem.at[i]))
            if i < n:
                reads[-1].start()
        mine = pl.ds(pl.multiple_of(place * units, units), units)
        rows = pl.ds(pl.multiple_of(place * depth, depth), depth)
        load(own_up.at[:, mine], up_ref.at[rows, :])
        load(own_down.at[mine, :], down_ref.at[:, rows])
        for k in range(1, n_dp):
            first = pl.multiple_of((place ^ k) * depth, depth)
            many = len(got[k])
            rows = depth // many
            for j in range(many):
                piece = weights.pop(0)
                which = mate ^ j if many > 1 else 0
                row = pl.multiple_of(first + which * rows, rows)
                load(piece.at[:, pl.ds(0, units)], up_ref.at[pl.ds(row, rows), :])
                for c in range(strips):
                    row = pl.multiple_of(which * (units // many) + c * rows, rows)
                    load(
                        piece.at[:, pl.ds(units + c * depth, depth)],
                        down_ref.at[pl.ds(row, rows), pl.ds(first, depth)],
                    )
        for one in reads[n:]:
            one.start()
        total[...] = jnp.zeros_like(total)
        for i in range(n_chunks):
            for one in reads[i * n : (i + 1) * n] + (loads if i == 0 else []):
                one.wait()

            @pl.loop(0, n // 2)
            def _(t):
                at = i * n + 2 * t
                span = pl.ds(pl.multiple_of(at * piece_rows, pair), pair)
                values = tok[pl.ds(at, 2), :piece_rows].reshape(pair, width).astype(jnp.float32)
                centred = values - jnp.mean(values, axis=-1, keepdims=True)
                inv_std = lax.rsqrt(jnp.mean(centred * centred, axis=-1, keepdims=True) + epsilon)
                standard = centred * inv_std
                normed = (standard * gain_ref[...] + bias_ref[...]).astype(dtype)
                norm[span, :] = normed
                x = jnp.dot(normed, up_ref[...], preferred_element_type=jnp.float32)
                gate = jnp.tanh(slope * (x + 0.044715 * (x * x * x)))
                half = 0.5 + 0.5 * gate
                hidden = (x * half).astype(dtype)
                hid[span, :] = hidden
                rise = half + (0.5 * slope) * x * (1.0 - gate * gate) * (1.0 + (3 * 0.044715) * (x * x))
                grads = tok[pl.ds(at, 2), piece_rows:].reshape(pair, width)
                grad_pre = (contract_last(grads, down_ref[...]) * rise).astype(dtype)
                pre[span, :] = grad_pre
                branch = jnp.dot(hidden, down_ref[...], preferred_element_type=jnp.float32)
                grad_normed = contract_last(grad_pre, up_ref[...])
                total[0:1, :] += jnp.sum(grad_normed * standard, axis=0, keepdims=True)
                total[1:2, :] += jnp.sum(grad_normed, axis=0, keepdims=True)
                row = pl.multiple_of(t * pair, pair)
                for odd in range(2):
                    own = slice(odd * piece_rows, (odd + 1) * piece_rows)
                    part[2 * i + odd, pl.ds(row, piece_rows), :] = branch[own].astype(dtype)
                    part[2 * i + odd, pl.ds(row + piece_rows, piece_rows), :] = grad_normed[own].astype(dtype)

            for odd in (1, 0):
                at = 2 * i + odd
                out = outs[at].at[pl.ds(0, half[0]), :]
                writes.append(pltpu.make_async_copy(part.at[at], out, out_sem.at[at]))
                writes[-1].start()
        stat_ref[...] = jnp.zeros_like(stat_ref)
        stat_ref[0:2, :] = total[0:2, :].astype(dtype)
        stat_ref[2:4, :] = (total[0:2, :] - stat_ref[0:2, :].astype(jnp.float32)).astype(dtype)
        tail = outs[1].at[pl.ds(half[0], EXTRA), :]
        writes.append(pltpu.make_async_copy(stat_ref, tail, out_sem.at[2 * n_chunks]))
        writes[-1].start()
        top = bits_of(n_dp)[0]
        for k in sorted(range(n_dp), key=lambda k: (k < top, k)):
            columns = pl.ds(pl.multiple_of((place ^ k) * depth, depth), depth)
            block[k, :depth, :] = contract_tokens(norm[:, columns], pre[...]).astype(dtype)
            grads = tok[:, piece_rows:, columns].reshape(n_chunks * n * piece_rows, depth)
            down_block = contract_tokens(hid[...], grads).astype(dtype)
            for c in range(strips):
                block[k, depth:, c * depth : (c + 1) * depth] = down_block[c * depth : (c + 1) * depth]
            writes.append(pltpu.make_async_copy(block.at[k], blocks[k], b_sem.at[k]))
            writes[-1].start()
        for one in writes:
            one.wait()

    rows = n_chunks * n * piece_rows
    half = (n // 2 * pair, width)
    far = pl.BlockSpec(memory_space=pl.ANY)
    near = pl.BlockSpec(memory_space=pltpu.VMEM)
    out = pl.pallas_call(
        kernel,
        out_shape=[
            jax.ShapeDtypeStruct((half[0] + (EXTRA if at == 1 else 0), width), dtype) for at in range(2 * n_chunks)
        ]
        + [jax.ShapeDtypeStruct((2 * depth, units), dtype)] * n_dp
        + [jax.ShapeDtypeStruct((EXTRA, width), dtype)],
        in_specs=[far] * (n_chunks * n + 2 + n_got) + [near] * 2,
        out_specs=[far] * (2 * n_chunks + n_dp) + [near],
        scratch_shapes=[
            pltpu.VMEM((n_chunks * n, pair, width), dtype),
            pltpu.VMEM((rows, width), dtype),
            pltpu.VMEM((rows, units), dtype),
            pltpu.VMEM((rows, units), dtype),
            pltpu.VMEM((2 * n_chunks, *half), dtype),
            pltpu.VMEM((n_dp, 2 * depth, units), dtype),
            pltpu.VMEM((width, units), dtype),
            pltpu.VMEM((units, width), dtype),
            pltpu.VMEM((EXTRA, width), jnp.float32),
            pltpu.SemaphoreType.DMA((n_chunks * n,)),
            pltpu.SemaphoreType.DMA((2 + n_got * (1 + strips),)),
            pltpu.SemaphoreType.DMA((2 * n_chunks + 1,)),
            pltpu.SemaphoreType.DMA((n_dp,)),
        ],
        compiler_params=pltpu.CompilerParams(vmem_limit_bytes=56 * 1024 * 1024),
        cost_estimate=pl.CostEstimate(
            flops=10 * rows * width * units,
            bytes_accessed=8 * rows * width + 8 * width * units,
            transcendentals=rows * units,
        ),
        name="core",
    )(
        *[piece for chunk in chunks for piece in chunk],
        w_up,
        w_down,
        *pieces_of_weights,
        gain.reshape(1, width),
        bias.reshape(1, width),
    )
    halves = [out[2 * i : 2 * i + 2] for i in range(n_chunks)]
    return halves, list(out[2 * n_chunks : -1]), out[-1]


def finish(blocks, terms, stats, first_out, second_out, grad_first, gain, bias, w_shapes, scale):
    (rows, width), n_dp = first_out.shape, len(blocks)
    depth, units = w_shapes[0][0], w_shapes[0][1] // n_dp
    strips, n_terms = units // depth, len(terms)

    def kernel(*refs):
        parts, adds, (stat_ref, first_ref, second_ref, grad_ref, gain_ref, bias_ref), outs = (
            refs[:n_dp],
            refs[n_dp : n_dp + n_terms],
            refs[n_dp + n_terms : n_dp + n_terms + 6],
            refs[n_dp + n_terms + 6 :],
        )
        second_in, grad_in, up_out, down_out, norm_out = outs
        place = lax.axis_index("dp")
        for k in range(n_dp):
            first = pl.multiple_of((place ^ k) * units, units)
            up_out[:, pl.ds(first, units)] = parts[k][:depth, :].astype(jnp.float32) * scale
            for c in range(strips):
                block = parts[k][depth : 2 * depth, c * depth : (c + 1) * depth]
                row = pl.multiple_of(first + c * depth, depth)
                down_out[pl.ds(row, depth), :] = block.astype(jnp.float32) * scale
        total = sum(ref[: 2 * rows, :].astype(jnp.float32) for ref in adds)
        second_in[...] = (second_ref[...].astype(jnp.float32) - total[:rows]).astype(second_in.dtype)
        values = first_ref[...].astype(jnp.float32)
        centred = values - jnp.mean(values, axis=-1, keepdims=True)
        inv_std = lax.rsqrt(jnp.mean(centred * centred, axis=-1, keepdims=True) + epsilon)
        standard = centred * inv_std
        grad_std = total[rows:] * gain_ref[...]
        grad_rows = inv_std * (
            grad_std
            - jnp.mean(grad_std, axis=-1, keepdims=True)
            - standard * jnp.mean(grad_std * standard, axis=-1, keepdims=True)
        )
        grad_in[...] = grad_ref[...].astype(jnp.float32) + grad_rows
        one, two = stat_ref[...].astype(jnp.float32), adds[-1][2 * rows :, :].astype(jnp.float32)
        norm_out[...] = ((one[0:2] + one[2:4]) + (two[0:2] + two[2:4])) * scale

    def whole(x):
        return pl.BlockSpec(x.shape, lambda i: (0, 0))

    arrays = [*blocks, *terms, stats, first_out, second_out, grad_first, gain.reshape(1, width), bias.reshape(1, width)]
    in_specs = [whole(x) for x in arrays]
    for i in range(n_terms - 1):
        in_specs[n_dp + i] = pl.BlockSpec((2 * rows, width), lambda i: (0, 0))
    out_shape = [
        jax.ShapeDtypeStruct((rows, width), second_out.dtype),
        jax.ShapeDtypeStruct((rows, width), jnp.float32),
        jax.ShapeDtypeStruct(w_shapes[0], jnp.float32),
        jax.ShapeDtypeStruct(w_shapes[1], jnp.float32),
        jax.ShapeDtypeStruct((2, width), jnp.float32),
    ]
    return pl.pallas_call(
        kernel,
        out_shape=out_shape,
        grid=(1,),
        in_specs=in_specs,
        out_specs=[whole(x) for x in out_shape],
        compiler_params=pltpu.CompilerParams(vmem_limit_bytes=48 * 1024 * 1024),
        cost_estimate=pl.CostEstimate(
            flops=0, bytes_accessed=12 * w_shapes[0][0] * w_shapes[0][1], transcendentals=0
        ),
        name="finish",
    )(*arrays)


def join(rows, terms, stats=()):
    width = terms[0][0].shape[1]
    arrays = [*terms, *stats]
    n_terms = len(terms)

    def kernel(*refs):
        out = refs[len(arrays)]
        total = sum(ref[...].astype(jnp.float32) for ref in refs[:n_terms])
        out[:rows, :] = total.astype(out.dtype)
        if stats:
            one, two = (ref[...].astype(jnp.float32) for ref in refs[n_terms : n_terms + 2])
            both = (one[0:2] + one[2:4]) + (two[0:2] + two[2:4])
            tail = refs[-1]
            tail[...] = jnp.zeros_like(tail)
            tail[0:2, :] = both.astype(tail.dtype)
            tail[2:4, :] = (both - tail[0:2, :].astype(jnp.float32)).astype(tail.dtype)
            out[rows:, :] = tail[...]

    def spec(height, place):
        return pl.BlockSpec((height, width), lambda i: (place, 0))

    out_shape = [jax.ShapeDtypeStruct((rows + (EXTRA if stats else 0), width), jnp.bfloat16)]
    out_specs = [spec(out_shape[0].shape[0], 0)]
    if stats:
        out_shape.append(jax.ShapeDtypeStruct((EXTRA, width), jnp.bfloat16))
        out_specs.append(spec(EXTRA, 0))
    out = pl.pallas_call(
        kernel,
        out_shape=out_shape,
        grid=(1,),
        in_specs=[spec(rows, place) for _, place in terms] + [spec(EXTRA, place) for _, place in stats],
        out_specs=out_specs,
        cost_estimate=pl.CostEstimate(
            flops=0, bytes_accessed=2 * (len(terms) + 1) * rows * width, transcendentals=0
        ),
        name="join",
    )(*(x for x, _ in arrays))
    return out if stats else out[0]


def after(values, *others):
    return lax.optimization_barrier((values, *others))[0]


def gather_tokens_body(
    first_out, second_out, grad_first, grad_second, w_up, w_down, norm_gain, norm_bias
):
    n_dp, n_tensor, n_groups = (lax.axis_size(axis) for axis in ("dp", "tensor", "groups"))
    own_rows, depth = first_out.shape[0], w_up.shape[0]
    units = w_up.shape[1] // n_dp
    mates = 2 if n_groups % 2 == 0 else 1
    place = lax.axis_index("dp")
    top = bits_of(n_dp)[0]

    high, others = bits_of(n_tensor)[0], bits_of(n_tensor)[1:]
    own, *sends = pack(first_out, grad_second, w_up, w_down, mates)
    tokens, chunks, got, crossed = {0: own}, {}, {}, {}

    def tokens_dp(k, *first):
        tokens[k] = swap(after(tokens[k & (k - 1)], *first), "dp", k & -k, f"tokens_{k}")

    def tokens_tensor(k, *first):
        start = after(tokens[k], *first)
        chunks[k] = {0: tokens[k], high: swap(start, "tensor", high, f"tokens_{k}_{high}")}

    def tokens_rest(k, *first):
        for bit in others:
            for j in list(chunks[k]):
                piece = after(chunks[k][j], *first)
                chunks[k][j | bit] = swap(piece, "tensor", bit, f"tokens_{k}_{j | bit}")

    def weights_groups(k, *first):
        if mates == 2:
            crossed[k] = swap(after(got[k], *first), "groups", 1, f"weights_{k}")

    def weights_dp(k, *first):
        got[k] = swap(after(sends[k - 1], *first), "dp", k, f"weights_{k}")

    for bit in reversed(bits_of(n_dp)):
        tokens_dp(bit)
    tokens_tensor(0)
    tokens_rest(0)
    tokens_tensor(1, tokens[top], chunks[0][high])
    stage = [*tokens.values(), *chunks[0].values()]
    for k in range(2, n_dp):
        if k & (k - 1):
            tokens_dp(k, *stage)
        weights_dp(k, *stage, *([got[top]] if top in got else []))
    for k in range(2, n_dp):
        tokens_rest(k - 1)
        stage = [got[top]]
        if k & (k - 1):
            weights_groups(top)
            stage = [tokens[k], *got.values(), *crossed.values(), *chunks[k - 2].values()]
        tokens_tensor(k, *stage, chunks[k - 1][high])
    weights_dp(1, *stage)
    for k in [*range(2, n_dp), 1]:
        if k not in crossed:
            weights_groups(k)
    tokens_rest(n_dp - 1, *crossed.values())
    got = {k: [got[k]] + ([crossed[k]] if k in crossed else []) for k in got}

    order = sorted(chunks, reverse=True)
    halves, blocks, stats = core(
        [[chunks[k][j] for j in range(n_tensor)] for k in order], w_up, w_down, got, mates, norm_gain, norm_bias
    )
    blocks = dict(enumerate(blocks))
    blocks[top] = swap(blocks[top], "dp", top, f"grads_{top}")

    for k in range(top + 1, n_dp):
        blocks[k] = swap(after(blocks[k], blocks[top]), "dp", k, f"grads_{k}")

    def add(terms):
        spans = (x[place * span : (place + 1) * span].astype(jnp.float32) for x, place in terms)
        return sum(spans).astype(jnp.bfloat16)

    sums, behind, span, waiting = {}, (), 2 * own_rows, None
    for k, (even, odd) in zip(order, halves, strict=True):
        came = swap(odd, "tensor", 1, f"sums_{k}_1")
        if k == order[0]:
            waiting = (came, even.shape[0] // EXTRA)
        parts = {2 * j: [(x, j) for x in (even, came)] for j in range(n_tensor // 2)}
        for bit in reversed(bits_of(n_tensor)[:-1]):
            for j in [j for j in parts if j & bit]:
                if k == order[0] and j == bit:
                    send, stats = join(span, parts.pop(j), [(stats, 0), waiting])
                else:
                    send = add(parts.pop(j))
                if k < top:
                    behind += (blocks[n_dp - 1 if k == 0 else top],)
                came = swap(after(send, *behind), "tensor", bit, f"sums_{k}_{j}")
                if k == order[0] and j == bit:
                    waiting = (came, span // EXTRA)
                parts[j ^ bit].append((came, 0))
                behind = (came,)
                if k == top:
                    for i in range(1, top):
                        blocks[i] = swap(after(blocks[i], came), "dp", i, f"grads_{i}")
        sums[k] = parts[0]
    came = {}
    for bit in bits_of(n_dp)[::-1]:
        for k in [k for k in order if k & bit and k in sums and k != bit]:
            if k == (n_dp - 1) & -bit:
                send, stats = join(span, sums.pop(k), [(stats, 0), waiting])
            else:
                send = add(sums.pop(k))
            came[k] = swap(send, "dp", bit, f"sums_{k}")
            if k == (n_dp - 1) & -bit:
                waiting = (came[k], span // EXTRA)
            sums[k ^ bit].append((came[k], 0))
    last, stats = join(span, sums[top], [(stats, 0), waiting])
    came[top] = swap(last, "dp", top, f"sums_{top}")
    for bit in bits_of(n_dp)[:0:-1]:
        came[bit] = swap(after(add(sums[bit]), last), "dp", bit, f"sums_{bit}")

    scale = (own_rows * n_tensor * n_dp) ** (-0.5)
    terms = [*(x for x, _ in sums[0]), *(came[bit] for bit in bits_of(n_dp)[::-1])]
    return tuple(
        finish(
            [blocks[k] for k in range(n_dp)],
            terms,
            stats,
            first_out,
            second_out,
            grad_first,
            norm_gain,
            norm_bias,
            (w_up.shape, w_down.shape),
            scale,
        )
    )


def body(first_out, second_out, grad_first, grad_second, w_up, *rest):
    n_dp, n_tensor = lax.axis_size("dp"), lax.axis_size("tensor")
    powers = all(size > 1 and size & (size - 1) == 0 for size in (n_dp, n_tensor))
    few_tokens = first_out.shape[0] * n_tensor < w_up.shape[1]
    units, depth = w_up.shape[1] // n_dp, w_up.shape[0]
    fits = w_up.shape[1] % n_dp == 0 and units % depth == 0 and depth % 128 == 0
    fits = fits and first_out.shape[1] == 2 * units and n_dp > 2 and n_tensor > 2
    pick = gather_tokens_body if powers and few_tokens and fits else gather_weights_body
    return pick(first_out, second_out, grad_first, grad_second, w_up, *rest)


def solution(mesh):
    in_specs = (
        P(("groups", "tensor", "dp"), None),
        P(("groups", "tensor", "dp"), None),
        P(("groups", "tensor", "dp"), None),
        P(("groups", "tensor", "dp"), None),
        P("dp", "tensor"),
        P("tensor", "dp"),
        P(),
        P(),
    )
    out_specs = (
        P(("groups", "tensor", "dp"), None),
        P(("groups", "tensor", "dp"), None),
        P(("groups", "dp"), "tensor"),
        P(("groups", "tensor"), "dp"),
        P("groups", None),
    )
    return jax.shard_map(body, mesh=mesh, in_specs=in_specs, out_specs=out_specs, check_vma=False)
```

```python
import math

import jax
import jax.numpy as jnp
from jax import lax
from jax.experimental import pallas as pl
from jax.experimental.pallas import tpu as pltpu
from jax.sharding import PartitionSpec as P

epsilon = 1e-06
EXTRA = 16


def normalize(row_data, norm_gain, norm_bias):
    values = row_data.astype(jnp.float32)
    row_mean = jnp.mean(values, axis=-1, keepdims=True)
    centred = values - row_mean
    inv_std = lax.rsqrt(jnp.mean(centred * centred, axis=-1, keepdims=True) + epsilon)
    standard = centred * inv_std
    normed = (standard * norm_gain + norm_bias).astype(jnp.bfloat16)
    return (standard, inv_std, normed)


def contract_tokens(left_rows, right_rows):
    return lax.dot_general(
        left_rows, right_rows, (((0,), (0,)), ((), ())), preferred_element_type=jnp.float32
    )


def contract_last(left_rows, right_rows):
    return lax.dot_general(
        left_rows, right_rows, (((1,), (1,)), ((), ())), preferred_element_type=jnp.float32
    )


def finish_rows(branch, grad_normed, second_out, grad_first, first_out, norm_gain, norm_bias):
    standard, inv_std, _ = normalize(first_out, norm_gain, norm_bias)
    second_in = (second_out.astype(jnp.float32) - branch).astype(jnp.bfloat16)
    grad_std = grad_normed * norm_gain
    grad_rows = inv_std * (
        grad_std
        - jnp.mean(grad_std, axis=-1, keepdims=True)
        - standard * jnp.mean(grad_std * standard, axis=-1, keepdims=True)
    )
    return second_in, grad_first.astype(jnp.float32) + grad_rows


def gather_weights_body(
    first_out, second_out, grad_first, grad_second, w_up, w_down, norm_gain, norm_bias
):
    own_rows = first_out.shape[0]
    up_full = lax.all_gather(w_up, "dp", axis=0, tiled=True)
    down_full = lax.all_gather(w_down, "dp", axis=1, tiled=True)
    first_all = lax.all_gather(first_out, "tensor", axis=0, tiled=True)
    grad_all = lax.all_gather(grad_second, "tensor", axis=0, tiled=True)
    standard_all, _, normed = normalize(first_all, norm_gain, norm_bias)
    offset = lax.axis_index("tensor") * own_rows
    standard = lax.dynamic_slice_in_dim(standard_all, offset, own_rows, 0)
    preact = jnp.dot(normed, up_full, preferred_element_type=jnp.float32)
    hidden = jax.nn.gelu(preact).astype(jnp.bfloat16)
    branch = lax.psum_scatter(
        jnp.dot(hidden, down_full, preferred_element_type=jnp.float32).astype(jnp.bfloat16),
        "tensor",
        scatter_dimension=0,
        tiled=True,
    ).astype(jnp.float32)
    tokens = own_rows * lax.axis_size("tensor") * lax.axis_size("dp")
    grad_scale = tokens ** (-0.5)
    grad_down_part = contract_tokens(hidden, grad_all)
    grad_down = (
        lax.psum_scatter(
            grad_down_part.astype(jnp.bfloat16), "dp", scatter_dimension=1, tiled=True
        ).astype(jnp.float32)
        * grad_scale
    )
    grad_hidden = contract_last(grad_all, down_full)
    grad_pre = jax.vjp(jax.nn.gelu, preact)[1](grad_hidden)[0].astype(jnp.bfloat16)
    grad_up_part = contract_tokens(normed, grad_pre)
    grad_up = (
        lax.psum_scatter(
            grad_up_part.astype(jnp.bfloat16), "dp", scatter_dimension=0, tiled=True
        ).astype(jnp.float32)
        * grad_scale
    )
    grad_normed = lax.psum_scatter(
        contract_last(grad_pre, up_full).astype(jnp.bfloat16),
        "tensor",
        scatter_dimension=0,
        tiled=True,
    ).astype(jnp.float32)
    second_in, grad_first_in = finish_rows(
        branch, grad_normed, second_out, grad_first, first_out, norm_gain, norm_bias
    )
    local_stats = jnp.stack([jnp.sum(grad_normed * standard, axis=0), jnp.sum(grad_normed, axis=0)])
    grad_norm = lax.psum(local_stats, ("tensor", "dp")) * grad_scale
    return (second_in, grad_first_in, grad_up, grad_down, grad_norm)


def swap(values, axis, mask, scope):
    with jax.named_scope(scope):
        return lax.ppermute(values, axis, [(i, i ^ mask) for i in range(lax.axis_size(axis))])


def bits_of(size):
    return [1 << b for b in reversed(range(size.bit_length() - 1))]


def pack(first_out, grad_second, w_up, w_down, mates):
    n_dp, (own_rows, width) = lax.axis_size("dp"), first_out.shape
    depth, units = w_up.shape[0], w_up.shape[1] // n_dp
    strips, rows = units // depth, depth // mates

    def kernel(first_ref, grad_ref, up_ref, down_ref, own, *sends):
        place, mate = lax.axis_index("dp"), lax.rem(lax.axis_index("groups"), mates)
        own[:own_rows, :] = first_ref[...]
        own[own_rows:, :] = grad_ref[...]
        for k in range(1, n_dp):
            first = pl.multiple_of((place ^ k) * units, units)
            send = sends[k - 1]
            send[:, :units] = up_ref[pl.ds(pl.multiple_of(mate * rows, rows), rows), pl.ds(first, units)]
            for c in range(strips):
                row = pl.multiple_of(first + mate * (units // mates) + c * rows, rows)
                send[:, units + c * depth : units + (c + 1) * depth] = down_ref[pl.ds(row, rows), :]

    return pl.pallas_call(
        kernel,
        out_shape=[jax.ShapeDtypeStruct((2 * own_rows, width), w_up.dtype)]
        + [jax.ShapeDtypeStruct((rows, width), w_up.dtype)] * (n_dp - 1),
        in_specs=[pl.BlockSpec(memory_space=pltpu.VMEM)] * 4,
        out_specs=[pl.BlockSpec(memory_space=pltpu.VMEM)] * n_dp,
        cost_estimate=pl.CostEstimate(flops=0, bytes_accessed=8 * w_up.size, transcendentals=0),
        name="pack",
    )(first_out, grad_second, w_up, w_down)


def unpack(w_up, w_down, got, mates):
    n_dp = lax.axis_size("dp")
    depth, units = w_up.shape[0], w_up.shape[1] // n_dp
    strips = units // depth
    pieces = [piece for k in range(1, n_dp) for piece in got[k]]

    def kernel(own_up, own_down, *rest):
        left, (up_ref, down_ref, sem) = list(rest[:-3]), rest[-3:]
        place, mate = lax.axis_index("dp"), lax.rem(lax.axis_index("groups"), mates)
        loads = []

        def load(src, dst):
            loads.append(pltpu.make_async_copy(src, dst, sem.at[len(loads)]))
            loads[-1].start()

        mine = pl.ds(pl.multiple_of(place * units, units), units)
        rows = pl.ds(pl.multiple_of(place * depth, depth), depth)
        load(own_up.at[:, mine], up_ref.at[rows, :])
        load(own_down.at[mine, :], down_ref.at[:, rows])
        for k in range(1, n_dp):
            first = pl.multiple_of((place ^ k) * depth, depth)
            many = len(got[k])
            rows = depth // many
            for j in range(many):
                piece = left.pop(0)
                which = mate ^ j if many > 1 else 0
                row = pl.multiple_of(first + which * rows, rows)
                load(piece.at[:, pl.ds(0, units)], up_ref.at[pl.ds(row, rows), :])
                for c in range(strips):
                    row = pl.multiple_of(which * (units // many) + c * rows, rows)
                    load(
                        piece.at[:, pl.ds(units + c * depth, depth)],
                        down_ref.at[pl.ds(row, rows), pl.ds(first, depth)],
                    )
        for one in loads:
            one.wait()

    return pl.pallas_call(
        kernel,
        out_shape=[
            jax.ShapeDtypeStruct((depth * n_dp, units), w_up.dtype),
            jax.ShapeDtypeStruct((units, depth * n_dp), w_down.dtype),
        ],
        in_specs=[pl.BlockSpec(memory_space=pl.ANY)] * (2 + len(pieces)),
        out_specs=[pl.BlockSpec(memory_space=pltpu.VMEM)] * 2,
        scratch_shapes=[pltpu.SemaphoreType.DMA((2 + len(pieces) * (1 + strips),))],
        cost_estimate=pl.CostEstimate(flops=0, bytes_accessed=8 * w_up.size, transcendentals=0),
        name="unpack",
    )(w_up, w_down, *pieces)


def core(chunks, up, down, gain, bias):
    n_chunks, n, n_dp = len(chunks), len(chunks[0]), lax.axis_size("dp")
    (piece_rows, width), units = chunks[0][0].shape, up.shape[1]
    piece_rows //= 2
    depth = width // n_dp
    strips, pair = units // depth, 2 * piece_rows
    slope = (2.0 / math.pi) ** 0.5
    dtype = up.dtype

    def kernel(*refs):
        toks, refs = refs[: n_chunks * n], refs[n_chunks * n :]
        (up_hbm, down_hbm, gain_ref, bias_ref), refs = refs[:4], refs[4:]
        outs, blocks, stat_ref = refs[: 2 * n_chunks], refs[2 * n_chunks : 2 * n_chunks + n_dp], refs[2 * n_chunks + n_dp]
        scratch = refs[2 * n_chunks + n_dp + 1 :]
        tok, norm, hid, pre, part, block, up_ref, down_ref, total, in_sem, w_sem, out_sem, b_sem = scratch
        place = lax.axis_index("dp")
        reads, writes = [], []
        for i, ref in enumerate(toks):
            reads.append(pltpu.make_async_copy(ref, tok.at[i], in_sem.at[i]))
        loads = [
            pltpu.make_async_copy(up_hbm, up_ref, w_sem.at[0]),
            pltpu.make_async_copy(down_hbm, down_ref, w_sem.at[1]),
        ]
        for one in reads[:n] + loads:
            one.start()
        for one in reads[n:]:
            one.start()
        total[...] = jnp.zeros_like(total)
        for i in range(n_chunks):
            for one in reads[i * n : (i + 1) * n] + (loads if i == 0 else []):
                one.wait()

            @pl.loop(0, n // 2)
            def _(t):
                at = i * n + 2 * t
                span = pl.ds(pl.multiple_of(at * piece_rows, pair), pair)
                values = tok[pl.ds(at, 2), :piece_rows].reshape(pair, width).astype(jnp.float32)
                centred = values - jnp.mean(values, axis=-1, keepdims=True)
                inv_std = lax.rsqrt(jnp.mean(centred * centred, axis=-1, keepdims=True) + epsilon)
                standard = centred * inv_std
                normed = (standard * gain_ref[...] + bias_ref[...]).astype(dtype)
                norm[span, :] = normed
                x = jnp.dot(normed, up_ref[...], preferred_element_type=jnp.float32)
                gate = jnp.tanh(slope * (x + 0.044715 * (x * x * x)))
                half = 0.5 + 0.5 * gate
                hidden = (x * half).astype(dtype)
                hid[span, :] = hidden
                rise = half + (0.5 * slope) * x * (1.0 - gate * gate) * (1.0 + (3 * 0.044715) * (x * x))
                grads = tok[pl.ds(at, 2), piece_rows:].reshape(pair, width)
                grad_pre = (contract_last(grads, down_ref[...]) * rise).astype(dtype)
                pre[span, :] = grad_pre
                branch = jnp.dot(hidden, down_ref[...], preferred_element_type=jnp.float32)
                grad_normed = contract_last(grad_pre, up_ref[...])
                total[0:1, :] += jnp.sum(grad_normed * standard, axis=0, keepdims=True)
                total[1:2, :] += jnp.sum(grad_normed, axis=0, keepdims=True)
                row = pl.multiple_of(t * pair, pair)
                for odd in range(2):
                    own = slice(odd * piece_rows, (odd + 1) * piece_rows)
                    part[2 * i + odd, pl.ds(row, piece_rows), :] = branch[own].astype(dtype)
                    part[2 * i + odd, pl.ds(row + piece_rows, piece_rows), :] = grad_normed[own].astype(dtype)

            for odd in (1, 0):
                at = 2 * i + odd
                out = outs[at].at[pl.ds(0, half[0]), :]
                writes.append(pltpu.make_async_copy(part.at[at], out, out_sem.at[at]))
                writes[-1].start()
        stat_ref[...] = jnp.zeros_like(stat_ref)
        stat_ref[0:2, :] = total[0:2, :].astype(dtype)
        stat_ref[2:4, :] = (total[0:2, :] - stat_ref[0:2, :].astype(jnp.float32)).astype(dtype)
        tail = outs[1].at[pl.ds(half[0], EXTRA), :]
        writes.append(pltpu.make_async_copy(stat_ref, tail, out_sem.at[2 * n_chunks]))
        writes[-1].start()
        top = bits_of(n_dp)[0]
        for k in sorted(range(n_dp), key=lambda k: (k < top, k)):
            columns = pl.ds(pl.multiple_of((place ^ k) * depth, depth), depth)
            block[k, :depth, :] = contract_tokens(norm[:, columns], pre[...]).astype(dtype)
            grads = tok[:, piece_rows:, columns].reshape(n_chunks * n * piece_rows, depth)
            down_block = contract_tokens(hid[...], grads).astype(dtype)
            for c in range(strips):
                block[k, depth:, c * depth : (c + 1) * depth] = down_block[c * depth : (c + 1) * depth]
            writes.append(pltpu.make_async_copy(block.at[k], blocks[k], b_sem.at[k]))
            writes[-1].start()
        for one in writes:
            one.wait()

    rows = n_chunks * n * piece_rows
    half = (n // 2 * pair, width)
    far = pl.BlockSpec(memory_space=pl.ANY)
    near = pl.BlockSpec(memory_space=pltpu.VMEM)
    out = pl.pallas_call(
        kernel,
        out_shape=[
            jax.ShapeDtypeStruct((half[0] + (EXTRA if at == 1 else 0), width), dtype) for at in range(2 * n_chunks)
        ]
        + [jax.ShapeDtypeStruct((2 * depth, units), dtype)] * n_dp
        + [jax.ShapeDtypeStruct((EXTRA, width), dtype)],
        in_specs=[far] * (n_chunks * n + 2) + [near] * 2,
        out_specs=[far] * (2 * n_chunks + n_dp) + [near],
        scratch_shapes=[
            pltpu.VMEM((n_chunks * n, pair, width), dtype),
            pltpu.VMEM((rows, width), dtype),
            pltpu.VMEM((rows, units), dtype),
            pltpu.VMEM((rows, units), dtype),
            pltpu.VMEM((2 * n_chunks, *half), dtype),
            pltpu.VMEM((n_dp, 2 * depth, units), dtype),
            pltpu.VMEM((width, units), dtype),
            pltpu.VMEM((units, width), dtype),
            pltpu.VMEM((EXTRA, width), jnp.float32),
            pltpu.SemaphoreType.DMA((n_chunks * n,)),
            pltpu.SemaphoreType.DMA((2,)),
            pltpu.SemaphoreType.DMA((2 * n_chunks + 1,)),
            pltpu.SemaphoreType.DMA((n_dp,)),
        ],
        compiler_params=pltpu.CompilerParams(vmem_limit_bytes=56 * 1024 * 1024),
        cost_estimate=pl.CostEstimate(
            flops=10 * rows * width * units,
            bytes_accessed=8 * rows * width + 8 * width * units,
            transcendentals=rows * units,
        ),
        name="core",
    )(
        *[piece for chunk in chunks for piece in chunk],
        up,
        down,
        gain.reshape(1, width),
        bias.reshape(1, width),
    )
    halves = [out[2 * i : 2 * i + 2] for i in range(n_chunks)]
    return halves, list(out[2 * n_chunks : -1]), out[-1]


def finish(blocks, terms, stats, first_out, second_out, grad_first, gain, bias, w_shapes, scale):
    (rows, width), n_dp = first_out.shape, len(blocks)
    depth, units = w_shapes[0][0], w_shapes[0][1] // n_dp
    strips, n_terms = units // depth, len(terms)

    def kernel(*refs):
        parts, adds, (stat_ref, first_ref, second_ref, grad_ref, gain_ref, bias_ref), outs = (
            refs[:n_dp],
            refs[n_dp : n_dp + n_terms],
            refs[n_dp + n_terms : n_dp + n_terms + 6],
            refs[n_dp + n_terms + 6 :],
        )
        second_in, grad_in, up_out, down_out, norm_out = outs
        place = lax.axis_index("dp")
        for k in range(n_dp):
            first = pl.multiple_of((place ^ k) * units, units)
            up_out[:, pl.ds(first, units)] = parts[k][:depth, :].astype(jnp.float32) * scale
            for c in range(strips):
                block = parts[k][depth : 2 * depth, c * depth : (c + 1) * depth]
                row = pl.multiple_of(first + c * depth, depth)
                down_out[pl.ds(row, depth), :] = block.astype(jnp.float32) * scale
        total = sum(ref[: 2 * rows, :].astype(jnp.float32) for ref in adds)
        second_in[...] = (second_ref[...].astype(jnp.float32) - total[:rows]).astype(second_in.dtype)
        values = first_ref[...].astype(jnp.float32)
        centred = values - jnp.mean(values, axis=-1, keepdims=True)
        inv_std = lax.rsqrt(jnp.mean(centred * centred, axis=-1, keepdims=True) + epsilon)
        standard = centred * inv_std
        grad_std = total[rows:] * gain_ref[...]
        grad_rows = inv_std * (
            grad_std
            - jnp.mean(grad_std, axis=-1, keepdims=True)
            - standard * jnp.mean(grad_std * standard, axis=-1, keepdims=True)
        )
        grad_in[...] = grad_ref[...].astype(jnp.float32) + grad_rows
        one, two = stat_ref[...].astype(jnp.float32), adds[-1][2 * rows :, :].astype(jnp.float32)
        norm_out[...] = ((one[0:2] + one[2:4]) + (two[0:2] + two[2:4])) * scale

    def whole(x):
        return pl.BlockSpec(x.shape, lambda i: (0, 0))

    arrays = [*blocks, *terms, stats, first_out, second_out, grad_first, gain.reshape(1, width), bias.reshape(1, width)]
    in_specs = [whole(x) for x in arrays]
    for i in range(n_terms - 1):
        in_specs[n_dp + i] = pl.BlockSpec((2 * rows, width), lambda i: (0, 0))
    out_shape = [
        jax.ShapeDtypeStruct((rows, width), second_out.dtype),
        jax.ShapeDtypeStruct((rows, width), jnp.float32),
        jax.ShapeDtypeStruct(w_shapes[0], jnp.float32),
        jax.ShapeDtypeStruct(w_shapes[1], jnp.float32),
        jax.ShapeDtypeStruct((2, width), jnp.float32),
    ]
    return pl.pallas_call(
        kernel,
        out_shape=out_shape,
        grid=(1,),
        in_specs=in_specs,
        out_specs=[whole(x) for x in out_shape],
        compiler_params=pltpu.CompilerParams(vmem_limit_bytes=48 * 1024 * 1024),
        cost_estimate=pl.CostEstimate(
            flops=0, bytes_accessed=12 * w_shapes[0][0] * w_shapes[0][1], transcendentals=0
        ),
        name="finish",
    )(*arrays)


def join(rows, terms, stats=()):
    width = terms[0][0].shape[1]
    arrays = [*terms, *stats]
    n_terms = len(terms)

    def kernel(*refs):
        out = refs[len(arrays)]
        total = sum(ref[...].astype(jnp.float32) for ref in refs[:n_terms])
        out[:rows, :] = total.astype(out.dtype)
        if stats:
            one, two = (ref[...].astype(jnp.float32) for ref in refs[n_terms : n_terms + 2])
            both = (one[0:2] + one[2:4]) + (two[0:2] + two[2:4])
            tail = refs[-1]
            tail[...] = jnp.zeros_like(tail)
            tail[0:2, :] = both.astype(tail.dtype)
            tail[2:4, :] = (both - tail[0:2, :].astype(jnp.float32)).astype(tail.dtype)
            out[rows:, :] = tail[...]

    def spec(height, place):
        return pl.BlockSpec((height, width), lambda i: (place, 0))

    out_shape = [jax.ShapeDtypeStruct((rows + (EXTRA if stats else 0), width), jnp.bfloat16)]
    out_specs = [spec(out_shape[0].shape[0], 0)]
    if stats:
        out_shape.append(jax.ShapeDtypeStruct((EXTRA, width), jnp.bfloat16))
        out_specs.append(spec(EXTRA, 0))
    out = pl.pallas_call(
        kernel,
        out_shape=out_shape,
        grid=(1,),
        in_specs=[spec(rows, place) for _, place in terms] + [spec(EXTRA, place) for _, place in stats],
        out_specs=out_specs,
        cost_estimate=pl.CostEstimate(
            flops=0, bytes_accessed=2 * (len(terms) + 1) * rows * width, transcendentals=0
        ),
        name="join",
    )(*(x for x, _ in arrays))
    return out if stats else out[0]


def after(values, *others):
    return lax.optimization_barrier((values, *others))[0]


def gather_tokens_body(
    first_out, second_out, grad_first, grad_second, w_up, w_down, norm_gain, norm_bias
):
    n_dp, n_tensor, n_groups = (lax.axis_size(axis) for axis in ("dp", "tensor", "groups"))
    own_rows, depth = first_out.shape[0], w_up.shape[0]
    units = w_up.shape[1] // n_dp
    mates = 2 if n_groups % 2 == 0 else 1
    place = lax.axis_index("dp")
    top = bits_of(n_dp)[0]

    high, others = bits_of(n_tensor)[0], bits_of(n_tensor)[1:]
    own, *sends = pack(first_out, grad_second, w_up, w_down, mates)
    tokens, chunks, got, crossed = {0: own}, {}, {}, {}

    def tokens_dp(k, *first):
        tokens[k] = swap(after(tokens[k & (k - 1)], *first), "dp", k & -k, f"tokens_{k}")

    def tokens_tensor(k, *first):
        start = after(tokens[k], *first)
        chunks[k] = {0: tokens[k], high: swap(start, "tensor", high, f"tokens_{k}_{high}")}

    def tokens_rest(k, *first):
        for bit in others:
            for j in list(chunks[k]):
                piece = chunks[k][j] if j else after(chunks[k][j], *first)
                chunks[k][j | bit] = swap(piece, "tensor", bit, f"tokens_{k}_{j | bit}")

    def weights_groups(k, *first):
        if mates == 2:
            crossed[k] = swap(after(got[k], *first), "groups", 1, f"weights_{k}")

    def weights_dp(k, *first):
        got[k] = swap(after(sends[k - 1], *first), "dp", k, f"weights_{k}")

    for bit in reversed(bits_of(n_dp)):
        tokens_dp(bit)
    tokens_tensor(0)
    tokens_rest(0)
    tokens_tensor(1, tokens[top], chunks[0][high])
    stage = [*tokens.values(), *chunks[0].values()]
    for k in range(2, n_dp):
        if k & (k - 1):
            tokens_dp(k, *stage)
        if k == top:
            weights_dp(1, *stage)
        weights_dp(k, *stage, *([got[top]] if top in got else []))
    for k in range(2, n_dp):
        tokens_rest(k - 1)
        stage = [got[top]]
        if k & (k - 1):
            for bit in reversed(bits_of(n_dp)):
                if bit not in crossed:
                    weights_groups(bit)
            stage = [tokens[k], *got.values(), *crossed.values(), *chunks[k - 2].values()]
        tokens_tensor(k, *stage, chunks[k - 1][high])
    for k in range(1, n_dp):
        if k not in crossed:
            weights_groups(k)
    got = {k: [got[k]] + ([crossed[k]] if k in crossed else []) for k in got}
    up, down = unpack(w_up, w_down, got, mates)
    tokens_rest(n_dp - 1, up)


    order = sorted(chunks, reverse=True)
    halves, blocks, stats = core(
        [[chunks[k][j] for j in range(n_tensor)] for k in order], up, down, norm_gain, norm_bias
    )
    blocks = dict(enumerate(blocks))
    blocks[top] = swap(blocks[top], "dp", top, f"grads_{top}")


    def add(terms):
        spans = (x[place * span : (place + 1) * span].astype(jnp.float32) for x, place in terms)
        return sum(spans).astype(jnp.bfloat16)

    span, first = 2 * own_rows, order[0]
    sums, came, behind = {}, {}, ()
    for k, (even, odd) in zip(order, halves, strict=True):
        other = swap(odd, "tensor", 1, f"sums_{k}_1")
        if k == first:
            waiting = (other, even.shape[0] // EXTRA)
        parts = {2 * j: [(x, j) for x in (even, other)] for j in range(n_tensor // 2)}
        for bit in reversed(bits_of(n_tensor)[:-1]):
            for j in [j for j in parts if j & bit]:
                carries = k == first and j == bit
                if carries:
                    send, stats = join(span, parts.pop(j), [(stats, 0), waiting])
                else:
                    send = add(parts.pop(j))
                if k in (0, top):
                    behind += (blocks[top if k else n_dp - 1],)
                other = swap(after(send, *behind), "tensor", bit, f"sums_{k}_{j}")
                if carries:
                    waiting = (other, span // EXTRA)
                parts[j ^ bit].append((other, 0))
                behind = (other,)
        sums[k] = parts[0]
        if k == first:
            send, stats = join(span, sums.pop(k), [(stats, 0), waiting])
            came[k] = swap(send, "dp", k & -k, f"sums_{k}")
            waiting = (came[k], span // EXTRA)
            for i in range(top + 1, n_dp):
                blocks[i] = swap(after(blocks[i], blocks[top], send), "dp", i, f"grads_{i}")
    sums[first & (first - 1)].append((came[first], 0))
    for bit in bits_of(n_dp)[::-1]:
        for k in [k for k in order if k & bit and k in sums and k != bit]:
            carries = k == (n_dp - 1) & -bit
            if carries:
                send, stats = join(span, sums.pop(k), [(stats, 0), waiting])
            else:
                send = add(sums.pop(k))
            came[k] = swap(send, "dp", bit, f"sums_{k}")
            if carries:
                waiting = (came[k], span // EXTRA)
            sums[k ^ bit].append((came[k], 0))
    last, stats = join(span, sums[top], [(stats, 0), waiting])
    came[top] = swap(last, "dp", top, f"sums_{top}")
    for k in range(1, top):
        blocks[k] = swap(after(blocks[k], last), "dp", k, f"grads_{k}")
    for bit in bits_of(n_dp)[:0:-1]:
        came[bit] = swap(after(add(sums[bit]), last), "dp", bit, f"sums_{bit}")

    scale = (own_rows * n_tensor * n_dp) ** (-0.5)
    terms = [*(x for x, _ in sums[0]), *(came[bit] for bit in bits_of(n_dp)[::-1])]
    return tuple(
        finish(
            [blocks[k] for k in range(n_dp)],
            terms,
            stats,
            first_out,
            second_out,
            grad_first,
            norm_gain,
            norm_bias,
            (w_up.shape, w_down.shape),
            scale,
        )
    )


def body(first_out, second_out, grad_first, grad_second, w_up, *rest):
    n_dp, n_tensor = lax.axis_size("dp"), lax.axis_size("tensor")
    powers = all(size > 1 and size & (size - 1) == 0 for size in (n_dp, n_tensor))
    few_tokens = first_out.shape[0] * n_tensor < w_up.shape[1]
    units, depth = w_up.shape[1] // n_dp, w_up.shape[0]
    fits = w_up.shape[1] % n_dp == 0 and units % depth == 0 and depth % 128 == 0
    fits = fits and first_out.shape[1] == 2 * units and n_dp > 2 and n_tensor > 2
    pick = gather_tokens_body if powers and few_tokens and fits else gather_weights_body
    return pick(first_out, second_out, grad_first, grad_second, w_up, *rest)


def solution(mesh):
    in_specs = (
        P(("groups", "tensor", "dp"), None),
        P(("groups", "tensor", "dp"), None),
        P(("groups", "tensor", "dp"), None),
        P(("groups", "tensor", "dp"), None),
        P("dp", "tensor"),
        P("tensor", "dp"),
        P(),
        P(),
    )
    out_specs = (
        P(("groups", "tensor", "dp"), None),
        P(("groups", "tensor", "dp"), None),
        P(("groups", "dp"), "tensor"),
        P(("groups", "tensor"), "dp"),
        P("groups", None),
    )
    return jax.shard_map(body, mesh=mesh, in_specs=in_specs, out_specs=out_specs, check_vma=False)
```

```python
import math

import jax
import jax.numpy as jnp
from jax import lax
from jax.experimental import pallas as pl
from jax.experimental.pallas import tpu as pltpu
from jax.sharding import PartitionSpec as P

epsilon = 1e-06


def normalize(row_data, norm_gain, norm_bias):
    values = row_data.astype(jnp.float32)
    row_mean = jnp.mean(values, axis=-1, keepdims=True)
    centred = values - row_mean
    inv_std = lax.rsqrt(jnp.mean(centred * centred, axis=-1, keepdims=True) + epsilon)
    standard = centred * inv_std
    normed = (standard * norm_gain + norm_bias).astype(jnp.bfloat16)
    return (standard, inv_std, normed)


def contract_tokens(left_rows, right_rows):
    return lax.dot_general(
        left_rows, right_rows, (((0,), (0,)), ((), ())), preferred_element_type=jnp.float32
    )


def contract_last(left_rows, right_rows):
    return lax.dot_general(
        left_rows, right_rows, (((1,), (1,)), ((), ())), preferred_element_type=jnp.float32
    )


def finish_rows(branch, grad_normed, second_out, grad_first, first_out, norm_gain, norm_bias):
    standard, inv_std, _ = normalize(first_out, norm_gain, norm_bias)
    second_in = (second_out.astype(jnp.float32) - branch).astype(jnp.bfloat16)
    grad_std = grad_normed * norm_gain
    grad_rows = inv_std * (
        grad_std
        - jnp.mean(grad_std, axis=-1, keepdims=True)
        - standard * jnp.mean(grad_std * standard, axis=-1, keepdims=True)
    )
    return second_in, grad_first.astype(jnp.float32) + grad_rows


def gather_weights_body(
    first_out, second_out, grad_first, grad_second, w_up, w_down, norm_gain, norm_bias
):
    own_rows = first_out.shape[0]
    up_full = lax.all_gather(w_up, "dp", axis=0, tiled=True)
    down_full = lax.all_gather(w_down, "dp", axis=1, tiled=True)
    first_all = lax.all_gather(first_out, "tensor", axis=0, tiled=True)
    grad_all = lax.all_gather(grad_second, "tensor", axis=0, tiled=True)
    standard_all, _, normed = normalize(first_all, norm_gain, norm_bias)
    offset = lax.axis_index("tensor") * own_rows
    standard = lax.dynamic_slice_in_dim(standard_all, offset, own_rows, 0)
    preact = jnp.dot(normed, up_full, preferred_element_type=jnp.float32)
    hidden = jax.nn.gelu(preact).astype(jnp.bfloat16)
    branch = lax.psum_scatter(
        jnp.dot(hidden, down_full, preferred_element_type=jnp.float32).astype(jnp.bfloat16),
        "tensor",
        scatter_dimension=0,
        tiled=True,
    ).astype(jnp.float32)
    tokens = own_rows * lax.axis_size("tensor") * lax.axis_size("dp")
    grad_scale = tokens ** (-0.5)
    grad_down_part = contract_tokens(hidden, grad_all)
    grad_down = (
        lax.psum_scatter(
            grad_down_part.astype(jnp.bfloat16), "dp", scatter_dimension=1, tiled=True
        ).astype(jnp.float32)
        * grad_scale
    )
    grad_hidden = contract_last(grad_all, down_full)
    grad_pre = jax.vjp(jax.nn.gelu, preact)[1](grad_hidden)[0].astype(jnp.bfloat16)
    grad_up_part = contract_tokens(normed, grad_pre)
    grad_up = (
        lax.psum_scatter(
            grad_up_part.astype(jnp.bfloat16), "dp", scatter_dimension=0, tiled=True
        ).astype(jnp.float32)
        * grad_scale
    )
    grad_normed = lax.psum_scatter(
        contract_last(grad_pre, up_full).astype(jnp.bfloat16),
        "tensor",
        scatter_dimension=0,
        tiled=True,
    ).astype(jnp.float32)
    second_in, grad_first_in = finish_rows(
        branch, grad_normed, second_out, grad_first, first_out, norm_gain, norm_bias
    )
    local_stats = jnp.stack([jnp.sum(grad_normed * standard, axis=0), jnp.sum(grad_normed, axis=0)])
    grad_norm = lax.psum(local_stats, ("tensor", "dp")) * grad_scale
    return (second_in, grad_first_in, grad_up, grad_down, grad_norm)


def swap(values, axis, mask, scope):
    with jax.named_scope(scope):
        return lax.ppermute(values, axis, [(i, i ^ mask) for i in range(lax.axis_size(axis))])


def bits_of(size):
    return [1 << b for b in reversed(range(size.bit_length() - 1))]


def pack(first_out, grad_second, w_up, w_down, mates):
    n_dp, (own_rows, width) = lax.axis_size("dp"), first_out.shape
    depth, units = w_up.shape[0], w_up.shape[1] // n_dp
    strips, rows = units // depth, depth // mates

    def kernel(first_ref, grad_ref, up_ref, down_ref, own, *sends):
        place, mate = lax.axis_index("dp"), lax.rem(lax.axis_index("groups"), mates)
        own[:own_rows, :] = first_ref[...]
        own[own_rows:, :] = grad_ref[...]
        for k in range(1, n_dp):
            first = pl.multiple_of((place ^ k) * units, units)
            send = sends[k - 1]
            send[:, :units] = up_ref[pl.ds(pl.multiple_of(mate * rows, rows), rows), pl.ds(first, units)]
            for c in range(strips):
                row = pl.multiple_of(first + mate * (units // mates) + c * rows, rows)
                send[:, units + c * depth : units + (c + 1) * depth] = down_ref[pl.ds(row, rows), :]

    return pl.pallas_call(
        kernel,
        out_shape=[jax.ShapeDtypeStruct((2 * own_rows, width), w_up.dtype)]
        + [jax.ShapeDtypeStruct((rows, width), w_up.dtype)] * (n_dp - 1),
        in_specs=[pl.BlockSpec(memory_space=pltpu.VMEM)] * 4,
        out_specs=[pl.BlockSpec(memory_space=pltpu.VMEM)] * n_dp,
        cost_estimate=pl.CostEstimate(flops=0, bytes_accessed=8 * w_up.size, transcendentals=0),
        name="pack",
    )(first_out, grad_second, w_up, w_down)


def core(chunks, w_up, w_down, got, mates, gain, bias):
    n_chunks, n, n_dp = len(chunks), len(chunks[0]), lax.axis_size("dp")
    (piece_rows, width), units = chunks[0][0].shape, w_up.shape[1] // n_dp
    piece_rows //= 2
    depth = width // n_dp
    strips, pair = units // depth, 2 * piece_rows
    slope = (2.0 / math.pi) ** 0.5
    dtype = w_up.dtype
    pieces_of_weights = [piece for k in range(1, n_dp) for piece in got[k]]
    n_got = len(pieces_of_weights)

    def kernel(*refs):
        toks, refs = refs[: n_chunks * n], refs[n_chunks * n :]
        (own_up, own_down), weights, (gain_ref, bias_ref), refs = (
            refs[:2],
            list(refs[2 : 2 + n_got]),
            refs[2 + n_got : 4 + n_got],
            refs[4 + n_got :],
        )
        outs, blocks, stat_ref = refs[: 2 * n_chunks], refs[2 * n_chunks : 2 * n_chunks + n_dp], refs[2 * n_chunks + n_dp]
        tok, norm, hid, pre, part, block, up_ref, down_ref, in_sem, w_sem, out_sem, b_sem = refs[2 * n_chunks + n_dp + 1 :]
        place, mate = lax.axis_index("dp"), lax.rem(lax.axis_index("groups"), mates)
        reads, loads, writes = [], [], []

        def load(src, dst):
            loads.append(pltpu.make_async_copy(src, dst, w_sem.at[len(loads)]))
            loads[-1].start()

        for i, ref in enumerate(toks):
            reads.append(pltpu.make_async_copy(ref, tok.at[i], in_sem.at[i]))
            if i < n:
                reads[-1].start()
        mine = pl.ds(pl.multiple_of(place * units, units), units)
        rows = pl.ds(pl.multiple_of(place * depth, depth), depth)
        load(own_up.at[:, mine], up_ref.at[rows, :])
        load(own_down.at[mine, :], down_ref.at[:, rows])
        for k in range(1, n_dp):
            first = pl.multiple_of((place ^ k) * depth, depth)
            many = len(got[k])
            rows = depth // many
            for j in range(many):
                piece = weights.pop(0)
                which = mate ^ j if many > 1 else 0
                row = pl.multiple_of(first + which * rows, rows)
                load(piece.at[:, pl.ds(0, units)], up_ref.at[pl.ds(row, rows), :])
                for c in range(strips):
                    row = pl.multiple_of(which * (units // many) + c * rows, rows)
                    load(
                        piece.at[:, pl.ds(units + c * depth, depth)],
                        down_ref.at[pl.ds(row, rows), pl.ds(first, depth)],
                    )
        for one in reads[n:]:
            one.start()
        stat_ref[...] = jnp.zeros_like(stat_ref)
        for i in range(n_chunks):
            for one in reads[i * n : (i + 1) * n] + (loads if i == 0 else []):
                one.wait()

            @pl.loop(0, n // 2)
            def _(t):
                at = i * n + 2 * t
                span = pl.ds(pl.multiple_of(at * piece_rows, pair), pair)
                values = tok[pl.ds(at, 2), :piece_rows].reshape(pair, width).astype(jnp.float32)
                centred = values - jnp.mean(values, axis=-1, keepdims=True)
                inv_std = lax.rsqrt(jnp.mean(centred * centred, axis=-1, keepdims=True) + epsilon)
                standard = centred * inv_std
                normed = (standard * gain_ref[...] + bias_ref[...]).astype(dtype)
                norm[span, :] = normed
                x = jnp.dot(normed, up_ref[...], preferred_element_type=jnp.float32)
                gate = jnp.tanh(slope * (x + 0.044715 * (x * x * x)))
                half = 0.5 + 0.5 * gate
                hidden = (x * half).astype(dtype)
                hid[span, :] = hidden
                rise = half + (0.5 * slope) * x * (1.0 - gate * gate) * (1.0 + (3 * 0.044715) * (x * x))
                grads = tok[pl.ds(at, 2), piece_rows:].reshape(pair, width)
                grad_pre = (contract_last(grads, down_ref[...]) * rise).astype(dtype)
                pre[span, :] = grad_pre
                branch = jnp.dot(hidden, down_ref[...], preferred_element_type=jnp.float32)
                grad_normed = contract_last(grad_pre, up_ref[...])
                stat_ref[0:1, :] += jnp.sum(grad_normed * standard, axis=0, keepdims=True)
                stat_ref[1:2, :] += jnp.sum(grad_normed, axis=0, keepdims=True)
                row = pl.multiple_of(t * pair, pair)
                for odd in range(2):
                    own = slice(odd * piece_rows, (odd + 1) * piece_rows)
                    part[2 * i + odd, pl.ds(row, piece_rows), :] = branch[own].astype(dtype)
                    part[2 * i + odd, pl.ds(row + piece_rows, piece_rows), :] = grad_normed[own].astype(dtype)

            for odd in (1, 0):
                at = 2 * i + odd
                writes.append(pltpu.make_async_copy(part.at[at], outs[at], out_sem.at[at]))
                writes[-1].start()
        top = bits_of(n_dp)[0]
        for k in sorted(range(n_dp), key=lambda k: (k < top, k)):
            columns = pl.ds(pl.multiple_of((place ^ k) * depth, depth), depth)
            block[k, :depth, :] = contract_tokens(norm[:, columns], pre[...]).astype(dtype)
            grads = tok[:, piece_rows:, columns].reshape(n_chunks * n * piece_rows, depth)
            down_block = contract_tokens(hid[...], grads).astype(dtype)
            for c in range(strips):
                block[k, depth:, c * depth : (c + 1) * depth] = down_block[c * depth : (c + 1) * depth]
            writes.append(pltpu.make_async_copy(block.at[k], blocks[k], b_sem.at[k]))
            writes[-1].start()
        for one in writes:
            one.wait()

    rows = n_chunks * n * piece_rows
    half = (n // 2 * pair, width)
    far = pl.BlockSpec(memory_space=pl.ANY)
    near = pl.BlockSpec(memory_space=pltpu.VMEM)
    out = pl.pallas_call(
        kernel,
        out_shape=[jax.ShapeDtypeStruct(half, dtype)] * (2 * n_chunks)
        + [jax.ShapeDtypeStruct((2 * depth, units), dtype)] * n_dp
        + [jax.ShapeDtypeStruct((2, width), jnp.float32)],
        in_specs=[far] * (n_chunks * n + 2 + n_got) + [near] * 2,
        out_specs=[far] * (2 * n_chunks + n_dp) + [near],
        scratch_shapes=[
            pltpu.VMEM((n_chunks * n, pair, width), dtype),
            pltpu.VMEM((rows, width), dtype),
            pltpu.VMEM((rows, units), dtype),
            pltpu.VMEM((rows, units), dtype),
            pltpu.VMEM((2 * n_chunks, *half), dtype),
            pltpu.VMEM((n_dp, 2 * depth, units), dtype),
            pltpu.VMEM((width, units), dtype),
            pltpu.VMEM((units, width), dtype),
            pltpu.SemaphoreType.DMA((n_chunks * n,)),
            pltpu.SemaphoreType.DMA((2 + n_got * (1 + strips),)),
            pltpu.SemaphoreType.DMA((2 * n_chunks,)),
            pltpu.SemaphoreType.DMA((n_dp,)),
        ],
        compiler_params=pltpu.CompilerParams(vmem_limit_bytes=56 * 1024 * 1024),
        cost_estimate=pl.CostEstimate(
            flops=10 * rows * width * units,
            bytes_accessed=8 * rows * width + 8 * width * units,
            transcendentals=rows * units,
        ),
        name="core",
    )(
        *[piece for chunk in chunks for piece in chunk],
        w_up,
        w_down,
        *pieces_of_weights,
        gain.reshape(1, width),
        bias.reshape(1, width),
    )
    halves = [out[2 * i : 2 * i + 2] for i in range(n_chunks)]
    return halves, list(out[2 * n_chunks : -1]), out[-1]


def finish(blocks, terms, own_stats, first_out, second_out, grad_first, gain, bias, w_shapes, scale):
    (rows, width), n_dp = first_out.shape, len(blocks)
    depth, units = w_shapes[0][0], w_shapes[0][1] // n_dp
    strips, top, n_terms = units // depth, bits_of(n_dp)[0], len(terms)

    def kernel(*refs):
        parts, adds, (stat_ref, first_ref, second_ref, grad_ref, gain_ref, bias_ref), outs = (
            refs[:n_dp],
            refs[n_dp : n_dp + n_terms],
            refs[n_dp + n_terms : n_dp + n_terms + 6],
            refs[n_dp + n_terms + 6 :],
        )
        second_in, grad_in, up_out, down_out, norm_out = outs
        place = lax.axis_index("dp")
        for k in range(n_dp):
            first = pl.multiple_of((place ^ k) * units, units)
            up_out[:, pl.ds(first, units)] = parts[k][:depth, :].astype(jnp.float32) * scale
            for c in range(strips):
                block = parts[k][depth : 2 * depth, c * depth : (c + 1) * depth]
                row = pl.multiple_of(first + c * depth, depth)
                down_out[pl.ds(row, depth), :] = block.astype(jnp.float32) * scale
        total = sum(ref[: 2 * rows, :].astype(jnp.float32) for ref in adds)
        second_in[...] = (second_ref[...].astype(jnp.float32) - total[:rows]).astype(second_in.dtype)
        values = first_ref[...].astype(jnp.float32)
        centred = values - jnp.mean(values, axis=-1, keepdims=True)
        inv_std = lax.rsqrt(jnp.mean(centred * centred, axis=-1, keepdims=True) + epsilon)
        standard = centred * inv_std
        grad_std = total[rows:] * gain_ref[...]
        grad_rows = inv_std * (
            grad_std
            - jnp.mean(grad_std, axis=-1, keepdims=True)
            - standard * jnp.mean(grad_std * standard, axis=-1, keepdims=True)
        )
        grad_in[...] = grad_ref[...].astype(jnp.float32) + grad_rows
        stats = []
        for k in range(n_dp):
            if k == 0:
                one = stat_ref[...].astype(jnp.float32)
            elif k == top:
                one = adds[-1][2 * rows :, :].astype(jnp.float32)[:2]
            else:
                tail = parts[k][2 * depth :, :].astype(jnp.float32)
                per = width // units
                one = jnp.concatenate(
                    [
                        jnp.concatenate([tail[i * per + j : i * per + j + 1] for j in range(per)], axis=1)
                        for i in range(2)
                    ],
                    axis=0,
                )
            stats.append(one)
        while len(stats) > 1:
            stats = [one + two for one, two in zip(stats[0::2], stats[1::2], strict=True)]
        norm_out[...] = stats[0] * scale

    def whole(x):
        return pl.BlockSpec(x.shape, lambda i: (0, 0))

    arrays = [*blocks, *terms, own_stats, first_out, second_out, grad_first, gain.reshape(1, width), bias.reshape(1, width)]
    in_specs = [whole(x) for x in arrays]
    for i in range(n_terms - 1):
        in_specs[n_dp + i] = pl.BlockSpec((2 * rows, width), lambda i: (0, 0))
    out_shape = [
        jax.ShapeDtypeStruct((rows, width), second_out.dtype),
        jax.ShapeDtypeStruct((rows, width), jnp.float32),
        jax.ShapeDtypeStruct(w_shapes[0], jnp.float32),
        jax.ShapeDtypeStruct(w_shapes[1], jnp.float32),
        jax.ShapeDtypeStruct((2, width), jnp.float32),
    ]
    return pl.pallas_call(
        kernel,
        out_shape=out_shape,
        grid=(1,),
        in_specs=in_specs,
        out_specs=[whole(x) for x in out_shape],
        compiler_params=pltpu.CompilerParams(vmem_limit_bytes=48 * 1024 * 1024),
        cost_estimate=pl.CostEstimate(
            flops=0, bytes_accessed=12 * w_shapes[0][0] * w_shapes[0][1], transcendentals=0
        ),
        name="finish",
    )(*arrays)


def after(values, *others):
    return lax.optimization_barrier((values, *others))[0]


def gather_tokens_body(
    first_out, second_out, grad_first, grad_second, w_up, w_down, norm_gain, norm_bias
):
    n_dp, n_tensor, n_groups = (lax.axis_size(axis) for axis in ("dp", "tensor", "groups"))
    own_rows, depth = first_out.shape[0], w_up.shape[0]
    units = w_up.shape[1] // n_dp
    mates = 2 if n_groups % 2 == 0 else 1
    place = lax.axis_index("dp")
    top = bits_of(n_dp)[0]

    high, others = bits_of(n_tensor)[0], bits_of(n_tensor)[1:]
    own, *sends = pack(first_out, grad_second, w_up, w_down, mates)
    tokens, chunks, got, crossed = {0: own}, {}, {}, {}

    def tokens_dp(k, *first):
        tokens[k] = swap(after(tokens[k & (k - 1)], *first), "dp", k & -k, f"tokens_{k}")

    def tokens_tensor(k, *first):
        start = after(tokens[k], *first)
        chunks[k] = {0: tokens[k], high: swap(start, "tensor", high, f"tokens_{k}_{high}")}

    def tokens_rest(k, *first):
        for bit in others:
            for j in list(chunks[k]):
                piece = after(chunks[k][j], *first)
                chunks[k][j | bit] = swap(piece, "tensor", bit, f"tokens_{k}_{j | bit}")

    def weights_groups(k, *first):
        if mates == 2:
            crossed[k] = swap(after(got[k], *first), "groups", 1, f"weights_{k}")

    def weights_dp(k, *first):
        got[k] = swap(after(sends[k - 1], *first), "dp", k, f"weights_{k}")

    for bit in reversed(bits_of(n_dp)):
        tokens_dp(bit)
    tokens_tensor(0)
    tokens_rest(0)
    tokens_tensor(1, tokens[top], chunks[0][high])
    stage = [*tokens.values(), *chunks[0].values()]
    for k in range(2, n_dp):
        if k & (k - 1):
            tokens_dp(k, *stage)
        weights_dp(k, *stage, *([got[top]] if top in got else []))
    for k in range(2, n_dp):
        tokens_rest(k - 1)
        stage = [got[top]]
        if k & (k - 1):
            weights_groups(top)
            stage = [tokens[k], *got.values(), *crossed.values(), *chunks[k - 2].values()]
        tokens_tensor(k, *stage, chunks[k - 1][high])
    weights_dp(1, *stage)
    for k in [*range(2, n_dp), 1]:
        if k not in crossed:
            weights_groups(k)
    tokens_rest(n_dp - 1, *crossed.values())
    got = {k: [got[k]] + ([crossed[k]] if k in crossed else []) for k in got}

    order = sorted(chunks, reverse=True)
    halves, blocks, stats = core(
        [[chunks[k][j] for j in range(n_tensor)] for k in order], w_up, w_down, got, mates, norm_gain, norm_bias
    )
    blocks = dict(enumerate(blocks))
    blocks[top] = swap(blocks[top], "dp", top, f"grads_{top}")

    sums, behind, hops = {}, (), []
    for k, (even, odd) in zip(order, halves, strict=True):
        came = swap(odd, "tensor", 1, f"sums_{k}_1")
        spans = [slice(j * 2 * own_rows, (j + 1) * 2 * own_rows) for j in range(n_tensor // 2)]
        parts = {2 * j: (even[span], came[span]) for j, span in enumerate(spans)}
        parts[0] = (even, came)
        for bit in reversed(bits_of(n_tensor)[:-1]):
            for j in [j for j in parts if j & bit]:
                send = after(sum(parts.pop(j)), *behind)
                if not hops:
                    stats = after(stats, send)
                parts[j ^ bit] += (swap(send, "tensor", bit, f"sums_{k}_{j}"),)
                behind = parts[j ^ bit][-1:]
                hops += behind
        sums[k] = parts[0]

    def add(terms):
        return sum(term[: 2 * own_rows].astype(jnp.float32) for term in terms).astype(jnp.bfloat16)

    for bit in bits_of(n_tensor):
        stats = stats + swap(stats, "tensor", bit, "stats")
    stats = stats.astype(jnp.bfloat16)
    extra = 16

    came = {}
    for bit in bits_of(n_dp)[::-1]:
        for k in [k for k in order if k & bit and k in sums and k != bit]:
            came[k] = swap(add(sums.pop(k)), "dp", bit, f"sums_{k}")
            sums[k ^ bit] += (came[k],)
    last = jnp.concatenate([add(sums[top]), jnp.pad(stats, ((0, extra - 2), (0, 0)))])
    came[top] = swap(last, "dp", top, f"sums_{top}")
    rows = stats.reshape(-1, units)
    rows = jnp.pad(rows, ((0, extra - rows.shape[0]), (0, 0)))
    for k in range(1, n_dp):
        if k != top:
            block = jnp.concatenate([blocks[k], rows])
            first = [last] if k < top else [blocks[top], *hops[:1]]
            blocks[k] = swap(after(block, *first), "dp", k, f"grads_{k}")
    for bit in bits_of(n_dp)[:0:-1]:
        came[bit] = swap(after(add(sums[bit]), last), "dp", bit, f"sums_{bit}")

    scale = (own_rows * n_tensor * n_dp) ** (-0.5)
    terms = [*sums[0], *(came[bit] for bit in bits_of(n_dp)[::-1])]
    return tuple(
        finish(
            [blocks[k] for k in range(n_dp)],
            terms,
            stats,
            first_out,
            second_out,
            grad_first,
            norm_gain,
            norm_bias,
            (w_up.shape, w_down.shape),
            scale,
        )
    )


def body(first_out, second_out, grad_first, grad_second, w_up, *rest):
    n_dp, n_tensor = lax.axis_size("dp"), lax.axis_size("tensor")
    powers = all(size > 1 and size & (size - 1) == 0 for size in (n_dp, n_tensor))
    few_tokens = first_out.shape[0] * n_tensor < w_up.shape[1]
    units, depth = w_up.shape[1] // n_dp, w_up.shape[0]
    fits = w_up.shape[1] % n_dp == 0 and units % depth == 0 and depth % 128 == 0
    fits = fits and first_out.shape[1] == 2 * units and n_dp > 2 and n_tensor > 2
    pick = gather_tokens_body if powers and few_tokens and fits else gather_weights_body
    return pick(first_out, second_out, grad_first, grad_second, w_up, *rest)


def solution(mesh):
    in_specs = (
        P(("groups", "tensor", "dp"), None),
        P(("groups", "tensor", "dp"), None),
        P(("groups", "tensor", "dp"), None),
        P(("groups", "tensor", "dp"), None),
        P("dp", "tensor"),
        P("tensor", "dp"),
        P(),
        P(),
    )
    out_specs = (
        P(("groups", "tensor", "dp"), None),
        P(("groups", "tensor", "dp"), None),
        P(("groups", "dp"), "tensor"),
        P(("groups", "tensor"), "dp"),
        P("groups", None),
    )
    return jax.shard_map(body, mesh=mesh, in_specs=in_specs, out_specs=out_specs, check_vma=False)
```

```python
import math

import jax
import jax.numpy as jnp
from jax import lax
from jax.experimental import pallas as pl
from jax.experimental.pallas import tpu as pltpu
from jax.sharding import PartitionSpec as P

epsilon = 1e-06


def normalize(row_data, norm_gain, norm_bias):
    values = row_data.astype(jnp.float32)
    row_mean = jnp.mean(values, axis=-1, keepdims=True)
    centred = values - row_mean
    inv_std = lax.rsqrt(jnp.mean(centred * centred, axis=-1, keepdims=True) + epsilon)
    standard = centred * inv_std
    normed = (standard * norm_gain + norm_bias).astype(jnp.bfloat16)
    return (standard, inv_std, normed)


def contract_tokens(left_rows, right_rows):
    return lax.dot_general(
        left_rows, right_rows, (((0,), (0,)), ((), ())), preferred_element_type=jnp.float32
    )


def contract_last(left_rows, right_rows):
    return lax.dot_general(
        left_rows, right_rows, (((1,), (1,)), ((), ())), preferred_element_type=jnp.float32
    )


def finish_rows(branch, grad_normed, second_out, grad_first, first_out, norm_gain, norm_bias):
    standard, inv_std, _ = normalize(first_out, norm_gain, norm_bias)
    second_in = (second_out.astype(jnp.float32) - branch).astype(jnp.bfloat16)
    grad_std = grad_normed * norm_gain
    grad_rows = inv_std * (
        grad_std
        - jnp.mean(grad_std, axis=-1, keepdims=True)
        - standard * jnp.mean(grad_std * standard, axis=-1, keepdims=True)
    )
    return second_in, grad_first.astype(jnp.float32) + grad_rows


def gather_weights_body(
    first_out, second_out, grad_first, grad_second, w_up, w_down, norm_gain, norm_bias
):
    own_rows = first_out.shape[0]
    up_full = lax.all_gather(w_up, "dp", axis=0, tiled=True)
    down_full = lax.all_gather(w_down, "dp", axis=1, tiled=True)
    first_all = lax.all_gather(first_out, "tensor", axis=0, tiled=True)
    grad_all = lax.all_gather(grad_second, "tensor", axis=0, tiled=True)
    standard_all, _, normed = normalize(first_all, norm_gain, norm_bias)
    offset = lax.axis_index("tensor") * own_rows
    standard = lax.dynamic_slice_in_dim(standard_all, offset, own_rows, 0)
    preact = jnp.dot(normed, up_full, preferred_element_type=jnp.float32)
    hidden = jax.nn.gelu(preact).astype(jnp.bfloat16)
    branch = lax.psum_scatter(
        jnp.dot(hidden, down_full, preferred_element_type=jnp.float32).astype(jnp.bfloat16),
        "tensor",
        scatter_dimension=0,
        tiled=True,
    ).astype(jnp.float32)
    tokens = own_rows * lax.axis_size("tensor") * lax.axis_size("dp")
    grad_scale = tokens ** (-0.5)
    grad_down_part = contract_tokens(hidden, grad_all)
    grad_down = (
        lax.psum_scatter(
            grad_down_part.astype(jnp.bfloat16), "dp", scatter_dimension=1, tiled=True
        ).astype(jnp.float32)
        * grad_scale
    )
    grad_hidden = contract_last(grad_all, down_full)
    grad_pre = jax.vjp(jax.nn.gelu, preact)[1](grad_hidden)[0].astype(jnp.bfloat16)
    grad_up_part = contract_tokens(normed, grad_pre)
    grad_up = (
        lax.psum_scatter(
            grad_up_part.astype(jnp.bfloat16), "dp", scatter_dimension=0, tiled=True
        ).astype(jnp.float32)
        * grad_scale
    )
    grad_normed = lax.psum_scatter(
        contract_last(grad_pre, up_full).astype(jnp.bfloat16),
        "tensor",
        scatter_dimension=0,
        tiled=True,
    ).astype(jnp.float32)
    second_in, grad_first_in = finish_rows(
        branch, grad_normed, second_out, grad_first, first_out, norm_gain, norm_bias
    )
    local_stats = jnp.stack([jnp.sum(grad_normed * standard, axis=0), jnp.sum(grad_normed, axis=0)])
    grad_norm = lax.psum(local_stats, ("tensor", "dp")) * grad_scale
    return (second_in, grad_first_in, grad_up, grad_down, grad_norm)


def swap(values, axis, mask, scope):
    with jax.named_scope(scope):
        return lax.ppermute(values, axis, [(i, i ^ mask) for i in range(lax.axis_size(axis))])


def bits_of(size):
    return [1 << b for b in reversed(range(size.bit_length() - 1))]


def pack(first_out, grad_second, w_up, w_down, mates):
    n_dp, (own_rows, width) = lax.axis_size("dp"), first_out.shape
    depth, units = w_up.shape[0], w_up.shape[1] // n_dp
    strips, rows = units // depth, depth // mates

    def kernel(first_ref, grad_ref, up_ref, down_ref, own, *sends):
        place, mate = lax.axis_index("dp"), lax.rem(lax.axis_index("groups"), mates)
        own[:own_rows, :] = first_ref[...]
        own[own_rows:, :] = grad_ref[...]
        for k in range(1, n_dp):
            first = pl.multiple_of((place ^ k) * units, units)
            send = sends[k - 1]
            send[:, :units] = up_ref[pl.ds(pl.multiple_of(mate * rows, rows), rows), pl.ds(first, units)]
            for c in range(strips):
                row = pl.multiple_of(first + mate * (units // mates) + c * rows, rows)
                send[:, units + c * depth : units + (c + 1) * depth] = down_ref[pl.ds(row, rows), :]

    return pl.pallas_call(
        kernel,
        out_shape=[jax.ShapeDtypeStruct((2 * own_rows, width), w_up.dtype)]
        + [jax.ShapeDtypeStruct((rows, width), w_up.dtype)] * (n_dp - 1),
        in_specs=[pl.BlockSpec(memory_space=pltpu.VMEM)] * 4,
        out_specs=[pl.BlockSpec(memory_space=pltpu.VMEM)] * n_dp,
        cost_estimate=pl.CostEstimate(flops=0, bytes_accessed=8 * w_up.size, transcendentals=0),
        name="pack",
    )(first_out, grad_second, w_up, w_down)


def core(chunks, w_up, w_down, got, mates, gain, bias):
    n_chunks, n, n_dp = len(chunks), len(chunks[0]), lax.axis_size("dp")
    (piece_rows, width), units = chunks[0][0].shape, w_up.shape[1] // n_dp
    piece_rows //= 2
    depth = width // n_dp
    strips, pair = units // depth, 2 * piece_rows
    slope = (2.0 / math.pi) ** 0.5
    dtype = w_up.dtype
    pieces_of_weights = [piece for k in range(1, n_dp) for piece in got[k]]
    n_got = len(pieces_of_weights)

    def kernel(*refs):
        toks, refs = refs[: n_chunks * n], refs[n_chunks * n :]
        (own_up, own_down), weights, (gain_ref, bias_ref), refs = (
            refs[:2],
            list(refs[2 : 2 + n_got]),
            refs[2 + n_got : 4 + n_got],
            refs[4 + n_got :],
        )
        outs, blocks, stat_ref = refs[: 2 * n_chunks], refs[2 * n_chunks : 2 * n_chunks + n_dp], refs[2 * n_chunks + n_dp]
        tok, norm, hid, pre, part, block, up_ref, down_ref, in_sem, w_sem, out_sem, b_sem = refs[2 * n_chunks + n_dp + 1 :]
        place, mate = lax.axis_index("dp"), lax.rem(lax.axis_index("groups"), mates)
        reads, loads, writes = [], [], []

        def load(src, dst):
            loads.append(pltpu.make_async_copy(src, dst, w_sem.at[len(loads)]))
            loads[-1].start()

        for i, ref in enumerate(toks):
            reads.append(pltpu.make_async_copy(ref, tok.at[i], in_sem.at[i]))
            if i < n:
                reads[-1].start()
        mine = pl.ds(pl.multiple_of(place * units, units), units)
        rows = pl.ds(pl.multiple_of(place * depth, depth), depth)
        load(own_up.at[:, mine], up_ref.at[rows, :])
        load(own_down.at[mine, :], down_ref.at[:, rows])
        for k in range(1, n_dp):
            first = pl.multiple_of((place ^ k) * depth, depth)
            many = len(got[k])
            rows = depth // many
            for j in range(many):
                piece = weights.pop(0)
                which = mate ^ j if many > 1 else 0
                row = pl.multiple_of(first + which * rows, rows)
                load(piece.at[:, pl.ds(0, units)], up_ref.at[pl.ds(row, rows), :])
                for c in range(strips):
                    row = pl.multiple_of(which * (units // many) + c * rows, rows)
                    load(
                        piece.at[:, pl.ds(units + c * depth, depth)],
                        down_ref.at[pl.ds(row, rows), pl.ds(first, depth)],
                    )
        for one in reads[n:]:
            one.start()
        stat_ref[...] = jnp.zeros_like(stat_ref)
        for i in range(n_chunks):
            for one in reads[i * n : (i + 1) * n] + (loads if i == 0 else []):
                one.wait()

            @pl.loop(0, n // 2)
            def _(t):
                at = i * n + 2 * t
                span = pl.ds(pl.multiple_of(at * piece_rows, pair), pair)
                values = tok[pl.ds(at, 2), :piece_rows].reshape(pair, width).astype(jnp.float32)
                centred = values - jnp.mean(values, axis=-1, keepdims=True)
                inv_std = lax.rsqrt(jnp.mean(centred * centred, axis=-1, keepdims=True) + epsilon)
                standard = centred * inv_std
                normed = (standard * gain_ref[...] + bias_ref[...]).astype(dtype)
                norm[span, :] = normed
                x = jnp.dot(normed, up_ref[...], preferred_element_type=jnp.float32)
                gate = jnp.tanh(slope * (x + 0.044715 * (x * x * x)))
                half = 0.5 + 0.5 * gate
                hidden = (x * half).astype(dtype)
                hid[span, :] = hidden
                rise = half + (0.5 * slope) * x * (1.0 - gate * gate) * (1.0 + (3 * 0.044715) * (x * x))
                grads = tok[pl.ds(at, 2), piece_rows:].reshape(pair, width)
                grad_pre = (contract_last(grads, down_ref[...]) * rise).astype(dtype)
                pre[span, :] = grad_pre
                branch = jnp.dot(hidden, down_ref[...], preferred_element_type=jnp.float32)
                grad_normed = contract_last(grad_pre, up_ref[...])
                stat_ref[0:1, :] += jnp.sum(grad_normed * standard, axis=0, keepdims=True)
                stat_ref[1:2, :] += jnp.sum(grad_normed, axis=0, keepdims=True)
                row = pl.multiple_of(t * pair, pair)
                for odd in range(2):
                    own = slice(odd * piece_rows, (odd + 1) * piece_rows)
                    part[2 * i + odd, pl.ds(row, piece_rows), :] = branch[own].astype(dtype)
                    part[2 * i + odd, pl.ds(row + piece_rows, piece_rows), :] = grad_normed[own].astype(dtype)

            for odd in (1, 0):
                at = 2 * i + odd
                writes.append(pltpu.make_async_copy(part.at[at], outs[at], out_sem.at[at]))
                writes[-1].start()
        top = bits_of(n_dp)[0]
        for k in sorted(range(n_dp), key=lambda k: (k < top, k)):
            columns = pl.ds(pl.multiple_of((place ^ k) * depth, depth), depth)
            block[k, :depth, :] = contract_tokens(norm[:, columns], pre[...]).astype(dtype)
            grads = tok[:, piece_rows:, columns].reshape(n_chunks * n * piece_rows, depth)
            down_block = contract_tokens(hid[...], grads).astype(dtype)
            for c in range(strips):
                block[k, depth:, c * depth : (c + 1) * depth] = down_block[c * depth : (c + 1) * depth]
            writes.append(pltpu.make_async_copy(block.at[k], blocks[k], b_sem.at[k]))
            writes[-1].start()
        for one in writes:
            one.wait()

    rows = n_chunks * n * piece_rows
    half = (n // 2 * pair, width)
    far = pl.BlockSpec(memory_space=pl.ANY)
    near = pl.BlockSpec(memory_space=pltpu.VMEM)
    out = pl.pallas_call(
        kernel,
        out_shape=[jax.ShapeDtypeStruct(half, dtype)] * (2 * n_chunks)
        + [jax.ShapeDtypeStruct((2 * depth, units), dtype)] * n_dp
        + [jax.ShapeDtypeStruct((2, width), jnp.float32)],
        in_specs=[far] * (n_chunks * n + 2 + n_got) + [near] * 2,
        out_specs=[far] * (2 * n_chunks + n_dp) + [near],
        scratch_shapes=[
            pltpu.VMEM((n_chunks * n, pair, width), dtype),
            pltpu.VMEM((rows, width), dtype),
            pltpu.VMEM((rows, units), dtype),
            pltpu.VMEM((rows, units), dtype),
            pltpu.VMEM((2 * n_chunks, *half), dtype),
            pltpu.VMEM((n_dp, 2 * depth, units), dtype),
            pltpu.VMEM((width, units), dtype),
            pltpu.VMEM((units, width), dtype),
            pltpu.SemaphoreType.DMA((n_chunks * n,)),
            pltpu.SemaphoreType.DMA((2 + n_got * (1 + strips),)),
            pltpu.SemaphoreType.DMA((2 * n_chunks,)),
            pltpu.SemaphoreType.DMA((n_dp,)),
        ],
        compiler_params=pltpu.CompilerParams(vmem_limit_bytes=56 * 1024 * 1024),
        cost_estimate=pl.CostEstimate(
            flops=10 * rows * width * units,
            bytes_accessed=8 * rows * width + 8 * width * units,
            transcendentals=rows * units,
        ),
        name="core",
    )(
        *[piece for chunk in chunks for piece in chunk],
        w_up,
        w_down,
        *pieces_of_weights,
        gain.reshape(1, width),
        bias.reshape(1, width),
    )
    halves = [out[2 * i : 2 * i + 2] for i in range(n_chunks)]
    return halves, list(out[2 * n_chunks : -1]), out[-1]


def finish(blocks, terms, own_stats, first_out, second_out, grad_first, gain, bias, w_shapes, scale):
    (rows, width), n_dp = first_out.shape, len(blocks)
    depth, units = w_shapes[0][0], w_shapes[0][1] // n_dp
    strips, n_bits, n_terms = units // depth, len(bits_of(n_dp)), len(terms)

    def kernel(*refs):
        parts, adds, (stat_ref, first_ref, second_ref, grad_ref, gain_ref, bias_ref), outs = (
            refs[:n_dp],
            refs[n_dp : n_dp + n_terms],
            refs[n_dp + n_terms : n_dp + n_terms + 6],
            refs[n_dp + n_terms + 6 :],
        )
        second_in, grad_in, up_out, down_out, norm_out = outs
        place = lax.axis_index("dp")
        for k in range(n_dp):
            first = pl.multiple_of((place ^ k) * units, units)
            up_out[:, pl.ds(first, units)] = parts[k][:depth, :].astype(jnp.float32) * scale
            for c in range(strips):
                block = parts[k][depth : 2 * depth, c * depth : (c + 1) * depth]
                row = pl.multiple_of(first + c * depth, depth)
                down_out[pl.ds(row, depth), :] = block.astype(jnp.float32) * scale
        total = sum(ref[: 2 * rows, :].astype(jnp.float32) for ref in adds)
        second_in[...] = (second_ref[...].astype(jnp.float32) - total[:rows]).astype(second_in.dtype)
        values = first_ref[...].astype(jnp.float32)
        centred = values - jnp.mean(values, axis=-1, keepdims=True)
        inv_std = lax.rsqrt(jnp.mean(centred * centred, axis=-1, keepdims=True) + epsilon)
        standard = centred * inv_std
        grad_std = total[rows:] * gain_ref[...]
        grad_rows = inv_std * (
            grad_std
            - jnp.mean(grad_std, axis=-1, keepdims=True)
            - standard * jnp.mean(grad_std * standard, axis=-1, keepdims=True)
        )
        grad_in[...] = grad_ref[...].astype(jnp.float32) + grad_rows
        stats = []
        for k in range(n_dp):
            if k == 0:
                one = stat_ref[...].astype(jnp.float32)
            elif k & (k - 1) == 0:
                one = adds[n_terms - n_bits + k.bit_length() - 1][2 * rows :, :].astype(jnp.float32)[:2]
            else:
                tail = parts[k][2 * depth :, :].astype(jnp.float32)
                per = width // units
                one = jnp.concatenate(
                    [
                        jnp.concatenate([tail[i * per + j : i * per + j + 1] for j in range(per)], axis=1)
                        for i in range(2)
                    ],
                    axis=0,
                )
            stats.append(one)
        while len(stats) > 1:
            stats = [one + two for one, two in zip(stats[0::2], stats[1::2], strict=True)]
        norm_out[...] = stats[0] * scale

    def whole(x):
        return pl.BlockSpec(x.shape, lambda i: (0, 0))

    arrays = [*blocks, *terms, own_stats, first_out, second_out, grad_first, gain.reshape(1, width), bias.reshape(1, width)]
    in_specs = [whole(x) for x in arrays]
    for i in range(n_terms - n_bits):
        in_specs[n_dp + i] = pl.BlockSpec((2 * rows, width), lambda i: (0, 0))
    out_shape = [
        jax.ShapeDtypeStruct((rows, width), second_out.dtype),
        jax.ShapeDtypeStruct((rows, width), jnp.float32),
        jax.ShapeDtypeStruct(w_shapes[0], jnp.float32),
        jax.ShapeDtypeStruct(w_shapes[1], jnp.float32),
        jax.ShapeDtypeStruct((2, width), jnp.float32),
    ]
    return pl.pallas_call(
        kernel,
        out_shape=out_shape,
        grid=(1,),
        in_specs=in_specs,
        out_specs=[whole(x) for x in out_shape],
        compiler_params=pltpu.CompilerParams(vmem_limit_bytes=48 * 1024 * 1024),
        cost_estimate=pl.CostEstimate(
            flops=0, bytes_accessed=12 * w_shapes[0][0] * w_shapes[0][1], transcendentals=0
        ),
        name="finish",
    )(*arrays)


def after(values, *others):
    return lax.optimization_barrier((values, *others))[0]


def gather_tokens_body(
    first_out, second_out, grad_first, grad_second, w_up, w_down, norm_gain, norm_bias
):
    n_dp, n_tensor, n_groups = (lax.axis_size(axis) for axis in ("dp", "tensor", "groups"))
    own_rows, depth = first_out.shape[0], w_up.shape[0]
    units = w_up.shape[1] // n_dp
    mates = 2 if n_groups % 2 == 0 else 1
    place = lax.axis_index("dp")
    top = bits_of(n_dp)[0]

    high, others = bits_of(n_tensor)[0], bits_of(n_tensor)[1:]
    own, *sends = pack(first_out, grad_second, w_up, w_down, mates)
    tokens, chunks, got, crossed = {0: own}, {}, {}, {}

    def tokens_dp(k, *first):
        tokens[k] = swap(after(tokens[k & (k - 1)], *first), "dp", k & -k, f"tokens_{k}")

    def tokens_tensor(k, *first):
        start = after(tokens[k], *first)
        chunks[k] = {0: tokens[k], high: swap(start, "tensor", high, f"tokens_{k}_{high}")}

    def tokens_rest(k, *first):
        for bit in others:
            for j in list(chunks[k]):
                piece = after(chunks[k][j], *first)
                chunks[k][j | bit] = swap(piece, "tensor", bit, f"tokens_{k}_{j | bit}")

    def weights_groups(k, *first):
        if mates == 2:
            crossed[k] = swap(after(got[k], *first), "groups", 1, f"weights_{k}")

    def weights_dp(k, *first):
        got[k] = swap(after(sends[k - 1], *first), "dp", k, f"weights_{k}")

    for bit in reversed(bits_of(n_dp)):
        tokens_dp(bit)
    tokens_tensor(0)
    tokens_rest(0)
    tokens_tensor(1, tokens[top], chunks[0][high])
    stage = [*tokens.values(), *chunks[0].values()]
    for k in range(2, n_dp):
        if k & (k - 1):
            tokens_dp(k, *stage)
        weights_dp(k, *stage, *([got[top]] if top in got else []))
    for k in range(2, n_dp):
        tokens_rest(k - 1)
        stage = [got[top]]
        if k & (k - 1):
            weights_groups(top)
            stage = [tokens[k], *got.values(), *crossed.values(), *chunks[k - 2].values()]
        tokens_tensor(k, *stage, chunks[k - 1][high])
    weights_dp(1, *stage)
    for k in [*range(2, n_dp), 1]:
        if k not in crossed:
            weights_groups(k)
    tokens_rest(n_dp - 1, *crossed.values())
    got = {k: [got[k]] + ([crossed[k]] if k in crossed else []) for k in got}

    order = sorted(chunks, reverse=True)
    halves, blocks, stats = core(
        [[chunks[k][j] for j in range(n_tensor)] for k in order], w_up, w_down, got, mates, norm_gain, norm_bias
    )
    blocks = dict(enumerate(blocks))
    for bit in bits_of(n_dp):
        blocks[bit] = swap(blocks[bit], "dp", bit, f"grads_{bit}")

    sums, behind, hops = {}, (), []
    for k, (even, odd) in zip(order, halves, strict=True):
        came = swap(odd, "tensor", 1, f"sums_{k}_1")
        spans = [slice(j * 2 * own_rows, (j + 1) * 2 * own_rows) for j in range(n_tensor // 2)]
        parts = {2 * j: (even[span], came[span]) for j, span in enumerate(spans)}
        parts[0] = (even, came)
        for bit in reversed(bits_of(n_tensor)[:-1]):
            for j in [j for j in parts if j & bit]:
                send = after(sum(parts.pop(j)), *behind)
                if not hops:
                    stats = after(stats, send)
                came = swap(send, "tensor", bit, f"sums_{k}_{j}")
                if k == top:
                    came = after(came, blocks[top])
                parts[j ^ bit] += (came,)
                behind = parts[j ^ bit][-1:]
                hops += behind
        sums[k] = parts[0]

    def add(terms):
        return sum(term[: 2 * own_rows].astype(jnp.float32) for term in terms).astype(jnp.bfloat16)

    for bit in bits_of(n_tensor):
        stats = stats + swap(stats, "tensor", bit, "stats")
    stats = stats.astype(jnp.bfloat16)
    extra = 16

    came = {}
    for bit in bits_of(n_dp)[::-1]:
        for k in [k for k in order if k & bit and k in sums and k != bit]:
            came[k] = swap(add(sums.pop(k)), "dp", bit, f"sums_{k}")
            sums[k ^ bit] += (came[k],)
    last = jnp.concatenate([add(sums[top]), jnp.pad(stats, ((0, extra - 2), (0, 0)))])
    came[top] = swap(last, "dp", top, f"sums_{top}")
    rows = stats.reshape(-1, units)
    rows = jnp.pad(rows, ((0, extra - rows.shape[0]), (0, 0)))
    for k in range(1, n_dp):
        if k & (k - 1):
            block = jnp.concatenate([blocks[k], rows])
            block = after(block, blocks[top], *hops[:1])
            blocks[k] = swap(block, "dp", k, f"grads_{k}")
    for bit in bits_of(n_dp)[:0:-1]:
        send = jnp.concatenate([add(sums[bit]), jnp.pad(after(stats, last), ((0, extra - 2), (0, 0)))])
        came[bit] = swap(send, "dp", bit, f"sums_{bit}")

    scale = (own_rows * n_tensor * n_dp) ** (-0.5)
    terms = [*sums[0], *(came[bit] for bit in bits_of(n_dp)[::-1])]
    return tuple(
        finish(
            [blocks[k] for k in range(n_dp)],
            terms,
            stats,
            first_out,
            second_out,
            grad_first,
            norm_gain,
            norm_bias,
            (w_up.shape, w_down.shape),
            scale,
        )
    )


def body(first_out, second_out, grad_first, grad_second, w_up, *rest):
    n_dp, n_tensor = lax.axis_size("dp"), lax.axis_size("tensor")
    powers = all(size > 1 and size & (size - 1) == 0 for size in (n_dp, n_tensor))
    few_tokens = first_out.shape[0] * n_tensor < w_up.shape[1]
    units, depth = w_up.shape[1] // n_dp, w_up.shape[0]
    fits = w_up.shape[1] % n_dp == 0 and units % depth == 0 and depth % 128 == 0
    fits = fits and first_out.shape[1] == 2 * units and n_dp > 2 and n_tensor > 2
    pick = gather_tokens_body if powers and few_tokens and fits else gather_weights_body
    return pick(first_out, second_out, grad_first, grad_second, w_up, *rest)


def solution(mesh):
    in_specs = (
        P(("groups", "tensor", "dp"), None),
        P(("groups", "tensor", "dp"), None),
        P(("groups", "tensor", "dp"), None),
        P(("groups", "tensor", "dp"), None),
        P("dp", "tensor"),
        P("tensor", "dp"),
        P(),
        P(),
    )
    out_specs = (
        P(("groups", "tensor", "dp"), None),
        P(("groups", "tensor", "dp"), None),
        P(("groups", "dp"), "tensor"),
        P(("groups", "tensor"), "dp"),
        P("groups", None),
    )
    return jax.shard_map(body, mesh=mesh, in_specs=in_specs, out_specs=out_specs, check_vma=False)
```

```python
import math

import jax
import jax.numpy as jnp
from jax import lax
from jax.experimental import pallas as pl
from jax.experimental.pallas import tpu as pltpu
from jax.sharding import PartitionSpec as P

epsilon = 1e-06


def normalize(row_data, norm_gain, norm_bias):
    values = row_data.astype(jnp.float32)
    row_mean = jnp.mean(values, axis=-1, keepdims=True)
    centred = values - row_mean
    inv_std = lax.rsqrt(jnp.mean(centred * centred, axis=-1, keepdims=True) + epsilon)
    standard = centred * inv_std
    normed = (standard * norm_gain + norm_bias).astype(jnp.bfloat16)
    return (standard, inv_std, normed)


def contract_tokens(left_rows, right_rows):
    return lax.dot_general(
        left_rows, right_rows, (((0,), (0,)), ((), ())), preferred_element_type=jnp.float32
    )


def contract_last(left_rows, right_rows):
    return lax.dot_general(
        left_rows, right_rows, (((1,), (1,)), ((), ())), preferred_element_type=jnp.float32
    )


def finish_rows(branch, grad_normed, second_out, grad_first, first_out, norm_gain, norm_bias):
    standard, inv_std, _ = normalize(first_out, norm_gain, norm_bias)
    second_in = (second_out.astype(jnp.float32) - branch).astype(jnp.bfloat16)
    grad_std = grad_normed * norm_gain
    grad_rows = inv_std * (
        grad_std
        - jnp.mean(grad_std, axis=-1, keepdims=True)
        - standard * jnp.mean(grad_std * standard, axis=-1, keepdims=True)
    )
    return second_in, grad_first.astype(jnp.float32) + grad_rows


def gather_weights_body(
    first_out, second_out, grad_first, grad_second, w_up, w_down, norm_gain, norm_bias
):
    own_rows = first_out.shape[0]
    up_full = lax.all_gather(w_up, "dp", axis=0, tiled=True)
    down_full = lax.all_gather(w_down, "dp", axis=1, tiled=True)
    first_all = lax.all_gather(first_out, "tensor", axis=0, tiled=True)
    grad_all = lax.all_gather(grad_second, "tensor", axis=0, tiled=True)
    standard_all, _, normed = normalize(first_all, norm_gain, norm_bias)
    offset = lax.axis_index("tensor") * own_rows
    standard = lax.dynamic_slice_in_dim(standard_all, offset, own_rows, 0)
    preact = jnp.dot(normed, up_full, preferred_element_type=jnp.float32)
    hidden = jax.nn.gelu(preact).astype(jnp.bfloat16)
    branch = lax.psum_scatter(
        jnp.dot(hidden, down_full, preferred_element_type=jnp.float32).astype(jnp.bfloat16),
        "tensor",
        scatter_dimension=0,
        tiled=True,
    ).astype(jnp.float32)
    tokens = own_rows * lax.axis_size("tensor") * lax.axis_size("dp")
    grad_scale = tokens ** (-0.5)
    grad_down_part = contract_tokens(hidden, grad_all)
    grad_down = (
        lax.psum_scatter(
            grad_down_part.astype(jnp.bfloat16), "dp", scatter_dimension=1, tiled=True
        ).astype(jnp.float32)
        * grad_scale
    )
    grad_hidden = contract_last(grad_all, down_full)
    grad_pre = jax.vjp(jax.nn.gelu, preact)[1](grad_hidden)[0].astype(jnp.bfloat16)
    grad_up_part = contract_tokens(normed, grad_pre)
    grad_up = (
        lax.psum_scatter(
            grad_up_part.astype(jnp.bfloat16), "dp", scatter_dimension=0, tiled=True
        ).astype(jnp.float32)
        * grad_scale
    )
    grad_normed = lax.psum_scatter(
        contract_last(grad_pre, up_full).astype(jnp.bfloat16),
        "tensor",
        scatter_dimension=0,
        tiled=True,
    ).astype(jnp.float32)
    second_in, grad_first_in = finish_rows(
        branch, grad_normed, second_out, grad_first, first_out, norm_gain, norm_bias
    )
    local_stats = jnp.stack([jnp.sum(grad_normed * standard, axis=0), jnp.sum(grad_normed, axis=0)])
    grad_norm = lax.psum(local_stats, ("tensor", "dp")) * grad_scale
    return (second_in, grad_first_in, grad_up, grad_down, grad_norm)


def swap(values, axis, mask, scope):
    with jax.named_scope(scope):
        return lax.ppermute(values, axis, [(i, i ^ mask) for i in range(lax.axis_size(axis))])


def bits_of(size):
    return [1 << b for b in reversed(range(size.bit_length() - 1))]


def pack(first_out, grad_second, w_up, w_down, mates):
    n_dp, (own_rows, width) = lax.axis_size("dp"), first_out.shape
    depth, units = w_up.shape[0], w_up.shape[1] // n_dp
    strips, rows = units // depth, depth // mates

    def kernel(first_ref, grad_ref, up_ref, down_ref, own, *sends):
        place, mate = lax.axis_index("dp"), lax.rem(lax.axis_index("groups"), mates)
        own[:own_rows, :] = first_ref[...]
        own[own_rows:, :] = grad_ref[...]
        for k in range(1, n_dp):
            first = pl.multiple_of((place ^ k) * units, units)
            send = sends[k - 1]
            send[:, :units] = up_ref[pl.ds(pl.multiple_of(mate * rows, rows), rows), pl.ds(first, units)]
            for c in range(strips):
                row = pl.multiple_of(first + mate * (units // mates) + c * rows, rows)
                send[:, units + c * depth : units + (c + 1) * depth] = down_ref[pl.ds(row, rows), :]

    return pl.pallas_call(
        kernel,
        out_shape=[jax.ShapeDtypeStruct((2 * own_rows, width), w_up.dtype)]
        + [jax.ShapeDtypeStruct((rows, width), w_up.dtype)] * (n_dp - 1),
        in_specs=[pl.BlockSpec(memory_space=pltpu.VMEM)] * 4,
        out_specs=[pl.BlockSpec(memory_space=pltpu.VMEM)] * n_dp,
        cost_estimate=pl.CostEstimate(flops=0, bytes_accessed=8 * w_up.size, transcendentals=0),
        name="pack",
    )(first_out, grad_second, w_up, w_down)


def core(chunks, w_up, w_down, got, mates, gain, bias):
    n_chunks, n, n_dp = len(chunks), len(chunks[0]), lax.axis_size("dp")
    (piece_rows, width), units = chunks[0][0].shape, w_up.shape[1] // n_dp
    piece_rows //= 2
    depth = width // n_dp
    strips, pair = units // depth, 2 * piece_rows
    slope = (2.0 / math.pi) ** 0.5
    dtype = w_up.dtype
    pieces_of_weights = [piece for k in range(1, n_dp) for piece in got[k]]
    n_got = len(pieces_of_weights)

    def kernel(*refs):
        toks, refs = refs[: n_chunks * n], refs[n_chunks * n :]
        (own_up, own_down), weights, (gain_ref, bias_ref), refs = (
            refs[:2],
            list(refs[2 : 2 + n_got]),
            refs[2 + n_got : 4 + n_got],
            refs[4 + n_got :],
        )
        outs, blocks, stat_ref = refs[: 2 * n_chunks], refs[2 * n_chunks : 2 * n_chunks + n_dp], refs[2 * n_chunks + n_dp]
        tok, norm, hid, pre, part, block, up_ref, down_ref, in_sem, w_sem, out_sem, b_sem = refs[2 * n_chunks + n_dp + 1 :]
        place, mate = lax.axis_index("dp"), lax.rem(lax.axis_index("groups"), mates)
        reads, loads, writes = [], [], []

        def load(src, dst):
            loads.append(pltpu.make_async_copy(src, dst, w_sem.at[len(loads)]))
            loads[-1].start()

        for i, ref in enumerate(toks):
            reads.append(pltpu.make_async_copy(ref, tok.at[i], in_sem.at[i]))
            if i < n:
                reads[-1].start()
        mine = pl.ds(pl.multiple_of(place * units, units), units)
        rows = pl.ds(pl.multiple_of(place * depth, depth), depth)
        load(own_up.at[:, mine], up_ref.at[rows, :])
        load(own_down.at[mine, :], down_ref.at[:, rows])
        for k in range(1, n_dp):
            first = pl.multiple_of((place ^ k) * depth, depth)
            many = len(got[k])
            rows = depth // many
            for j in range(many):
                piece = weights.pop(0)
                which = mate ^ j if many > 1 else 0
                row = pl.multiple_of(first + which * rows, rows)
                load(piece.at[:, pl.ds(0, units)], up_ref.at[pl.ds(row, rows), :])
                for c in range(strips):
                    row = pl.multiple_of(which * (units // many) + c * rows, rows)
                    load(
                        piece.at[:, pl.ds(units + c * depth, depth)],
                        down_ref.at[pl.ds(row, rows), pl.ds(first, depth)],
                    )
        for one in reads[n:]:
            one.start()
        stat_ref[...] = jnp.zeros_like(stat_ref)
        for i in range(n_chunks):
            for one in reads[i * n : (i + 1) * n] + (loads if i == 0 else []):
                one.wait()

            @pl.loop(0, n // 2)
            def _(t):
                at = i * n + 2 * t
                span = pl.ds(pl.multiple_of(at * piece_rows, pair), pair)
                values = tok[pl.ds(at, 2), :piece_rows].reshape(pair, width).astype(jnp.float32)
                centred = values - jnp.mean(values, axis=-1, keepdims=True)
                inv_std = lax.rsqrt(jnp.mean(centred * centred, axis=-1, keepdims=True) + epsilon)
                standard = centred * inv_std
                normed = (standard * gain_ref[...] + bias_ref[...]).astype(dtype)
                norm[span, :] = normed
                x = jnp.dot(normed, up_ref[...], preferred_element_type=jnp.float32)
                gate = jnp.tanh(slope * (x + 0.044715 * (x * x * x)))
                half = 0.5 + 0.5 * gate
                hidden = (x * half).astype(dtype)
                hid[span, :] = hidden
                rise = half + (0.5 * slope) * x * (1.0 - gate * gate) * (1.0 + (3 * 0.044715) * (x * x))
                grads = tok[pl.ds(at, 2), piece_rows:].reshape(pair, width)
                grad_pre = (contract_last(grads, down_ref[...]) * rise).astype(dtype)
                pre[span, :] = grad_pre
                branch = jnp.dot(hidden, down_ref[...], preferred_element_type=jnp.float32)
                grad_normed = contract_last(grad_pre, up_ref[...])
                stat_ref[0:1, :] += jnp.sum(grad_normed * standard, axis=0, keepdims=True)
                stat_ref[1:2, :] += jnp.sum(grad_normed, axis=0, keepdims=True)
                row = pl.multiple_of(t * pair, pair)
                for odd in range(2):
                    own = slice(odd * piece_rows, (odd + 1) * piece_rows)
                    part[2 * i + odd, pl.ds(row, piece_rows), :] = branch[own].astype(dtype)
                    part[2 * i + odd, pl.ds(row + piece_rows, piece_rows), :] = grad_normed[own].astype(dtype)

            for odd in (1, 0):
                at = 2 * i + odd
                writes.append(pltpu.make_async_copy(part.at[at], outs[at], out_sem.at[at]))
                writes[-1].start()
        top = bits_of(n_dp)[0]
        for k in sorted(range(n_dp), key=lambda k: (k < top, k)):
            columns = pl.ds(pl.multiple_of((place ^ k) * depth, depth), depth)
            block[k, :depth, :] = contract_tokens(norm[:, columns], pre[...]).astype(dtype)
            grads = tok[:, piece_rows:, columns].reshape(n_chunks * n * piece_rows, depth)
            down_block = contract_tokens(hid[...], grads).astype(dtype)
            for c in range(strips):
                block[k, depth:, c * depth : (c + 1) * depth] = down_block[c * depth : (c + 1) * depth]
            writes.append(pltpu.make_async_copy(block.at[k], blocks[k], b_sem.at[k]))
            writes[-1].start()
        for one in writes:
            one.wait()

    rows = n_chunks * n * piece_rows
    half = (n // 2 * pair, width)
    far = pl.BlockSpec(memory_space=pl.ANY)
    near = pl.BlockSpec(memory_space=pltpu.VMEM)
    out = pl.pallas_call(
        kernel,
        out_shape=[jax.ShapeDtypeStruct(half, dtype)] * (2 * n_chunks)
        + [jax.ShapeDtypeStruct((2 * depth, units), dtype)] * n_dp
        + [jax.ShapeDtypeStruct((2, width), jnp.float32)],
        in_specs=[far] * (n_chunks * n + 2 + n_got) + [near] * 2,
        out_specs=[far] * (2 * n_chunks + n_dp) + [near],
        scratch_shapes=[
            pltpu.VMEM((n_chunks * n, pair, width), dtype),
            pltpu.VMEM((rows, width), dtype),
            pltpu.VMEM((rows, units), dtype),
            pltpu.VMEM((rows, units), dtype),
            pltpu.VMEM((2 * n_chunks, *half), dtype),
            pltpu.VMEM((n_dp, 2 * depth, units), dtype),
            pltpu.VMEM((width, units), dtype),
            pltpu.VMEM((units, width), dtype),
            pltpu.SemaphoreType.DMA((n_chunks * n,)),
            pltpu.SemaphoreType.DMA((2 + n_got * (1 + strips),)),
            pltpu.SemaphoreType.DMA((2 * n_chunks,)),
            pltpu.SemaphoreType.DMA((n_dp,)),
        ],
        compiler_params=pltpu.CompilerParams(vmem_limit_bytes=56 * 1024 * 1024),
        cost_estimate=pl.CostEstimate(
            flops=10 * rows * width * units,
            bytes_accessed=8 * rows * width + 8 * width * units,
            transcendentals=rows * units,
        ),
        name="core",
    )(
        *[piece for chunk in chunks for piece in chunk],
        w_up,
        w_down,
        *pieces_of_weights,
        gain.reshape(1, width),
        bias.reshape(1, width),
    )
    halves = [out[2 * i : 2 * i + 2] for i in range(n_chunks)]
    return halves, list(out[2 * n_chunks : -1]), out[-1]


def finish(blocks, terms, own_stats, first_out, second_out, grad_first, gain, bias, w_shapes, scale):
    (rows, width), n_dp = first_out.shape, len(blocks)
    depth, units = w_shapes[0][0], w_shapes[0][1] // n_dp
    strips, n_bits, n_terms = units // depth, len(bits_of(n_dp)), len(terms)

    def kernel(*refs):
        parts, adds, (stat_ref, first_ref, second_ref, grad_ref, gain_ref, bias_ref), outs = (
            refs[:n_dp],
            refs[n_dp : n_dp + n_terms],
            refs[n_dp + n_terms : n_dp + n_terms + 6],
            refs[n_dp + n_terms + 6 :],
        )
        second_in, grad_in, up_out, down_out, norm_out = outs
        place = lax.axis_index("dp")
        for k in range(n_dp):
            first = pl.multiple_of((place ^ k) * units, units)
            up_out[:, pl.ds(first, units)] = parts[k][:depth, :].astype(jnp.float32) * scale
            for c in range(strips):
                block = parts[k][depth : 2 * depth, c * depth : (c + 1) * depth]
                row = pl.multiple_of(first + c * depth, depth)
                down_out[pl.ds(row, depth), :] = block.astype(jnp.float32) * scale
        total = sum(ref[: 2 * rows, :].astype(jnp.float32) for ref in adds)
        second_in[...] = (second_ref[...].astype(jnp.float32) - total[:rows]).astype(second_in.dtype)
        values = first_ref[...].astype(jnp.float32)
        centred = values - jnp.mean(values, axis=-1, keepdims=True)
        inv_std = lax.rsqrt(jnp.mean(centred * centred, axis=-1, keepdims=True) + epsilon)
        standard = centred * inv_std
        grad_std = total[rows:] * gain_ref[...]
        grad_rows = inv_std * (
            grad_std
            - jnp.mean(grad_std, axis=-1, keepdims=True)
            - standard * jnp.mean(grad_std * standard, axis=-1, keepdims=True)
        )
        grad_in[...] = grad_ref[...].astype(jnp.float32) + grad_rows
        stats = []
        for k in range(n_dp):
            if k == 0:
                one = stat_ref[...].astype(jnp.float32)
            elif k & (k - 1) == 0:
                one = adds[n_terms - n_bits + k.bit_length() - 1][2 * rows :, :].astype(jnp.float32)[:2]
            else:
                tail = parts[k][2 * depth :, :].astype(jnp.float32)
                per = width // units
                one = jnp.concatenate(
                    [
                        jnp.concatenate([tail[i * per + j : i * per + j + 1] for j in range(per)], axis=1)
                        for i in range(2)
                    ],
                    axis=0,
                )
            stats.append(one)
        while len(stats) > 1:
            stats = [one + two for one, two in zip(stats[0::2], stats[1::2], strict=True)]
        norm_out[...] = stats[0] * scale

    def whole(x):
        return pl.BlockSpec(x.shape, lambda i: (0, 0))

    arrays = [*blocks, *terms, own_stats, first_out, second_out, grad_first, gain.reshape(1, width), bias.reshape(1, width)]
    in_specs = [whole(x) for x in arrays]
    for i in range(n_terms - n_bits):
        in_specs[n_dp + i] = pl.BlockSpec((2 * rows, width), lambda i: (0, 0))
    out_shape = [
        jax.ShapeDtypeStruct((rows, width), second_out.dtype),
        jax.ShapeDtypeStruct((rows, width), jnp.float32),
        jax.ShapeDtypeStruct(w_shapes[0], jnp.float32),
        jax.ShapeDtypeStruct(w_shapes[1], jnp.float32),
        jax.ShapeDtypeStruct((2, width), jnp.float32),
    ]
    return pl.pallas_call(
        kernel,
        out_shape=out_shape,
        grid=(1,),
        in_specs=in_specs,
        out_specs=[whole(x) for x in out_shape],
        compiler_params=pltpu.CompilerParams(vmem_limit_bytes=48 * 1024 * 1024),
        cost_estimate=pl.CostEstimate(
            flops=0, bytes_accessed=12 * w_shapes[0][0] * w_shapes[0][1], transcendentals=0
        ),
        name="finish",
    )(*arrays)


def after(values, *others):
    return lax.optimization_barrier((values, *others))[0]


def gather_tokens_body(
    first_out, second_out, grad_first, grad_second, w_up, w_down, norm_gain, norm_bias
):
    n_dp, n_tensor, n_groups = (lax.axis_size(axis) for axis in ("dp", "tensor", "groups"))
    own_rows, depth = first_out.shape[0], w_up.shape[0]
    units = w_up.shape[1] // n_dp
    mates = 2 if n_groups % 2 == 0 else 1
    place = lax.axis_index("dp")
    top = bits_of(n_dp)[0]

    high, others = bits_of(n_tensor)[0], bits_of(n_tensor)[1:]
    own, *sends = pack(first_out, grad_second, w_up, w_down, mates)
    tokens, chunks, got, crossed = {0: own}, {}, {}, {}

    def tokens_dp(k, *first):
        tokens[k] = swap(after(tokens[k & (k - 1)], *first), "dp", k & -k, f"tokens_{k}")

    def tokens_tensor(k, *first):
        start = after(tokens[k], *first)
        chunks[k] = {0: tokens[k], high: swap(start, "tensor", high, f"tokens_{k}_{high}")}

    def tokens_rest(k, *first):
        for bit in others:
            for j in list(chunks[k]):
                piece = after(chunks[k][j], *first)
                chunks[k][j | bit] = swap(piece, "tensor", bit, f"tokens_{k}_{j | bit}")

    def weights_groups(k, *first):
        if mates == 2:
            crossed[k] = swap(after(got[k], *first), "groups", 1, f"weights_{k}")

    def weights_dp(k, *first):
        got[k] = swap(after(sends[k - 1], *first), "dp", k, f"weights_{k}")

    for bit in reversed(bits_of(n_dp)):
        tokens_dp(bit)
    tokens_tensor(0)
    tokens_rest(0)
    tokens_tensor(1, tokens[top], chunks[0][high])
    stage = [*tokens.values(), *chunks[0].values()]
    for k in range(2, n_dp):
        if k & (k - 1):
            tokens_dp(k, *stage)
        weights_dp(k, *stage, *([got[top]] if top in got else []))
    for k in range(2, n_dp):
        tokens_rest(k - 1)
        stage = [tokens[top]]
        if k & (k - 1):
            weights_groups(top)
            stage = [tokens[k], *got.values(), *crossed.values(), *chunks[k - 2].values()]
        tokens_tensor(k, *stage, chunks[k - 1][high])
    weights_dp(1, *stage)
    for k in [*range(2, n_dp), 1]:
        if k not in crossed:
            weights_groups(k)
    tokens_rest(n_dp - 1, *crossed.values())
    got = {k: [got[k]] + ([crossed[k]] if k in crossed else []) for k in got}

    order = sorted(chunks, reverse=True)
    halves, blocks, stats = core(
        [[chunks[k][j] for j in range(n_tensor)] for k in order], w_up, w_down, got, mates, norm_gain, norm_bias
    )
    blocks = dict(enumerate(blocks))
    for bit in bits_of(n_dp):
        blocks[bit] = swap(blocks[bit], "dp", bit, f"grads_{bit}")

    sums, behind, hops = {}, (), []
    for k, (even, odd) in zip(order, halves, strict=True):
        came = swap(odd, "tensor", 1, f"sums_{k}_1")
        spans = [slice(j * 2 * own_rows, (j + 1) * 2 * own_rows) for j in range(n_tensor // 2)]
        parts = {2 * j: (even[span], came[span]) for j, span in enumerate(spans)}
        parts[0] = (even, came)
        for bit in reversed(bits_of(n_tensor)[:-1]):
            for j in [j for j in parts if j & bit]:
                send = after(sum(parts.pop(j)), *behind)
                if not hops:
                    stats = after(stats, send)
                came = swap(send, "tensor", bit, f"sums_{k}_{j}")
                if k == top:
                    came = after(came, blocks[top])
                parts[j ^ bit] += (came,)
                behind = parts[j ^ bit][-1:]
                hops += behind
        sums[k] = parts[0]

    def add(terms):
        return sum(term[: 2 * own_rows].astype(jnp.float32) for term in terms).astype(jnp.bfloat16)

    for bit in bits_of(n_tensor):
        stats = stats + swap(stats, "tensor", bit, "stats")
    stats = stats.astype(jnp.bfloat16)
    extra = 16

    came = {}
    for bit in bits_of(n_dp)[::-1]:
        for k in [k for k in order if k & bit and k in sums and k != bit]:
            came[k] = swap(add(sums.pop(k)), "dp", bit, f"sums_{k}")
            sums[k ^ bit] += (came[k],)
    last = jnp.concatenate([add(sums[top]), jnp.pad(stats, ((0, extra - 2), (0, 0)))])
    came[top] = swap(last, "dp", top, f"sums_{top}")
    rows = stats.reshape(-1, units)
    rows = jnp.pad(rows, ((0, extra - rows.shape[0]), (0, 0)))
    for k in range(1, n_dp):
        if k & (k - 1):
            block = jnp.concatenate([blocks[k], rows])
            block = after(block, blocks[top], *hops[:1])
            blocks[k] = swap(block, "dp", k, f"grads_{k}")
    for bit in bits_of(n_dp)[:0:-1]:
        send = jnp.concatenate([add(sums[bit]), jnp.pad(after(stats, last), ((0, extra - 2), (0, 0)))])
        came[bit] = swap(send, "dp", bit, f"sums_{bit}")

    scale = (own_rows * n_tensor * n_dp) ** (-0.5)
    terms = [*sums[0], *(came[bit] for bit in bits_of(n_dp)[::-1])]
    return tuple(
        finish(
            [blocks[k] for k in range(n_dp)],
            terms,
            stats,
            first_out,
            second_out,
            grad_first,
            norm_gain,
            norm_bias,
            (w_up.shape, w_down.shape),
            scale,
        )
    )


def body(first_out, second_out, grad_first, grad_second, w_up, *rest):
    n_dp, n_tensor = lax.axis_size("dp"), lax.axis_size("tensor")
    powers = all(size > 1 and size & (size - 1) == 0 for size in (n_dp, n_tensor))
    few_tokens = first_out.shape[0] * n_tensor < w_up.shape[1]
    units, depth = w_up.shape[1] // n_dp, w_up.shape[0]
    fits = w_up.shape[1] % n_dp == 0 and units % depth == 0 and depth % 128 == 0
    fits = fits and first_out.shape[1] == 2 * units and n_dp > 2 and n_tensor > 2
    pick = gather_tokens_body if powers and few_tokens and fits else gather_weights_body
    return pick(first_out, second_out, grad_first, grad_second, w_up, *rest)


def solution(mesh):
    in_specs = (
        P(("groups", "tensor", "dp"), None),
        P(("groups", "tensor", "dp"), None),
        P(("groups", "tensor", "dp"), None),
        P(("groups", "tensor", "dp"), None),
        P("dp", "tensor"),
        P("tensor", "dp"),
        P(),
        P(),
    )
    out_specs = (
        P(("groups", "tensor", "dp"), None),
        P(("groups", "tensor", "dp"), None),
        P(("groups", "dp"), "tensor"),
        P(("groups", "tensor"), "dp"),
        P("groups", None),
    )
    return jax.shard_map(body, mesh=mesh, in_specs=in_specs, out_specs=out_specs, check_vma=False)
```

```python
import math

import jax
import jax.numpy as jnp
from jax import lax
from jax.experimental import pallas as pl
from jax.experimental.pallas import tpu as pltpu
from jax.sharding import PartitionSpec as P

epsilon = 1e-06


def normalize(row_data, norm_gain, norm_bias):
    values = row_data.astype(jnp.float32)
    row_mean = jnp.mean(values, axis=-1, keepdims=True)
    centred = values - row_mean
    inv_std = lax.rsqrt(jnp.mean(centred * centred, axis=-1, keepdims=True) + epsilon)
    standard = centred * inv_std
    normed = (standard * norm_gain + norm_bias).astype(jnp.bfloat16)
    return (standard, inv_std, normed)


def contract_tokens(left_rows, right_rows):
    return lax.dot_general(
        left_rows, right_rows, (((0,), (0,)), ((), ())), preferred_element_type=jnp.float32
    )


def contract_last(left_rows, right_rows):
    return lax.dot_general(
        left_rows, right_rows, (((1,), (1,)), ((), ())), preferred_element_type=jnp.float32
    )


def finish_rows(branch, grad_normed, second_out, grad_first, first_out, norm_gain, norm_bias):
    standard, inv_std, _ = normalize(first_out, norm_gain, norm_bias)
    second_in = (second_out.astype(jnp.float32) - branch).astype(jnp.bfloat16)
    grad_std = grad_normed * norm_gain
    grad_rows = inv_std * (
        grad_std
        - jnp.mean(grad_std, axis=-1, keepdims=True)
        - standard * jnp.mean(grad_std * standard, axis=-1, keepdims=True)
    )
    return second_in, grad_first.astype(jnp.float32) + grad_rows


def gather_weights_body(
    first_out, second_out, grad_first, grad_second, w_up, w_down, norm_gain, norm_bias
):
    own_rows = first_out.shape[0]
    up_full = lax.all_gather(w_up, "dp", axis=0, tiled=True)
    down_full = lax.all_gather(w_down, "dp", axis=1, tiled=True)
    first_all = lax.all_gather(first_out, "tensor", axis=0, tiled=True)
    grad_all = lax.all_gather(grad_second, "tensor", axis=0, tiled=True)
    standard_all, _, normed = normalize(first_all, norm_gain, norm_bias)
    offset = lax.axis_index("tensor") * own_rows
    standard = lax.dynamic_slice_in_dim(standard_all, offset, own_rows, 0)
    preact = jnp.dot(normed, up_full, preferred_element_type=jnp.float32)
    hidden = jax.nn.gelu(preact).astype(jnp.bfloat16)
    branch = lax.psum_scatter(
        jnp.dot(hidden, down_full, preferred_element_type=jnp.float32).astype(jnp.bfloat16),
        "tensor",
        scatter_dimension=0,
        tiled=True,
    ).astype(jnp.float32)
    tokens = own_rows * lax.axis_size("tensor") * lax.axis_size("dp")
    grad_scale = tokens ** (-0.5)
    grad_down_part = contract_tokens(hidden, grad_all)
    grad_down = (
        lax.psum_scatter(
            grad_down_part.astype(jnp.bfloat16), "dp", scatter_dimension=1, tiled=True
        ).astype(jnp.float32)
        * grad_scale
    )
    grad_hidden = contract_last(grad_all, down_full)
    grad_pre = jax.vjp(jax.nn.gelu, preact)[1](grad_hidden)[0].astype(jnp.bfloat16)
    grad_up_part = contract_tokens(normed, grad_pre)
    grad_up = (
        lax.psum_scatter(
            grad_up_part.astype(jnp.bfloat16), "dp", scatter_dimension=0, tiled=True
        ).astype(jnp.float32)
        * grad_scale
    )
    grad_normed = lax.psum_scatter(
        contract_last(grad_pre, up_full).astype(jnp.bfloat16),
        "tensor",
        scatter_dimension=0,
        tiled=True,
    ).astype(jnp.float32)
    second_in, grad_first_in = finish_rows(
        branch, grad_normed, second_out, grad_first, first_out, norm_gain, norm_bias
    )
    local_stats = jnp.stack([jnp.sum(grad_normed * standard, axis=0), jnp.sum(grad_normed, axis=0)])
    grad_norm = lax.psum(local_stats, ("tensor", "dp")) * grad_scale
    return (second_in, grad_first_in, grad_up, grad_down, grad_norm)


def swap(values, axis, mask, scope):
    with jax.named_scope(scope):
        return lax.ppermute(values, axis, [(i, i ^ mask) for i in range(lax.axis_size(axis))])


def bits_of(size):
    return [1 << b for b in reversed(range(size.bit_length() - 1))]


def pack(first_out, grad_second, w_up, w_down, mates):
    n_dp, (own_rows, width) = lax.axis_size("dp"), first_out.shape
    depth, units = w_up.shape[0], w_up.shape[1] // n_dp
    strips, rows = units // depth, depth // mates

    def kernel(first_ref, grad_ref, up_ref, down_ref, own, *sends):
        place, mate = lax.axis_index("dp"), lax.rem(lax.axis_index("groups"), mates)
        own[:own_rows, :] = first_ref[...]
        own[own_rows:, :] = grad_ref[...]
        for k in range(1, n_dp):
            first = pl.multiple_of((place ^ k) * units, units)
            send = sends[k - 1]
            send[:, :units] = up_ref[pl.ds(pl.multiple_of(mate * rows, rows), rows), pl.ds(first, units)]
            for c in range(strips):
                row = pl.multiple_of(first + mate * (units // mates) + c * rows, rows)
                send[:, units + c * depth : units + (c + 1) * depth] = down_ref[pl.ds(row, rows), :]

    return pl.pallas_call(
        kernel,
        out_shape=[jax.ShapeDtypeStruct((2 * own_rows, width), w_up.dtype)]
        + [jax.ShapeDtypeStruct((rows, width), w_up.dtype)] * (n_dp - 1),
        in_specs=[pl.BlockSpec(memory_space=pltpu.VMEM)] * 4,
        out_specs=[pl.BlockSpec(memory_space=pltpu.VMEM)] * n_dp,
        cost_estimate=pl.CostEstimate(flops=0, bytes_accessed=8 * w_up.size, transcendentals=0),
        name="pack",
    )(first_out, grad_second, w_up, w_down)


def core(chunks, w_up, w_down, got, mates, gain, bias):
    n_chunks, n, n_dp = len(chunks), len(chunks[0]), lax.axis_size("dp")
    (piece_rows, width), units = chunks[0][0].shape, w_up.shape[1] // n_dp
    piece_rows //= 2
    depth = width // n_dp
    strips, pair = units // depth, 2 * piece_rows
    slope = (2.0 / math.pi) ** 0.5
    dtype = w_up.dtype
    pieces_of_weights = [piece for k in range(1, n_dp) for piece in got[k]]
    n_got = len(pieces_of_weights)

    def kernel(*refs):
        toks, refs = refs[: n_chunks * n], refs[n_chunks * n :]
        (own_up, own_down), weights, (gain_ref, bias_ref), refs = (
            refs[:2],
            list(refs[2 : 2 + n_got]),
            refs[2 + n_got : 4 + n_got],
            refs[4 + n_got :],
        )
        outs, blocks, stat_ref = refs[: 2 * n_chunks], refs[2 * n_chunks : 2 * n_chunks + n_dp], refs[2 * n_chunks + n_dp]
        tok, norm, hid, pre, part, block, up_ref, down_ref, in_sem, w_sem, out_sem, b_sem = refs[2 * n_chunks + n_dp + 1 :]
        place, mate = lax.axis_index("dp"), lax.rem(lax.axis_index("groups"), mates)
        reads, loads, writes = [], [], []

        def load(src, dst):
            loads.append(pltpu.make_async_copy(src, dst, w_sem.at[len(loads)]))
            loads[-1].start()

        for i, ref in enumerate(toks):
            reads.append(pltpu.make_async_copy(ref, tok.at[i], in_sem.at[i]))
            if i < n:
                reads[-1].start()
        mine = pl.ds(pl.multiple_of(place * units, units), units)
        rows = pl.ds(pl.multiple_of(place * depth, depth), depth)
        load(own_up.at[:, mine], up_ref.at[rows, :])
        load(own_down.at[mine, :], down_ref.at[:, rows])
        for k in range(1, n_dp):
            first = pl.multiple_of((place ^ k) * depth, depth)
            many = len(got[k])
            rows = depth // many
            for j in range(many):
                piece = weights.pop(0)
                which = mate ^ j if many > 1 else 0
                row = pl.multiple_of(first + which * rows, rows)
                load(piece.at[:, pl.ds(0, units)], up_ref.at[pl.ds(row, rows), :])
                for c in range(strips):
                    row = pl.multiple_of(which * (units // many) + c * rows, rows)
                    load(
                        piece.at[:, pl.ds(units + c * depth, depth)],
                        down_ref.at[pl.ds(row, rows), pl.ds(first, depth)],
                    )
        for one in reads[n:]:
            one.start()
        stat_ref[...] = jnp.zeros_like(stat_ref)
        for i in range(n_chunks):
            for one in reads[i * n : (i + 1) * n] + (loads if i == 0 else []):
                one.wait()

            @pl.loop(0, n // 2)
            def _(t):
                at = i * n + 2 * t
                span = pl.ds(pl.multiple_of(at * piece_rows, pair), pair)
                values = tok[pl.ds(at, 2), :piece_rows].reshape(pair, width).astype(jnp.float32)
                centred = values - jnp.mean(values, axis=-1, keepdims=True)
                inv_std = lax.rsqrt(jnp.mean(centred * centred, axis=-1, keepdims=True) + epsilon)
                standard = centred * inv_std
                normed = (standard * gain_ref[...] + bias_ref[...]).astype(dtype)
                norm[span, :] = normed
                x = jnp.dot(normed, up_ref[...], preferred_element_type=jnp.float32)
                gate = jnp.tanh(slope * (x + 0.044715 * (x * x * x)))
                half = 0.5 + 0.5 * gate
                hidden = (x * half).astype(dtype)
                hid[span, :] = hidden
                rise = half + (0.5 * slope) * x * (1.0 - gate * gate) * (1.0 + (3 * 0.044715) * (x * x))
                grads = tok[pl.ds(at, 2), piece_rows:].reshape(pair, width)
                grad_pre = (contract_last(grads, down_ref[...]) * rise).astype(dtype)
                pre[span, :] = grad_pre
                branch = jnp.dot(hidden, down_ref[...], preferred_element_type=jnp.float32)
                grad_normed = contract_last(grad_pre, up_ref[...])
                stat_ref[0:1, :] += jnp.sum(grad_normed * standard, axis=0, keepdims=True)
                stat_ref[1:2, :] += jnp.sum(grad_normed, axis=0, keepdims=True)
                row = pl.multiple_of(t * pair, pair)
                for odd in range(2):
                    own = slice(odd * piece_rows, (odd + 1) * piece_rows)
                    part[2 * i + odd, pl.ds(row, piece_rows), :] = branch[own].astype(dtype)
                    part[2 * i + odd, pl.ds(row + piece_rows, piece_rows), :] = grad_normed[own].astype(dtype)

            for odd in (1, 0):
                at = 2 * i + odd
                writes.append(pltpu.make_async_copy(part.at[at], outs[at], out_sem.at[at]))
                writes[-1].start()
        top = bits_of(n_dp)[0]
        for k in sorted(range(n_dp), key=lambda k: (k < top, k)):
            columns = pl.ds(pl.multiple_of((place ^ k) * depth, depth), depth)
            block[k, :depth, :] = contract_tokens(norm[:, columns], pre[...]).astype(dtype)
            grads = tok[:, piece_rows:, columns].reshape(n_chunks * n * piece_rows, depth)
            down_block = contract_tokens(hid[...], grads).astype(dtype)
            for c in range(strips):
                block[k, depth:, c * depth : (c + 1) * depth] = down_block[c * depth : (c + 1) * depth]
            writes.append(pltpu.make_async_copy(block.at[k], blocks[k], b_sem.at[k]))
            writes[-1].start()
        for one in writes:
            one.wait()

    rows = n_chunks * n * piece_rows
    half = (n // 2 * pair, width)
    far = pl.BlockSpec(memory_space=pl.ANY)
    near = pl.BlockSpec(memory_space=pltpu.VMEM)
    out = pl.pallas_call(
        kernel,
        out_shape=[jax.ShapeDtypeStruct(half, dtype)] * (2 * n_chunks)
        + [jax.ShapeDtypeStruct((2 * depth, units), dtype)] * n_dp
        + [jax.ShapeDtypeStruct((2, width), jnp.float32)],
        in_specs=[far] * (n_chunks * n + 2 + n_got) + [near] * 2,
        out_specs=[far] * (2 * n_chunks + n_dp) + [near],
        scratch_shapes=[
            pltpu.VMEM((n_chunks * n, pair, width), dtype),
            pltpu.VMEM((rows, width), dtype),
            pltpu.VMEM((rows, units), dtype),
            pltpu.VMEM((rows, units), dtype),
            pltpu.VMEM((2 * n_chunks, *half), dtype),
            pltpu.VMEM((n_dp, 2 * depth, units), dtype),
            pltpu.VMEM((width, units), dtype),
            pltpu.VMEM((units, width), dtype),
            pltpu.SemaphoreType.DMA((n_chunks * n,)),
            pltpu.SemaphoreType.DMA((2 + n_got * (1 + strips),)),
            pltpu.SemaphoreType.DMA((2 * n_chunks,)),
            pltpu.SemaphoreType.DMA((n_dp,)),
        ],
        compiler_params=pltpu.CompilerParams(vmem_limit_bytes=56 * 1024 * 1024),
        cost_estimate=pl.CostEstimate(
            flops=10 * rows * width * units,
            bytes_accessed=8 * rows * width + 8 * width * units,
            transcendentals=rows * units,
        ),
        name="core",
    )(
        *[piece for chunk in chunks for piece in chunk],
        w_up,
        w_down,
        *pieces_of_weights,
        gain.reshape(1, width),
        bias.reshape(1, width),
    )
    halves = [out[2 * i : 2 * i + 2] for i in range(n_chunks)]
    return halves, list(out[2 * n_chunks : -1]), out[-1]


def finish(blocks, terms, own_stats, first_out, second_out, grad_first, gain, bias, w_shapes, scale):
    (rows, width), n_dp = first_out.shape, len(blocks)
    depth, units = w_shapes[0][0], w_shapes[0][1] // n_dp
    strips, n_bits, n_terms = units // depth, len(bits_of(n_dp)), len(terms)

    def kernel(*refs):
        parts, adds, (stat_ref, first_ref, second_ref, grad_ref, gain_ref, bias_ref), outs = (
            refs[:n_dp],
            refs[n_dp : n_dp + n_terms],
            refs[n_dp + n_terms : n_dp + n_terms + 6],
            refs[n_dp + n_terms + 6 :],
        )
        second_in, grad_in, up_out, down_out, norm_out = outs
        place = lax.axis_index("dp")
        for k in range(n_dp):
            first = pl.multiple_of((place ^ k) * units, units)
            up_out[:, pl.ds(first, units)] = parts[k][:depth, :].astype(jnp.float32) * scale
            for c in range(strips):
                block = parts[k][depth : 2 * depth, c * depth : (c + 1) * depth]
                row = pl.multiple_of(first + c * depth, depth)
                down_out[pl.ds(row, depth), :] = block.astype(jnp.float32) * scale
        total = sum(ref[: 2 * rows, :].astype(jnp.float32) for ref in adds)
        second_in[...] = (second_ref[...].astype(jnp.float32) - total[:rows]).astype(second_in.dtype)
        values = first_ref[...].astype(jnp.float32)
        centred = values - jnp.mean(values, axis=-1, keepdims=True)
        inv_std = lax.rsqrt(jnp.mean(centred * centred, axis=-1, keepdims=True) + epsilon)
        standard = centred * inv_std
        grad_std = total[rows:] * gain_ref[...]
        grad_rows = inv_std * (
            grad_std
            - jnp.mean(grad_std, axis=-1, keepdims=True)
            - standard * jnp.mean(grad_std * standard, axis=-1, keepdims=True)
        )
        grad_in[...] = grad_ref[...].astype(jnp.float32) + grad_rows
        stats = []
        for k in range(n_dp):
            if k == 0:
                one = stat_ref[...].astype(jnp.float32)
            elif k & (k - 1) == 0:
                one = adds[n_terms - n_bits + k.bit_length() - 1][2 * rows :, :].astype(jnp.float32)[:2]
            else:
                tail = parts[k][2 * depth :, :].astype(jnp.float32)
                per = width // units
                one = jnp.concatenate(
                    [
                        jnp.concatenate([tail[i * per + j : i * per + j + 1] for j in range(per)], axis=1)
                        for i in range(2)
                    ],
                    axis=0,
                )
            stats.append(one)
        while len(stats) > 1:
            stats = [one + two for one, two in zip(stats[0::2], stats[1::2], strict=True)]
        norm_out[...] = stats[0] * scale

    def whole(x):
        return pl.BlockSpec(x.shape, lambda i: (0, 0))

    arrays = [*blocks, *terms, own_stats, first_out, second_out, grad_first, gain.reshape(1, width), bias.reshape(1, width)]
    in_specs = [whole(x) for x in arrays]
    for i in range(n_terms - n_bits):
        in_specs[n_dp + i] = pl.BlockSpec((2 * rows, width), lambda i: (0, 0))
    out_shape = [
        jax.ShapeDtypeStruct((rows, width), second_out.dtype),
        jax.ShapeDtypeStruct((rows, width), jnp.float32),
        jax.ShapeDtypeStruct(w_shapes[0], jnp.float32),
        jax.ShapeDtypeStruct(w_shapes[1], jnp.float32),
        jax.ShapeDtypeStruct((2, width), jnp.float32),
    ]
    return pl.pallas_call(
        kernel,
        out_shape=out_shape,
        grid=(1,),
        in_specs=in_specs,
        out_specs=[whole(x) for x in out_shape],
        compiler_params=pltpu.CompilerParams(vmem_limit_bytes=48 * 1024 * 1024),
        cost_estimate=pl.CostEstimate(
            flops=0, bytes_accessed=12 * w_shapes[0][0] * w_shapes[0][1], transcendentals=0
        ),
        name="finish",
    )(*arrays)


def after(values, *others):
    return lax.optimization_barrier((values, *others))[0]


def gather_tokens_body(
    first_out, second_out, grad_first, grad_second, w_up, w_down, norm_gain, norm_bias
):
    n_dp, n_tensor, n_groups = (lax.axis_size(axis) for axis in ("dp", "tensor", "groups"))
    own_rows, depth = first_out.shape[0], w_up.shape[0]
    units = w_up.shape[1] // n_dp
    mates = 2 if n_groups % 2 == 0 else 1
    place = lax.axis_index("dp")
    top = bits_of(n_dp)[0]

    high, others = bits_of(n_tensor)[0], bits_of(n_tensor)[1:]
    own, *sends = pack(first_out, grad_second, w_up, w_down, mates)
    tokens, chunks, got, crossed = {0: own}, {}, {}, {}

    def tokens_dp(k, *first):
        tokens[k] = swap(after(tokens[k & (k - 1)], *first), "dp", k & -k, f"tokens_{k}")

    def tokens_tensor(k, *first):
        start = after(tokens[k], *first)
        chunks[k] = {0: tokens[k], high: swap(start, "tensor", high, f"tokens_{k}_{high}")}

    def tokens_rest(k, *first):
        for bit in others:
            for j in list(chunks[k]):
                piece = after(chunks[k][j], *first)
                chunks[k][j | bit] = swap(piece, "tensor", bit, f"tokens_{k}_{j | bit}")

    def weights_groups(k, *first):
        if mates == 2:
            crossed[k] = swap(after(got[k], *first), "groups", 1, f"weights_{k}")

    def weights_dp(k, *first):
        got[k] = swap(after(sends[k - 1], *first), "dp", k, f"weights_{k}")

    for bit in reversed(bits_of(n_dp)):
        tokens_dp(bit)
    tokens_tensor(0)
    tokens_rest(0)
    tokens_tensor(1, tokens[top], chunks[0][high])
    stage = [*tokens.values(), *chunks[0].values()]
    for k in range(2, n_dp):
        if k & (k - 1):
            tokens_dp(k, *stage)
        weights_dp(k, *stage, *([got[top]] if top in got else []))
    for k in range(2, n_dp):
        tokens_rest(k - 1)
        stage = [tokens[top]]
        if k & (k - 1):
            weights_groups(top)
            stage = [tokens[k], *got.values(), *crossed.values(), *chunks[k - 2].values()]
        tokens_tensor(k, *stage, chunks[k - 1][high])
    weights_dp(1, *stage, chunks[top][high])
    for k in [*range(2, n_dp), 1]:
        if k not in crossed:
            weights_groups(k)
    tokens_rest(n_dp - 1, *crossed.values())
    got = {k: [got[k]] + ([crossed[k]] if k in crossed else []) for k in got}

    order = sorted(chunks, reverse=True)
    halves, blocks, stats = core(
        [[chunks[k][j] for j in range(n_tensor)] for k in order], w_up, w_down, got, mates, norm_gain, norm_bias
    )
    blocks = dict(enumerate(blocks))
    for bit in bits_of(n_dp):
        blocks[bit] = swap(blocks[bit], "dp", bit, f"grads_{bit}")

    sums, behind, hops = {}, (), []
    for k, (even, odd) in zip(order, halves, strict=True):
        came = swap(odd, "tensor", 1, f"sums_{k}_1")
        spans = [slice(j * 2 * own_rows, (j + 1) * 2 * own_rows) for j in range(n_tensor // 2)]
        parts = {2 * j: (even[span], came[span]) for j, span in enumerate(spans)}
        parts[0] = (even, came)
        for bit in reversed(bits_of(n_tensor)[:-1]):
            for j in [j for j in parts if j & bit]:
                send = after(sum(parts.pop(j)), *behind)
                if not hops:
                    stats = after(stats, send)
                came = swap(send, "tensor", bit, f"sums_{k}_{j}")
                if k == top:
                    came = after(came, blocks[top])
                parts[j ^ bit] += (came,)
                behind = parts[j ^ bit][-1:]
                hops += behind
        sums[k] = parts[0]

    def add(terms):
        return sum(term[: 2 * own_rows].astype(jnp.float32) for term in terms).astype(jnp.bfloat16)

    for bit in bits_of(n_tensor):
        stats = stats + swap(stats, "tensor", bit, "stats")
    stats = stats.astype(jnp.bfloat16)
    extra = 16

    came = {}
    for bit in bits_of(n_dp)[::-1]:
        for k in [k for k in order if k & bit and k in sums and k != bit]:
            came[k] = swap(add(sums.pop(k)), "dp", bit, f"sums_{k}")
            sums[k ^ bit] += (came[k],)
    last = jnp.concatenate([add(sums[top]), jnp.pad(stats, ((0, extra - 2), (0, 0)))])
    came[top] = swap(last, "dp", top, f"sums_{top}")
    rows = stats.reshape(-1, units)
    rows = jnp.pad(rows, ((0, extra - rows.shape[0]), (0, 0)))
    for k in range(1, n_dp):
        if k & (k - 1):
            block = jnp.concatenate([blocks[k], rows])
            block = after(block, blocks[top], *hops[:1])
            blocks[k] = swap(block, "dp", k, f"grads_{k}")
    for bit in bits_of(n_dp)[:0:-1]:
        send = jnp.concatenate([add(sums[bit]), jnp.pad(after(stats, last), ((0, extra - 2), (0, 0)))])
        came[bit] = swap(send, "dp", bit, f"sums_{bit}")

    scale = (own_rows * n_tensor * n_dp) ** (-0.5)
    terms = [*sums[0], *(came[bit] for bit in bits_of(n_dp)[::-1])]
    return tuple(
        finish(
            [blocks[k] for k in range(n_dp)],
            terms,
            stats,
            first_out,
            second_out,
            grad_first,
            norm_gain,
            norm_bias,
            (w_up.shape, w_down.shape),
            scale,
        )
    )


def body(first_out, second_out, grad_first, grad_second, w_up, *rest):
    n_dp, n_tensor = lax.axis_size("dp"), lax.axis_size("tensor")
    powers = all(size > 1 and size & (size - 1) == 0 for size in (n_dp, n_tensor))
    few_tokens = first_out.shape[0] * n_tensor < w_up.shape[1]
    units, depth = w_up.shape[1] // n_dp, w_up.shape[0]
    fits = w_up.shape[1] % n_dp == 0 and units % depth == 0 and depth % 128 == 0
    fits = fits and first_out.shape[1] == 2 * units and n_dp > 2 and n_tensor > 2
    pick = gather_tokens_body if powers and few_tokens and fits else gather_weights_body
    return pick(first_out, second_out, grad_first, grad_second, w_up, *rest)


def solution(mesh):
    in_specs = (
        P(("groups", "tensor", "dp"), None),
        P(("groups", "tensor", "dp"), None),
        P(("groups", "tensor", "dp"), None),
        P(("groups", "tensor", "dp"), None),
        P("dp", "tensor"),
        P("tensor", "dp"),
        P(),
        P(),
    )
    out_specs = (
        P(("groups", "tensor", "dp"), None),
        P(("groups", "tensor", "dp"), None),
        P(("groups", "dp"), "tensor"),
        P(("groups", "tensor"), "dp"),
        P("groups", None),
    )
    return jax.shard_map(body, mesh=mesh, in_specs=in_specs, out_specs=out_specs, check_vma=False)
```
